512 devices in a mesh: boxes: 512 (over z, x, y, core).
Axes of the slice: x: 4, y: 4, z: 16, core: 2. Of those that a mesh axis runs over, the one named last changes fastest.
Arguments:
- coarse_state: float32 [512, 5, 512], P('boxes'), may hold values from -1 to 6, as said below
- fine_state: float32 [512, 8, 5, 512], P('boxes'), may hold values from -1 to 6, as said below
- refined: int32 [512, 8], P('boxes'), may hold values from 0 to 1, as said below
Outputs:
- coarse_out: float32 [512, 5, 512], P('boxes')
- fine_out: float32 [512, 8, 5, 512], P('boxes')
The draws below stay inside these ranges and needn't reach their ends.
Inputs may be any that keep to these rules, and one draw needn't show every extreme that they name: `coarse_state`: per cell the five values are density, three momenta and total energy of a gas with density and pressure from 0.5 to 2 and each velocity component within 0.5. `fine_state`: per cell the five values are density, three momenta and total energy of a gas with density and pressure from 0.5 to 2 and each velocity component within 0.5. Each block has 1 to 4 refined octants, and some block has exactly 4.
All inputs are finite; a program needn't handle non-finite values.
Results may differ from the reference program's by a relative error of at most 0.0003.
Values sent between devices are 32-bit elements; how exact they have to be, the bound alone decides.
No kernel may reach another device: no remote copies, remote signals or barrier semaphores. Data moves between devices by JAX's collectives and lax.ppermute only.
A program may use at most 64 MiB of HBM per device.

```python
import jax
import jax.numpy as jnp
from jax import lax

CB = 8
MAXF = 4
BLOCKS = 512


def gas_state(key, new_shape):
    block_count = new_shape[0]
    sub_keys = jax.random.split(key, 5)
    position = jnp.arange(block_count, dtype=jnp.float32) / max(block_count - 1, 1)
    position = position.reshape((block_count,) + (1,) * (len(new_shape) - 1))
    rough_part = jax.random.uniform(sub_keys[0], new_shape, dtype=jnp.float32)
    density = 0.5 + 1.5 * rough_part
    upper = 0.7 + 1.3 * position
    press_part = jax.random.uniform(sub_keys[1], new_shape, dtype=jnp.float32)
    pressure = 0.5 + (upper - 0.5) * press_part
    spread = 0.2 + 0.3 * position
    velocity = [spread * jax.random.uniform(sub_keys[2 + comp_id], new_shape, dtype=jnp.float32, minval=-1.0, maxval=1.0) for comp_id in range(3)]
    kinetic = 0.5 * density * (velocity[0] * velocity[0] + velocity[1] * velocity[1] + velocity[2] * velocity[2])
    energy = pressure / 0.4 + kinetic
    fields = [density, density * velocity[0], density * velocity[1], density * velocity[2], energy]
    return jnp.stack(fields, axis=len(new_shape) - 1)


def draw_coarse_state(key, part):
    key = jax.random.fold_in(key, 11)
    return gas_state(key, (BLOCKS, CB * CB * CB))


def draw_fine_state(key, part):
    key = jax.random.fold_in(key, 23)
    return gas_state(key, (BLOCKS, 8, CB * CB * CB))


def draw_refined(key, part):
    key = jax.random.fold_in(key, 37)
    sub_keys = jax.random.split(key, 3)
    counts = jax.random.randint(sub_keys[0], (BLOCKS,), 1, MAXF + 1)
    fullest = jax.random.randint(sub_keys[1], (), 0, BLOCKS)
    counts = counts.at[fullest].set(MAXF)
    scores = jax.random.randint(sub_keys[2], (BLOCKS, 8), 0, 1 << 20) * 8 + jnp.arange(8, dtype=jnp.int32)
    ranks = jnp.argsort(jnp.argsort(scores, axis=1), axis=1)
    return (ranks < counts[:, None]).astype(jnp.int32)


def setup_inputs(seed: int = 0) -> dict:
    splits = jax.random.split(jax.random.key(seed), 4)
    return {
        "coarse_state": draw_coarse_state(jax.random.fold_in(splits[3], 71), 0),
        "fine_state": draw_fine_state(jax.random.fold_in(splits[3], 71), 0),
        "refined": draw_refined(jax.random.fold_in(splits[3], 71), 0),
    }


gamma_gas = 1.4
courant = 0.4

def pressure_speed(conserved):
    density = conserved[0]
    velocity = conserved[1:4] / density
    kinetic = 0.5 * lax.optimization_barrier(jnp.sum(conserved[1:4] * velocity, axis=0))
    pressure = (gamma_gas - 1.0) * (conserved[4] - kinetic)
    sound = jnp.sqrt(gamma_gas * pressure / density)
    return (velocity, pressure, sound)

def physical_flux(conserved, axis_id):
    velocity, pressure, sound = pressure_speed(conserved)
    normal = velocity[axis_id]
    components = [conserved[1 + axis_id]]
    for comp_id in range(3):
        momentum_flux = conserved[1 + comp_id] * normal
        if comp_id == axis_id:
            momentum_flux = momentum_flux + pressure
        components.append(momentum_flux)
    components.append((conserved[4] + pressure) * normal)
    return (jnp.stack(components), jnp.abs(normal) + sound)

def rusanov(left_state, right_state, axis_id):
    flux_left, wave_left = physical_flux(left_state, axis_id)
    flux_right, wave_right = physical_flux(right_state, axis_id)
    wave_speed = jnp.maximum(wave_left, wave_right)
    return 0.5 * (flux_left + flux_right) - 0.5 * wave_speed * (right_state - left_state)

def wave_bound(conserved):
    velocity, pressure, sound = pressure_speed(conserved)
    return jnp.max(lax.optimization_barrier(jnp.sum(jnp.abs(velocity), axis=0)) + 3.0 * sound)

def periodic_change(conserved, step_ratio):
    summed = None
    for axis_id in range(3):
        ahead_state = jnp.roll(conserved, -1, axis=1 + axis_id)
        face_flux = rusanov(conserved, ahead_state, axis_id)
        net_flux = face_flux - jnp.roll(face_flux, 1, axis=1 + axis_id)
        summed = net_flux if summed is None else summed + net_flux
    return -step_ratio * summed

def upsample(field_grid):
    channels, size_x, size_y, size_z = field_grid.shape
    spread_out = jnp.broadcast_to(field_grid[:, :, None, :, None, :, None], (channels, size_x, 2, size_y, 2, size_z, 2))
    return spread_out.reshape(channels, 2 * size_x, 2 * size_y, 2 * size_z)

def restrict(field_grid):
    channels, size_x, size_y, size_z = field_grid.shape
    grouped = field_grid.reshape(channels, size_x // 2, 2, size_y // 2, 2, size_z // 2, 2)
    return lax.optimization_barrier(jnp.sum(grouped, axis=(2, 4, 6))) * 0.125

def bit_axes(block_count):
    bit_count = block_count.bit_length() - 1
    bit_groups = []
    for axis_id in range(3):
        bit_groups.append([bit_count - 1 - bit_id for bit_id in range(bit_count - 1, -1, -1) if bit_id % 3 == axis_id])
    return (bit_count, bit_groups)

def dim_order(bit_count, bit_groups):
    return [bit_count] + bit_groups[0] + [bit_count + 1] + bit_groups[1] + [bit_count + 2] + bit_groups[2] + [bit_count + 3]

def to_global(blocks, side_len):
    block_count = blocks.shape[0]
    channels = blocks.shape[1]
    bit_count, bit_groups = bit_axes(block_count)
    reshaped = blocks.reshape([2] * bit_count + [channels, side_len, side_len, side_len])
    reshaped = jnp.transpose(reshaped, dim_order(bit_count, bit_groups))
    return reshaped.reshape(channels, side_len * 2 ** len(bit_groups[0]), side_len * 2 ** len(bit_groups[1]), side_len * 2 ** len(bit_groups[2]))

def from_global(field_grid, block_count, side_len):
    channels = field_grid.shape[0]
    bit_count, bit_groups = bit_axes(block_count)
    perm_order = dim_order(bit_count, bit_groups)
    new_shape = [channels] + [2] * len(bit_groups[0]) + [side_len] + [2] * len(bit_groups[1]) + [side_len] + [2] * len(bit_groups[2]) + [side_len]
    reshaped = field_grid.reshape(new_shape)
    inverse = [perm_order.index(dim_id) for dim_id in range(len(perm_order))]
    reshaped = jnp.transpose(reshaped, inverse)
    return reshaped.reshape(block_count, channels, side_len, side_len, side_len)

def octant_block(octants):
    block_count = octants.shape[0]
    side_len = octants.shape[-1]
    reshaped = octants.reshape(block_count, 2, 2, 2, 5, side_len, side_len, side_len)
    reshaped = jnp.transpose(reshaped, (0, 4, 1, 5, 2, 6, 3, 7))
    return reshaped.reshape(block_count, 5, 2 * side_len, 2 * side_len, 2 * side_len)

def block_octants(blocks, side_len):
    block_count = blocks.shape[0]
    reshaped = blocks.reshape(block_count, 5, 2, side_len, 2, side_len, 2, side_len)
    reshaped = jnp.transpose(reshaped, (0, 2, 4, 6, 1, 3, 5, 7))
    return reshaped.reshape(block_count, 8, 5, side_len * side_len * side_len)

def reference(coarse_state, fine_state, refined):
    block_count = coarse_state.shape[0]
    side_len = CB
    coarse0 = to_global(coarse_state.reshape(block_count, 5, side_len, side_len, side_len), side_len)
    fine0 = to_global(octant_block(fine_state.reshape(block_count, 8, 5, side_len, side_len, side_len)), 2 * side_len)
    octant_flags = refined.astype(jnp.float32).reshape(block_count, 1, 2, 1, 2, 1, 2, 1)
    octant_flags = jnp.broadcast_to(octant_flags, (block_count, 1, 2, side_len, 2, side_len, 2, side_len))
    octant_flags = octant_flags.reshape(block_count, 1, 2 * side_len, 2 * side_len, 2 * side_len)
    covered = to_global(octant_flags, 2 * side_len)[0] > 0.5
    composite0 = jnp.where(covered, fine0, upsample(coarse0))
    fastest = jnp.maximum(wave_bound(coarse0), wave_bound(composite0))
    fine_ratio = courant / fastest
    coarse_ratio = 0.5 * fine_ratio
    coarse1 = coarse0 + periodic_change(coarse0, coarse_ratio)
    fine1 = fine0 + periodic_change(composite0, fine_ratio)
    composite1 = jnp.where(covered, fine1, upsample(coarse1))
    coarse2 = 0.5 * coarse0 + 0.5 * (coarse1 + periodic_change(coarse1, coarse_ratio))
    fine2 = 0.5 * fine0 + 0.5 * (fine1 + periodic_change(composite1, fine_ratio))
    coarse_covered = covered[::2, ::2, ::2]
    coarse_grid = jnp.where(coarse_covered, restrict(fine2), coarse2)
    fine_grid = jnp.where(covered, fine2, jnp.zeros_like(fine2))
    coarse_out = from_global(coarse_grid, block_count, side_len).reshape(block_count, 5, side_len * side_len * side_len)
    fine_out = block_octants(from_global(fine_grid, block_count, 2 * side_len), side_len)
    return (coarse_out, fine_out)
```

```python
import functools

import jax
import jax.numpy as jnp
import ml_dtypes
import numpy as np
from jax import lax
from jax.experimental import pallas as pl
from jax.experimental.pallas import tpu as pltpu
from jax.sharding import PartitionSpec as P

PITCH = 10
LANES = 128
FINE = 40
COARSE = FINE
DEEP = COARSE + 5
COVER = DEEP + 5
COUNT = COVER + 1
ROWS0 = 56
INNER1 = 4 * 8
ROWS1 = INNER1 + 3 * 8
INNER2 = 6 * 8
ROWS2 = INNER2 + 5 * 8
gamma_gas = 1.4
courant = 0.4


def placement():
    fine = np.zeros((256, 512), np.float32)
    coarse = np.zeros((128, 128), np.float32)
    for oy in range(2):
        for oz in range(2):
            for j in range(8):
                for k in range(8):
                    row = oy * 128 + oz * 64 + j * 8 + k
                    lane = (oy * 4 + j // 2) * PITCH + oz * 4 + k // 2
                    fine[row, (j % 2 * 2 + k % 2) * 128 + lane] = 1
    for j in range(8):
        for k in range(8):
            coarse[j * 8 + k, j * PITCH + k] = 1
    return fine, coarse


def place(values, matrix):
    high = values.astype(jnp.bfloat16)
    rest = values - high.astype(jnp.float32)
    middle = rest.astype(jnp.bfloat16)
    low = (rest - middle.astype(jnp.float32)).astype(jnp.bfloat16)
    rows = values.shape[0]
    parts = jnp.concatenate([high, middle, low], axis=0)
    out = jnp.dot(parts, matrix, preferred_element_type=jnp.float32)
    return out[:rows] + out[rows : 2 * rows] + out[2 * rows :]


def roll(x, shift, axis):
    shift = shift % x.shape[axis]
    return pltpu.roll(x, shift, axis) if shift else x


def positions(rows):
    row = lax.broadcasted_iota(jnp.int32, (rows, LANES), 0)
    lane = lax.broadcasted_iota(jnp.int32, (rows, LANES), 1)
    x = jnp.where(row > 8, row - 16, row)
    along = (lane + PITCH + 1) & (LANES - 1)
    y1 = (along * 205) >> 11
    return lane, x, y1 - 1, along - y1 * PITCH - 1


def inside(pos):
    return (pos >= 0) & (pos < 8)


def primitive(u):
    inverse = 1.0 / u[0]
    v = [u[1 + d] * inverse for d in range(3)]
    pressure = 0.4 * (u[4] - 0.5 * (u[1] * v[0] + u[2] * v[1] + u[3] * v[2]))
    sound = jnp.sqrt(gamma_gas * pressure * inverse)
    return v, pressure, sound


def cell_flux(u, prim, d):
    v, pressure, sound = prim
    flux = [u[1 + d]] + [u[1 + e] * v[d] for e in range(3)] + [(u[4] + pressure) * v[d]]
    flux[1 + d] = flux[1 + d] + pressure
    return list(u) + flux + [jnp.abs(v[d]) + sound]


def face(left, right):
    speed = jnp.maximum(left[10], right[10])
    return [(left[5 + f] + right[5 + f]) - speed * (right[f] - left[f]) for f in range(5)]


def ahead(x, d):
    return roll(x, -1, 0) if d == 0 else roll(x, -PITCH if d == 1 else -1, 1)


def behind(x, d):
    return roll(x, 1, 0) if d == 0 else roll(x, PITCH if d == 1 else 1, 1)


def fine_net(u, inner):
    prims = [primitive(u[q]) for q in range(8)]
    total = [None] * 8
    for d in range(3):
        bit = 4 >> d
        cut = (lambda x: x[:8]) if inner and d > 0 else (lambda x: x)
        keep = (lambda x: x[:8]) if inner else (lambda x: x)
        for low in range(8):
            if low & bit:
                continue
            high = low | bit
            cells = []
            for q in (low, high):
                v, pressure, sound = prims[q]
                cells.append(cell_flux([cut(x) for x in u[q]], ([cut(x) for x in v], cut(pressure), cut(sound)), d))
            middle = face(cells[0], cells[1])
            after = face(cells[1], [ahead(x, d) for x in cells[0]])
            net_low = [keep(middle[f] - behind(after[f], d)) for f in range(5)]
            net_high = [keep(after[f] - middle[f]) for f in range(5)]
            for q, net in ((low, net_low), (high, net_high)):
                total[q] = net if total[q] is None else [s + n for s, n in zip(total[q], net)]
    return total


def coarse_net(u, deep, pos):
    prim = primitive(u)
    prim_deep = None if deep is None else primitive(deep)
    total = None
    for d in range(3):
        cell = cell_flux(u, prim, d)
        right = [ahead(x, d) for x in cell]
        if deep is not None:
            outer = cell_flux(deep, prim_deep, d)
            last, first = pos[d] == 8, pos[d] == -1
            right = [jnp.where(last, o, r) for o, r in zip(outer, right)]
        after = face(cell, right)
        before = [behind(x, d) for x in after]
        if deep is not None:
            before = [jnp.where(first, o, b) for o, b in zip(face(outer, cell), before)]
        net = [a - b for a, b in zip(after, before)]
        total = net if total is None else [s + n for s, n in zip(total, net)]
    return total


def prepare(pos_ref, refined_ref, coarse_ref, fine_ref, place_ref, place_coarse_ref, inner_ref, send_ref, scr, scr_c):
    lane, x, y, z = positions(8)
    left_half = lane < 64
    for o in range(8):
        for q in range(4):
            row = (o // 4 * 4 + q) * 8
            scr[o % 4, row : row + 5, :] = fine_ref[o, :, q * 128 : q * 128 + 128]
    for q in range(4):
        tile = coarse_ref[:, q * 128 : q * 128 + 128]
        scr_c[q * 16 : q * 16 + 5, :] = tile
        scr_c[q * 16 + 8 : q * 16 + 13, :] = roll(tile, 64, 1)
    sides = [[], []]
    for f in range(5):
        tile = [scr[c, pl.ds(f, 8, stride=8), :] for c in range(4)]
        sides[0].append(
            jnp.concatenate([jnp.where(left_half, tile[2 * h], roll(tile[2 * h + 1], 64, 1)) for h in range(2)], axis=1)
        )
        sides[1].append(
            jnp.concatenate([jnp.where(left_half, roll(tile[2 * h], 64, 1), tile[2 * h + 1]) for h in range(2)], axis=1)
        )
    fine = place(jnp.concatenate(sides[0] + sides[1], axis=0), place_ref[...])
    coarse = place(jnp.concatenate([scr_c[pl.ds(f, 8, stride=8), :] for f in range(5)], axis=0), place_coarse_ref[...])
    coarse = [coarse[f * 8 : f * 8 + 8] for f in range(5)]

    covered = jnp.zeros((8, LANES), jnp.float32)
    for o in range(8):
        here = ((x >= 4) == (o >= 4)) & ((y >= 4) == (o % 4 >= 2)) & ((z >= 4) == (o % 2 == 1))
        covered = jnp.where(here, (refined_ref[o] > 0).astype(jnp.float32), covered)
    state = []
    for f in range(5):
        for q in range(8):
            row = (q // 4 * 5 + f) * 8
            part = fine[row : row + 8, q % 4 * 128 : q % 4 * 128 + 128]
            state.append(jnp.where(covered > 0.5, part, coarse[f]))
    state += coarse
    fastest = None
    for u in [[state[f * 8 + q] for f in range(5)] for q in range(8)] + [coarse]:
        v, pressure, sound = primitive(u)
        speed = jnp.abs(v[0]) + jnp.abs(v[1]) + jnp.abs(v[2]) + 3.0 * sound
        fastest = speed if fastest is None else jnp.maximum(fastest, speed)
    fastest = jnp.where(inside(y) & inside(z), fastest, 0.0)
    fastest = jnp.broadcast_to(jnp.max(fastest), (1, LANES))

    zero = jnp.zeros((8, LANES), jnp.float32)
    stored = state + [zero] * 5 + [covered]
    for n in range(COUNT):
        inner_ref[n] = stored[n]
    up, down = pos_ref[0], pos_ref[1]
    for t in range(8):
        send_ref[t, COUNT : COUNT + 1, :] = fastest
    for n in range(COUNT):
        deep = DEEP <= n < COVER
        source = stored[n - 5] if deep else stored[n]
        high, low = (6, 1) if deep else (7, 0)
        send_ref[up, n : n + 1, :] = source[high : high + 1, :]
        send_ref[down, n : n + 1, :] = source[low : low + 1, :]


def forward_y(pos_ref, got_ref, inner_ref, outer_ref, send_ref):
    lane, x, y, z = positions(8)
    row = lax.broadcasted_iota(jnp.int32, (8, LANES), 0)
    up, down = pos_ref[0], pos_ref[1]
    fastest = got_ref[0, COUNT : COUNT + 1, :]
    for t in range(1, 8):
        fastest = jnp.maximum(fastest, got_ref[t, COUNT : COUNT + 1, :])
    fastest = jnp.broadcast_to(fastest, (8, LANES))
    for n in range(COUNT):
        above = jnp.broadcast_to(got_ref[up, n : n + 1, :], (8, LANES))
        below = jnp.broadcast_to(got_ref[down, n : n + 1, :], (8, LANES))
        outer_ref[n] = jnp.where(row == 0, above, jnp.where(row == 7, below, 0.0))
    for t in range(8):
        send_ref[t, INNER1 - 8 : INNER1, :] = fastest
    up, down = pos_ref[2], pos_ref[3]
    for slot, at, deep_at in ((up, 7, 6), (down, 0, 1)):
        for first, source, count in ((0, inner_ref, COUNT), (INNER1, outer_ref, DEEP)):
            for block in range((count + 15) // 16):
                packed = fastest
                for s in range(16):
                    n = block * 16 + s
                    if n >= count:
                        break
                    deep = DEEP <= n < COVER
                    value = source[n - 5 if deep else n]
                    value = roll(value, s * 8 - (deep_at if deep else at) * PITCH, 1)
                    packed = jnp.where((lane >> 3) == s, value, packed)
                send_ref[slot, first + block * 8 : first + block * 8 + 8, :] = packed


def forward_z(pos_ref, got_ref, inner_ref, outer_ref, inner_out, outer_out, send_ref):
    lane, x, y, z = positions(8)
    up, down = pos_ref[2], pos_ref[3]
    fastest = got_ref[0, INNER1 - 8 : INNER1, :]
    for t in range(1, 8):
        fastest = jnp.maximum(fastest, got_ref[t, INNER1 - 8 : INNER1, :])
    below_lanes = (lane >= LANES - PITCH) & (lane < LANES - PITCH + 8)
    above_lanes = (lane >= 8 * PITCH) & (lane < 8 * PITCH + 8)
    for first, source, target, count in ((0, inner_ref, inner_out, COUNT), (INNER1, outer_ref, outer_out, DEEP)):
        for n in range(COUNT):
            value = source[n]
            if n < count:
                block, s = n // 16, n % 16
                below = got_ref[down, first + block * 8 : first + block * 8 + 8, :]
                above = got_ref[up, first + block * 8 : first + block * 8 + 8, :]
                value = jnp.where(below_lanes, roll(below, -PITCH - s * 8, 1), value)
                value = jnp.where(above_lanes, roll(above, 8 * PITCH - s * 8, 1), value)
            target[n] = value
    for t in range(8):
        send_ref[t, 0:8, :] = fastest
    up, down = pos_ref[4], pos_ref[5]
    along = (lane + PITCH) & (LANES - 1)
    slots = along - ((along * 205) >> 11) * PITCH
    slots = jnp.where(along < 10 * PITCH, slots, -1)
    for slot, at, deep_at in ((up, 7, 6), (down, 0, 1)):
        for first, source, count in ((0, inner_out, COUNT), (INNER2, outer_out, DEEP)):
            for block in range((count + 9) // 10):
                packed = fastest
                for s in range(10):
                    n = block * 10 + s
                    if n >= count:
                        break
                    deep = DEEP <= n < COVER
                    value = roll(source[n - 5 if deep else n], s - (deep_at if deep else at), 1)
                    packed = jnp.where(slots == s, value, packed)
                send_ref[slot, first + block * 8 : first + block * 8 + 8, :] = packed


def advance(
    pos_ref, got_ref, inner_ref, outer_ref, back_ref, back_coarse_ref, coarse_out, fine_out, scr, scr_c
):
    lane, x, y, z = positions(16)
    up, down = pos_ref[4], pos_ref[5]
    fastest = got_ref[0, 0:8, :]
    for t in range(1, 8):
        fastest = jnp.maximum(fastest, got_ref[t, 0:8, :])
    fastest = jnp.where((lane[:8] >= 90) & (lane[:8] < 118), fastest, 0.0)
    fastest = jnp.broadcast_to(jnp.max(fastest), (8, LANES))
    half = 0.5 * (courant / fastest)
    half16 = jnp.concatenate([half, half], axis=0)

    below_lanes, above_lanes = z[:8] == -1, z[:8] == 8
    state = []
    for n in range(COUNT):
        parts = []
        for first, source, count in ((0, inner_ref, COUNT), (INNER2, outer_ref, DEEP)):
            value = source[n]
            if n < count:
                block, s = n // 10, n % 10
                below = got_ref[down, first + block * 8 : first + block * 8 + 8, :]
                above = got_ref[up, first + block * 8 : first + block * 8 + 8, :]
                value = jnp.where(below_lanes, roll(below, -1 - s, 1), value)
                value = jnp.where(above_lanes, roll(above, 8 - s, 1), value)
            parts.append(value)
        state.append(jnp.concatenate(parts, axis=0))
    covered = state[COVER] > 0.5
    fine0 = [[state[f * 8 + q] for f in range(5)] for q in range(8)]
    coarse0 = state[COARSE:DEEP]

    net = coarse_net(coarse0, state[DEEP:COVER], (x, y, z))
    coarse1 = [u - 0.5 * half16 * n for u, n in zip(coarse0, net)]
    net = fine_net(fine0, False)
    fine1 = [
        [jnp.where(covered, fine0[q][f] - half16 * net[q][f], coarse1[f]) for f in range(5)] for q in range(8)
    ]
    net = coarse_net(coarse1, None, None)
    coarse2 = [0.5 * c0[:8] + 0.5 * (c1[:8] - 0.5 * half * n[:8]) for c0, c1, n in zip(coarse0, coarse1, net)]
    net = fine_net(fine1, True)
    mine = inside(y[:8]) & inside(z[:8])
    refined = mine & covered[:8]
    fine2 = [
        [
            jnp.where(refined, 0.5 * fine0[q][f][:8] + 0.5 * (fine1[q][f][:8] - half * net[q][f]), 0.0)
            for f in range(5)
        ]
        for q in range(8)
    ]
    coarse = []
    for f in range(5):
        total = functools.reduce(jnp.add, [fine2[q][f] for q in range(8)])
        coarse.append(jnp.where(mine, jnp.where(refined, 0.125 * total, coarse2[f]), 0.0))

    left_half = lane[:8] < 64
    rows = [jnp.concatenate([fine2[a * 4 + q][f] for q in range(4)], axis=1) for a in range(2) for f in range(5)]
    back = place(jnp.concatenate(rows, axis=0), back_ref[...])
    for f in range(5):
        for h in range(2):
            even = back[f * 8 : f * 8 + 8, h * 128 : h * 128 + 128]
            odd = back[40 + f * 8 : 48 + f * 8, h * 128 : h * 128 + 128]
            scr[2 * h, pl.ds(f, 8, stride=8), :] = jnp.where(left_half, even, roll(odd, 64, 1))
            scr[2 * h + 1, pl.ds(f, 8, stride=8), :] = jnp.where(left_half, roll(even, 64, 1), odd)
    for o in range(8):
        for q in range(4):
            row = (o // 4 * 4 + q) * 8
            fine_out[o, :, q * 128 : q * 128 + 128] = scr[o % 4, row : row + 5, :]
    back = place(jnp.concatenate(coarse, axis=0), back_coarse_ref[...])
    for f in range(5):
        scr_c[pl.ds(f, 8, stride=8), :] = back[f * 8 : f * 8 + 8]
    for q in range(4):
        even = scr_c[q * 16 : q * 16 + 5, :]
        odd = scr_c[q * 16 + 8 : q * 16 + 13, :]
        coarse_out[:, q * 128 : q * 128 + 128] = jnp.where(left_half[:5], even, roll(odd, 64, 1))


def shape(*dims):
    return jax.ShapeDtypeStruct(dims, jnp.float32)


def call(kernel, kinds, outs, scratch, args):
    spaces = {"s": pltpu.SMEM, "v": pltpu.VMEM}
    return pl.pallas_call(
        kernel,
        out_shape=outs,
        in_specs=[pl.BlockSpec(memory_space=spaces[k]) for k in kinds],
        out_specs=[pl.BlockSpec(memory_space=pltpu.VMEM)] * len(outs),
        scratch_shapes=scratch,
        compiler_params=pltpu.CompilerParams(vmem_limit_bytes=32 * 1024 * 1024),
    )(*args)


def lines(count, dim):
    bits = count.bit_length() - 1
    mask = sum(1 << t for t in range(bits) if t % 3 == dim)
    groups = {}
    for device in range(count):
        groups.setdefault(device & ~mask, []).append(device)
    return list(groups.values())


def swap(block, dim):
    return lax.all_to_all(block, "boxes", 0, 0, axis_index_groups=lines(lax.axis_size("boxes"), dim))


def local(coarse_state, fine_state, refined):
    fine_place, coarse_place = placement()
    as_matrix = lambda m: jnp.asarray(np.ascontiguousarray(m).astype(ml_dtypes.bfloat16))
    device = lax.axis_index("boxes")
    pos = []
    for dim in range(3):
        here = sum(((device >> (3 * i + dim)) & 1) << i for i in range(3))
        pos += [(here + 1) & 7, (here + 7) & 7]
    pos = jnp.stack(pos).astype(jnp.int32)
    scratch = [pltpu.VMEM((4, 64, LANES), jnp.float32), pltpu.VMEM((64, LANES), jnp.float32)]
    field = shape(COUNT, 8, LANES)

    inner, send = call(
        prepare,
        "ssvvvv",
        [field, shape(8, ROWS0, LANES)],
        scratch,
        (pos, refined[0], coarse_state[0], fine_state[0], as_matrix(fine_place), as_matrix(coarse_place)),
    )
    got = swap(send, 0)
    outer, send = call(forward_y, "svv", [field, shape(8, ROWS1, LANES)], [], (pos, got, inner))
    got = swap(send, 1)
    inner, outer, send = call(
        forward_z, "svvv", [field, field, shape(8, ROWS2, LANES)], [], (pos, got, inner, outer)
    )
    got = swap(send, 2)
    coarse_out, fine_out = call(
        advance,
        "svvvvv",
        [shape(5, 512), shape(8, 5, 512)],
        scratch,
        (pos, got, inner, outer, as_matrix(fine_place.T), as_matrix(coarse_place.T)),
    )
    return coarse_out[None], fine_out[None]


def solution(mesh):
    in_specs = (P("boxes", None, None), P("boxes", None, None, None), P("boxes", None))
    out_specs = (P("boxes", None, None), P("boxes", None, None, None))
    return jax.shard_map(local, mesh=mesh, in_specs=in_specs, out_specs=out_specs, check_vma=False)
```

```python
import functools

import jax
import jax.numpy as jnp
import ml_dtypes
import numpy as np
from jax import lax
from jax.experimental import pallas as pl
from jax.experimental.pallas import tpu as pltpu
from jax.sharding import PartitionSpec as P

PITCH = 10
LANES = 128
FINE = 40
COARSE = FINE
DEEP = COARSE + 5
COVER = DEEP + 5
COUNT = COVER + 1
WHOLE = 34
ROWS0 = 40
ROWS1 = 32
ROWS2 = 32
gamma_gas = 1.4
courant = 0.4


def placement():
    fine = np.zeros((256, 512), np.float32)
    coarse = np.zeros((128, 128), np.float32)
    for oy in range(2):
        for oz in range(2):
            for j in range(8):
                for k in range(8):
                    row = oy * 128 + oz * 64 + j * 8 + k
                    lane = (oy * 4 + j // 2) * PITCH + oz * 4 + k // 2
                    fine[row, (j % 2 * 2 + k % 2) * 128 + lane] = 1
    for j in range(8):
        for k in range(8):
            coarse[j * 8 + k, j * PITCH + k] = 1
    return fine, coarse


def place(values, matrix):
    high = values.astype(jnp.bfloat16)
    rest = values - high.astype(jnp.float32)
    middle = rest.astype(jnp.bfloat16)
    low = (rest - middle.astype(jnp.float32)).astype(jnp.bfloat16)
    rows = values.shape[0]
    parts = jnp.concatenate([high, middle, low], axis=0)
    out = jnp.dot(parts, matrix, preferred_element_type=jnp.float32)
    return out[:rows] + out[rows : 2 * rows] + out[2 * rows :]


def roll(x, shift, axis):
    shift = shift % x.shape[axis]
    return pltpu.roll(x, shift, axis) if shift else x


def positions(rows):
    row = lax.broadcasted_iota(jnp.int32, (rows, LANES), 0)
    lane = lax.broadcasted_iota(jnp.int32, (rows, LANES), 1)
    x = jnp.where(row > 8, row - 16, row)
    along = (lane + PITCH + 1) & (LANES - 1)
    y1 = (along * 205) >> 11
    return lane, x, y1 - 1, along - y1 * PITCH - 1


def inside(pos):
    return (pos >= 0) & (pos < 8)


def primitive(u):
    inverse = 1.0 / u[0]
    v = [u[1 + d] * inverse for d in range(3)]
    pressure = 0.4 * (u[4] - 0.5 * (u[1] * v[0] + u[2] * v[1] + u[3] * v[2]))
    sound = jnp.sqrt(gamma_gas * pressure * inverse)
    return v, pressure, sound


def cell_flux(u, prim, d):
    v, pressure, sound = prim
    flux = [u[1 + d]] + [u[1 + e] * v[d] for e in range(3)] + [(u[4] + pressure) * v[d]]
    flux[1 + d] = flux[1 + d] + pressure
    return list(u) + flux + [jnp.abs(v[d]) + sound]


def face(left, right):
    speed = jnp.maximum(left[10], right[10])
    return [(left[5 + f] + right[5 + f]) - speed * (right[f] - left[f]) for f in range(5)]


def ahead(x, d):
    return roll(x, -1, 0) if d == 0 else roll(x, -PITCH if d == 1 else -1, 1)


def behind(x, d):
    return roll(x, 1, 0) if d == 0 else roll(x, PITCH if d == 1 else 1, 1)


def fine_net(u, inner):
    prims = [primitive(u[q]) for q in range(8)]
    total = [None] * 8
    for d in range(3):
        bit = 4 >> d
        cut = (lambda x: x[:8]) if inner and d > 0 else (lambda x: x)
        keep = (lambda x: x[:8]) if inner else (lambda x: x)
        for low in range(8):
            if low & bit:
                continue
            high = low | bit
            cells = []
            for q in (low, high):
                v, pressure, sound = prims[q]
                cells.append(cell_flux([cut(x) for x in u[q]], ([cut(x) for x in v], cut(pressure), cut(sound)), d))
            middle = face(cells[0], cells[1])
            after = face(cells[1], [ahead(x, d) for x in cells[0]])
            net_low = [keep(middle[f] - behind(after[f], d)) for f in range(5)]
            net_high = [keep(after[f] - middle[f]) for f in range(5)]
            for q, net in ((low, net_low), (high, net_high)):
                total[q] = net if total[q] is None else [s + n for s, n in zip(total[q], net)]
    return total


def coarse_net(u, deep, pos):
    prim = primitive(u)
    prim_deep = None if deep is None else primitive(deep)
    total = None
    for d in range(3):
        cell = cell_flux(u, prim, d)
        right = [ahead(x, d) for x in cell]
        if deep is not None:
            outer = cell_flux(deep, prim_deep, d)
            last, first = pos[d] == 8, pos[d] == -1
            right = [jnp.where(last, o, r) for o, r in zip(outer, right)]
        after = face(cell, right)
        before = [behind(x, d) for x in after]
        if deep is not None:
            before = [jnp.where(first, o, b) for o, b in zip(face(outer, cell), before)]
        net = [a - b for a, b in zip(after, before)]
        total = net if total is None else [s + n for s, n in zip(total, net)]
    return total


def rows_of(fields):
    row = lax.broadcasted_iota(jnp.int32, (8, LANES), 0)
    merged = []
    for j in range(0, len(fields), 4):
        packed = fields[j]
        for i, value in enumerate(fields[j : j + 4]):
            if i:
                here = (row == 2 * i) | (row == 2 * i - 1)
                packed = jnp.where(here, roll(value, 2 * i, 0), packed)
        merged.append(packed)
    return merged


def edge_fields(outer, fixed_bit, at_high):
    row = lax.broadcasted_iota(jnp.int32, (8, LANES), 0)
    fields = []
    for f in range(5):
        for other in range(2):
            q = (fixed_bit if at_high else 0) + (3 - fixed_bit) * other
            fields.append(jnp.where(row == 0, outer(f * 8 + q), outer(f * 8 + 4 + q)))
    return fields + [outer(COARSE + f) for f in range(5)]


def edge_targets(fixed_bit, from_below):
    targets = []
    for f in range(5):
        for other in range(2):
            q = (fixed_bit if from_below else 0) + (3 - fixed_bit) * other
            targets.append([f * 8 + q, f * 8 + 4 + q])
    return targets + [[COARSE + f] for f in range(5)]


def is_deep(n):
    return DEEP <= n < COVER


def prepare(pos_ref, refined_ref, coarse_ref, fine_ref, place_ref, place_coarse_ref, inner_ref, send_ref, scr, scr_c):
    lane, x, y, z = positions(8)
    row = lax.broadcasted_iota(jnp.int32, (8, LANES), 0)
    left_half = lane < 64
    for f in range(5):
        for q in range(4):
            tile = fine_ref[f, :, q * 128 : q * 128 + 128]
            for ox in range(2):
                scr[f, pl.ds(ox * 4 + q, 4, stride=8), :] = tile[ox * 4 : ox * 4 + 4]
            part = coarse_ref[f, :, q * 128 : q * 128 + 128]
            scr_c[f, 2 * q : 2 * q + 1, :] = part
            scr_c[f, 2 * q + 1 : 2 * q + 2, :] = part
    sides = [[], []]
    rows = []
    for f in range(5):
        tile = [scr[f, c * 8 : c * 8 + 8, :] for c in range(4)]
        sides[0].append(
            jnp.concatenate([jnp.where(left_half, tile[2 * h], roll(tile[2 * h + 1], 64, 1)) for h in range(2)], axis=1)
        )
        sides[1].append(
            jnp.concatenate([jnp.where(left_half, roll(tile[2 * h], 64, 1), tile[2 * h + 1]) for h in range(2)], axis=1)
        )
        value = scr_c[f]
        rows.append(jnp.where((row & 1) == 1, roll(value, 64, 1), value))
    fine = place(jnp.concatenate(sides[0] + sides[1], axis=0), place_ref[...])
    coarse = place(jnp.concatenate(rows, axis=0), place_coarse_ref[...])
    coarse = [coarse[f * 8 : f * 8 + 8] for f in range(5)]

    covered = jnp.zeros((8, LANES), jnp.float32)
    for o in range(8):
        here = ((x >= 4) == (o >= 4)) & ((y >= 4) == (o % 4 >= 2)) & ((z >= 4) == (o % 2 == 1))
        covered = jnp.where(here, (refined_ref[o] > 0).astype(jnp.float32), covered)
    state = []
    for f in range(5):
        for q in range(8):
            first = (q // 4 * 5 + f) * 8
            part = fine[first : first + 8, q % 4 * 128 : q % 4 * 128 + 128]
            state.append(jnp.where(covered > 0.5, part, coarse[f]))
    state += coarse
    fastest = None
    for u in [[state[f * 8 + q] for f in range(5)] for q in range(8)] + [coarse]:
        v, pressure, sound = primitive(u)
        speed = jnp.abs(v[0]) + jnp.abs(v[1]) + jnp.abs(v[2]) + 3.0 * sound
        fastest = speed if fastest is None else jnp.maximum(fastest, speed)
    fastest = jnp.where(inside(y) & inside(z), fastest, 0.0)
    fastest = jnp.broadcast_to(jnp.max(fastest), (1, LANES))

    zero = jnp.zeros((8, LANES), jnp.float32)
    stored = state + [zero] * 5 + [covered]
    for n in range(COUNT):
        inner_ref[n] = stored[n]
    for t in range(8):
        send_ref[t, WHOLE : WHOLE + 1, :] = fastest
    for slot, at, step in ((pos_ref[0], 7, 1), (pos_ref[1], 0, -1)):
        for n in range(WHOLE):
            m = WHOLE + n // 2
            half = roll(stored[m - 5], step, 0) if is_deep(m) else stored[m]
            packed = jnp.where(lane < 80, stored[n], roll(half, 40 if n % 2 else 80, 1))
            send_ref[slot, n : n + 1, :] = packed[at : at + 1, :]


def forward_y(pos_ref, got_ref, inner_ref, outer_ref, send_ref):
    lane, x, y, z = positions(8)
    row = lax.broadcasted_iota(jnp.int32, (8, LANES), 0)
    up, down = pos_ref[0], pos_ref[1]
    fastest = got_ref[0, WHOLE : WHOLE + 1, :]
    for t in range(1, 8):
        fastest = jnp.maximum(fastest, got_ref[t, WHOLE : WHOLE + 1, :])
    fastest = jnp.broadcast_to(fastest, (8, LANES))
    outer = []
    for n in range(WHOLE):
        above = jnp.broadcast_to(got_ref[up, n : n + 1, :], (8, LANES))
        below = jnp.broadcast_to(got_ref[down, n : n + 1, :], (8, LANES))
        outer.append(jnp.where(row == 0, above, below))
    for n in range(0, WHOLE, 2):
        outer.append(jnp.where(lane < 40, roll(outer[n], -80, 1), roll(outer[n + 1], -40, 1)))
    for n in range(COUNT):
        outer_ref[n] = outer[n]
    for t in range(8):
        send_ref[t, ROWS1 - 8 : ROWS1, :] = fastest
    for slot, at, deep_at in ((pos_ref[2], 7, 6), (pos_ref[3], 0, 1)):
        items = [(inner_ref[n - 5], deep_at) if is_deep(n) else (inner_ref[n], at) for n in range(COUNT)]
        items += [(value, at) for value in rows_of(edge_fields(lambda n: outer[n], 2, at == 7))]
        for block in range(4):
            packed = fastest
            for s, (value, where) in enumerate(items[block * 16 : block * 16 + 16]):
                packed = jnp.where((lane >> 3) == s, roll(value, s * 8 - where * PITCH, 1), packed)
            send_ref[slot, block * 8 : block * 8 + 8, :] = packed


def forward_z(pos_ref, got_ref, inner_ref, outer_ref, inner_out, outer_out, send_ref):
    lane, x, y, z = positions(8)
    fastest = got_ref[0, ROWS1 - 8 : ROWS1, :]
    for t in range(1, 8):
        fastest = jnp.maximum(fastest, got_ref[t, ROWS1 - 8 : ROWS1, :])
    inner = [inner_ref[n] for n in range(COUNT)]
    outer = [outer_ref[n] for n in range(COUNT)]
    for slot, at, from_below in ((pos_ref[3], -1, True), (pos_ref[2], 8, False)):
        first = at * PITCH % LANES
        here = (lane >= first) & (lane < first + 8)
        for n in range(COUNT):
            block, s = n // 16, n % 16
            value = got_ref[slot, block * 8 : block * 8 + 8, :]
            inner[n] = jnp.where(here, roll(value, first - s * 8, 1), inner[n])
        targets = edge_targets(2, from_below)
        for j in range(4):
            merged = roll(got_ref[slot, 24:32, :], first - (COUNT % 16 + j) * 8, 1)
            for i, names in enumerate(targets[4 * j : 4 * j + 4]):
                value = roll(merged, -2 * i, 0)
                for n in names:
                    outer[n] = jnp.where(here, value, outer[n])
    for n in range(COUNT):
        inner_out[n] = inner[n]
        outer_out[n] = outer[n]

    for t in range(8):
        send_ref[t, ROWS2 - 8 : ROWS2, :] = fastest
    along = (lane * 205) >> 11
    slots = lane - along * PITCH
    for slot, at, deep_at in ((pos_ref[4], 7, 6), (pos_ref[5], 0, 1)):
        high = at == 7
        halves = []
        for n in range(FINE, COUNT):
            value, where = (inner[n - 5], deep_at) if is_deep(n) else (inner[n], at)
            halves += [(value, 80 - where), (value, 40 - where)]
        for value in rows_of(edge_fields(lambda n: outer[n], 1, high)):
            halves += [(value, 80 - at), (value, 40 - at)]
        columns = []
        for f in range(5):
            for a in range(2):
                q = a * 4 + high
                columns += [(inner[f * 8 + q + 2], at - PITCH), (inner[f * 8 + q], at + 8 * PITCH)]
        for f in range(5):
            columns += [(inner[COARSE + f], at - PITCH), (inner[COARSE + f], at + 8 * PITCH)]
        for block in range(4):
            packed = fastest
            for s in range(10):
                packed = jnp.where((slots == s) & (lane < 80), roll(inner[block * 10 + s], s - at, 1), packed)
            for s, (value, shift) in enumerate(halves[block * 10 : block * 10 + 10]):
                here = (slots == s) & (lane >= 80) & (lane < 120)
                packed = jnp.where(here, roll(value, shift + s, 1), packed)
            for s, (value, place_) in enumerate(columns[block * 8 : block * 8 + 8]):
                packed = jnp.where(lane == 120 + s, roll(value, 120 + s - place_, 1), packed)
            send_ref[slot, block * 8 : block * 8 + 8, :] = packed


def take_z(pos_ref, got_ref, inner_ref, outer_ref):
    lane, x, y, z = positions(8)
    inner = [inner_ref[n] for n in range(COUNT)]
    outer = [outer_ref[n] for n in range(COUNT)]
    for slot, at, from_below in ((pos_ref[5], -1, True), (pos_ref[4], 8, False)):
        got = [got_ref[slot, block * 8 : block * 8 + 8, :] for block in range(4)]
        here = (z == at) & inside(y)
        low = here & (y < 4)
        for n in range(FINE):
            inner[n] = jnp.where(here, roll(got[n // 10], at - n % 10, 1), inner[n])

        def whole(h):
            first = roll(got[h // 10], at - 80 - h % 10, 1)
            second = roll(got[(h + 1) // 10], at - 40 - (h + 1) % 10, 1)
            return jnp.where(low, first, second)

        for n in range(FINE, COUNT):
            inner[n] = jnp.where(here, whole(2 * (n - FINE)), inner[n])
        targets = edge_targets(1, from_below)
        for j in range(4):
            merged = whole(2 * (COUNT - FINE) + 2 * j)
            for i, names in enumerate(targets[4 * j : 4 * j + 4]):
                value = roll(merged, -2 * i, 0)
                for n in names:
                    outer[n] = jnp.where(here, value, outer[n])
        columns = []
        for f in range(5):
            for a in range(2):
                q = a * 4 + from_below
                columns += [(f * 8 + q + 2, -1), (f * 8 + q, 8)]
        for f in range(5):
            columns += [(COARSE + f, -1), (COARSE + f, 8)]
        for k, (n, side) in enumerate(columns):
            target = side * PITCH + at
            value = roll(got[k // 8], target - (120 + k % 8), 1)
            inner[n] = jnp.where(lane == target % LANES, value, inner[n])
    return [jnp.concatenate([i, o], axis=0) for i, o in zip(inner, outer)]


def advance(
    pos_ref, got_ref, inner_ref, outer_ref, back_ref, back_coarse_ref, coarse_out, fine_out, scr, scr_c
):
    lane, x, y, z = positions(16)
    fastest = got_ref[0, ROWS2 - 8 : ROWS2, :]
    for t in range(1, 8):
        fastest = jnp.maximum(fastest, got_ref[t, ROWS2 - 8 : ROWS2, :])
    fastest = jnp.where((lane[:8] >= 80) & (lane[:8] < 120), fastest, 0.0)
    fastest = jnp.broadcast_to(jnp.max(fastest), (8, LANES))
    half = 0.5 * (courant / fastest)
    half16 = jnp.concatenate([half, half], axis=0)

    state = take_z(pos_ref, got_ref, inner_ref, outer_ref)
    covered = state[COVER] > 0.5
    fine0 = [[state[f * 8 + q] for f in range(5)] for q in range(8)]
    coarse0 = state[COARSE:DEEP]

    net = coarse_net(coarse0, state[DEEP:COVER], (x, y, z))
    coarse1 = [u - 0.5 * half16 * n for u, n in zip(coarse0, net)]
    net = fine_net(fine0, False)
    fine1 = [
        [jnp.where(covered, fine0[q][f] - half16 * net[q][f], coarse1[f]) for f in range(5)] for q in range(8)
    ]
    net = coarse_net(coarse1, None, None)
    coarse2 = [0.5 * c0[:8] + 0.5 * (c1[:8] - 0.5 * half * n[:8]) for c0, c1, n in zip(coarse0, coarse1, net)]
    net = fine_net(fine1, True)
    mine = inside(y[:8]) & inside(z[:8])
    refined = mine & covered[:8]
    fine2 = [
        [
            jnp.where(refined, 0.5 * fine0[q][f][:8] + 0.5 * (fine1[q][f][:8] - half * net[q][f]), 0.0)
            for f in range(5)
        ]
        for q in range(8)
    ]
    coarse = []
    for f in range(5):
        total = functools.reduce(jnp.add, [fine2[q][f] for q in range(8)])
        coarse.append(jnp.where(mine, jnp.where(refined, 0.125 * total, coarse2[f]), 0.0))

    left_half = lane[:8] < 64
    rows = [jnp.concatenate([fine2[a * 4 + q][f] for q in range(4)], axis=1) for a in range(2) for f in range(5)]
    back = place(jnp.concatenate(rows, axis=0), back_ref[...])
    for f in range(5):
        for h in range(2):
            even = back[f * 8 : f * 8 + 8, h * 128 : h * 128 + 128]
            odd = back[40 + f * 8 : 48 + f * 8, h * 128 : h * 128 + 128]
            scr[f, h * 16 : h * 16 + 8, :] = jnp.where(left_half, even, roll(odd, 64, 1))
            scr[f, h * 16 + 8 : h * 16 + 16, :] = jnp.where(left_half, roll(even, 64, 1), odd)
        for q in range(4):
            for ox in range(2):
                tile = scr[f, pl.ds(ox * 4 + q, 4, stride=8), :]
                fine_out[f, ox * 4 : ox * 4 + 4, q * 128 : q * 128 + 128] = tile
    back = place(jnp.concatenate(coarse, axis=0), back_coarse_ref[...])
    for f in range(5):
        value = back[f * 8 : f * 8 + 8]
        value = jnp.where(left_half, value, roll(roll(value, 64, 1), -1, 0))
        for q in range(4):
            coarse_out[f, :, q * 128 : q * 128 + 128] = value[2 * q : 2 * q + 1]


def shape(*dims):
    return jax.ShapeDtypeStruct(dims, jnp.float32)


def call(kernel, kinds, outs, scratch, args):
    spaces = {"s": pltpu.SMEM, "v": pltpu.VMEM}
    return pl.pallas_call(
        kernel,
        out_shape=outs,
        in_specs=[pl.BlockSpec(memory_space=spaces[k]) for k in kinds],
        out_specs=[pl.BlockSpec(memory_space=pltpu.VMEM)] * len(outs),
        scratch_shapes=scratch,
        compiler_params=pltpu.CompilerParams(vmem_limit_bytes=32 * 1024 * 1024),
    )(*args)


def lines(count, dim):
    bits = count.bit_length() - 1
    mask = sum(1 << t for t in range(bits) if t % 3 == dim)
    groups = {}
    for device in range(count):
        groups.setdefault(device & ~mask, []).append(device)
    return list(groups.values())


def swap(block, dim):
    return lax.all_to_all(block, "boxes", 0, 0, axis_index_groups=lines(lax.axis_size("boxes"), dim))


def local(coarse_state, fine_state, refined):
    fine_place, coarse_place = placement()
    as_matrix = lambda m: jnp.asarray(np.ascontiguousarray(m).astype(ml_dtypes.bfloat16))
    device = lax.axis_index("boxes")
    pos = []
    for dim in range(3):
        here = sum(((device >> (3 * i + dim)) & 1) << i for i in range(3))
        pos += [(here + 1) & 7, (here + 7) & 7]
    pos = jnp.stack(pos).astype(jnp.int32)
    scratch = [pltpu.VMEM((5, 32, LANES), jnp.float32), pltpu.VMEM((5, 8, LANES), jnp.float32)]
    field = shape(COUNT, 8, LANES)

    inner, send = call(
        prepare,
        "ssvvvv",
        [field, shape(8, ROWS0, LANES)],
        scratch,
        (
            pos,
            refined[0],
            jnp.swapaxes(coarse_state, 0, 1),
            jnp.swapaxes(fine_state[0], 0, 1),
            as_matrix(fine_place),
            as_matrix(coarse_place),
        ),
    )
    got = swap(send, 0)
    outer, send = call(forward_y, "svv", [field, shape(8, ROWS1, LANES)], [], (pos, got, inner))
    got = swap(send, 1)
    inner, outer, send = call(
        forward_z, "svvv", [field, field, shape(8, ROWS2, LANES)], [], (pos, got, inner, outer)
    )
    got = swap(send, 2)
    coarse_out, fine_out = call(
        advance,
        "svvvvv",
        [shape(5, 1, 512), shape(5, 8, 512)],
        scratch,
        (pos, got, inner, outer, as_matrix(fine_place.T), as_matrix(coarse_place.T)),
    )
    return jnp.swapaxes(coarse_out, 0, 1), jnp.swapaxes(fine_out, 0, 1)[None]


def solution(mesh):
    in_specs = (P("boxes", None, None), P("boxes", None, None, None), P("boxes", None))
    out_specs = (P("boxes", None, None), P("boxes", None, None, None))
    return jax.shard_map(local, mesh=mesh, in_specs=in_specs, out_specs=out_specs, check_vma=False)
```

```python
import functools

import jax
import jax.numpy as jnp
import ml_dtypes
import numpy as np
from jax import lax
from jax.experimental import pallas as pl
from jax.experimental.pallas import tpu as pltpu
from jax.sharding import PartitionSpec as P

PITCH = 10
LANES = 128
FINE = 40
COARSE = FINE
DEEP = COARSE + 5
COVER = DEEP + 5
COUNT = COVER + 1
FACE = 28
ROWS = 32
MAX_LANE = 120
PAIRED = 26
SIDES = ((0, 8), (1, -1))
PAIRS = ((0, 1), (0, 2), (1, 2))
gamma_gas = 1.4
courant = 0.4


def placement():
    fine = np.zeros((256, 512), np.float32)
    coarse = np.zeros((128, 128), np.float32)
    for oy in range(2):
        for oz in range(2):
            for j in range(8):
                for k in range(8):
                    row = oy * 128 + oz * 64 + j * 8 + k
                    lane = (oy * 4 + j // 2) * PITCH + oz * 4 + k // 2
                    fine[row, (j % 2 * 2 + k % 2) * 128 + lane] = 1
    for j in range(8):
        for k in range(8):
            coarse[j * 8 + k, j * PITCH + k] = 1
    return fine, coarse


def place(values, matrix):
    high = values.astype(jnp.bfloat16)
    rest = values - high.astype(jnp.float32)
    middle = rest.astype(jnp.bfloat16)
    low = (rest - middle.astype(jnp.float32)).astype(jnp.bfloat16)
    rows = values.shape[0]
    parts = jnp.concatenate([high, middle, low], axis=0)
    out = jnp.dot(parts, matrix, preferred_element_type=jnp.float32)
    return out[:rows] + out[rows : 2 * rows] + out[2 * rows :]


def roll(x, shift, axis):
    shift = shift % x.shape[axis]
    return pltpu.roll(x, shift, axis) if shift else x


def positions(rows):
    row = lax.broadcasted_iota(jnp.int32, (rows, LANES), 0)
    lane = lax.broadcasted_iota(jnp.int32, (rows, LANES), 1)
    x = jnp.where(row > 8, row - 16, row)
    along = (lane + PITCH + 1) & (LANES - 1)
    y1 = (along * 205) >> 11
    return lane, x, y1 - 1, along - y1 * PITCH - 1


def inside(pos):
    return (pos >= 0) & (pos < 8)


def primitive(u):
    inverse = 1.0 / u[0]
    v = [u[1 + d] * inverse for d in range(3)]
    pressure = 0.4 * (u[4] - 0.5 * (u[1] * v[0] + u[2] * v[1] + u[3] * v[2]))
    sound = jnp.sqrt(gamma_gas * pressure * inverse)
    return v, pressure, sound


def cell_flux(u, prim, d):
    v, pressure, sound = prim
    flux = [u[1 + d]] + [u[1 + e] * v[d] for e in range(3)] + [(u[4] + pressure) * v[d]]
    flux[1 + d] = flux[1 + d] + pressure
    return list(u) + flux + [jnp.abs(v[d]) + sound]


def face(left, right):
    speed = jnp.maximum(left[10], right[10])
    return [(left[5 + f] + right[5 + f]) - speed * (right[f] - left[f]) for f in range(5)]


def ahead(x, d):
    return roll(x, -1, 0) if d == 0 else roll(x, -PITCH if d == 1 else -1, 1)


def behind(x, d):
    return roll(x, 1, 0) if d == 0 else roll(x, PITCH if d == 1 else 1, 1)


def fine_net(u, inner):
    prims = [primitive(u[q]) for q in range(8)]
    total = [None] * 8
    for d in range(3):
        bit = 4 >> d
        cut = (lambda x: x[:8]) if inner and d > 0 else (lambda x: x)
        keep = (lambda x: x[:8]) if inner else (lambda x: x)
        for low in range(8):
            if low & bit:
                continue
            high = low | bit
            cells = []
            for q in (low, high):
                v, pressure, sound = prims[q]
                cells.append(cell_flux([cut(x) for x in u[q]], ([cut(x) for x in v], cut(pressure), cut(sound)), d))
            middle = face(cells[0], cells[1])
            after = face(cells[1], [ahead(x, d) for x in cells[0]])
            net_low = [keep(middle[f] - behind(after[f], d)) for f in range(5)]
            net_high = [keep(after[f] - middle[f]) for f in range(5)]
            for q, net in ((low, net_low), (high, net_high)):
                total[q] = net if total[q] is None else [s + n for s, n in zip(total[q], net)]
    return total


def coarse_net(u, deep, pos):
    prim = primitive(u)
    prim_deep = None if deep is None else primitive(deep)
    total = None
    for d in range(3):
        cell = cell_flux(u, prim, d)
        right = [ahead(x, d) for x in cell]
        if deep is not None:
            outer = cell_flux(deep, prim_deep, d)
            last, first = pos[d] == 8, pos[d] == -1
            right = [jnp.where(last, o, r) for o, r in zip(outer, right)]
        after = face(cell, right)
        before = [behind(x, d) for x in after]
        if deep is not None:
            before = [jnp.where(first, o, b) for o, b in zip(face(outer, cell), before)]
        net = [a - b for a, b in zip(after, before)]
        total = net if total is None else [s + n for s, n in zip(total, net)]
    return total


def is_deep(n):
    return DEEP <= n < COVER


def fine_index(f, a, b, c):
    return f * 8 + a * 4 + b * 2 + c


def y_order(near):
    rest = [fine_index(f, a, 1 - near, c) for f in range(5) for a in range(2) for c in range(2)]
    first = [fine_index(f, 1, near, c) for c in range(2) for f in range(5)]
    second = [fine_index(f, 0, near, c) for c in range(2) for f in range(5)]
    return (
        first + [COARSE + f for f in range(5)] + rest[:1],
        second + [DEEP + f for f in range(5)] + [COVER],
        rest[1:17],
        rest[17:],
    )


def z_order(near):
    rest = [fine_index(f, a, b, 1 - near) for f in range(5) for a in range(2) for b in range(2)]
    first = [fine_index(f, 1, b, near) for b in range(2) for f in range(5)]
    second = [fine_index(f, 0, b, near) for b in range(2) for f in range(5)]
    return (
        (first, [COARSE + f for f in range(5)]),
        (second, [DEEP + f for f in range(5)]),
        (rest[:10], [COVER] + rest[10:14]),
        (rest[14:19], rest[19:]),
    )


def block_transpose(value):
    row = lax.broadcasted_iota(jnp.int32, (8, LANES), 0)
    group = lax.broadcasted_iota(jnp.int32, (8, LANES), 1) >> 4
    out = value
    for step in range(1, 8):
        moved = roll(roll(value, -16 * step, 1), step, 0)
        out = jnp.where(((row - group) & 7) == step, moved, out)
    return out


def swapped(flag, first, second):
    return jnp.where(flag, second, first), jnp.where(flag, first, second)


def prepare(
    pos_ref, refined_ref, coarse_ref, fine_ref, place_ref, place_coarse_ref, dense_ref, inner_ref, send_ref, scr, scr_c, scr_x
):
    lane, x, y, z = positions(8)
    row = lax.broadcasted_iota(jnp.int32, (8, LANES), 0)
    left_half = lane < 64
    for f in range(5):
        for q in range(4):
            tile = fine_ref[f, :, q * 128 : q * 128 + 128]
            for ox in range(2):
                scr[f, pl.ds(ox * 4 + q, 4, stride=8), :] = tile[ox * 4 : ox * 4 + 4]
            part = coarse_ref[f, :, q * 128 : q * 128 + 128]
            scr_c[f, 2 * q : 2 * q + 1, :] = part
            scr_c[f, 2 * q + 1 : 2 * q + 2, :] = part
    sides = [[], []]
    rows = []
    for f in range(5):
        tile = [scr[f, c * 8 : c * 8 + 8, :] for c in range(4)]
        sides[0].append(
            jnp.concatenate([jnp.where(left_half, tile[2 * h], roll(tile[2 * h + 1], 64, 1)) for h in range(2)], axis=1)
        )
        sides[1].append(
            jnp.concatenate([jnp.where(left_half, roll(tile[2 * h], 64, 1), tile[2 * h + 1]) for h in range(2)], axis=1)
        )
        value = scr_c[f]
        rows.append(jnp.where((row & 1) == 1, roll(value, 64, 1), value))
    fine = place(jnp.concatenate(sides[0] + sides[1], axis=0), place_ref[...])
    coarse = place(jnp.concatenate(rows, axis=0), place_coarse_ref[...])
    coarse = [coarse[f * 8 : f * 8 + 8] for f in range(5)]

    covered = jnp.zeros((8, LANES), jnp.float32)
    for o in range(8):
        here = ((x >= 4) == (o >= 4)) & ((y >= 4) == (o % 4 >= 2)) & ((z >= 4) == (o % 2 == 1))
        covered = jnp.where(here, (refined_ref[o] > 0).astype(jnp.float32), covered)
    state = []
    for f in range(5):
        for q in range(8):
            first = (q // 4 * 5 + f) * 8
            part = fine[first : first + 8, q % 4 * 128 : q % 4 * 128 + 128]
            state.append(jnp.where(covered > 0.5, part, coarse[f]))
    state += coarse
    fastest = None
    for u in [[state[f * 8 + q] for f in range(5)] for q in range(8)] + [coarse]:
        v, pressure, sound = primitive(u)
        speed = jnp.abs(v[0]) + jnp.abs(v[1]) + jnp.abs(v[2]) + 3.0 * sound
        fastest = speed if fastest is None else jnp.maximum(fastest, speed)
    fastest = jnp.where(inside(y) & inside(z), fastest, 0.0)
    fastest = jnp.broadcast_to(jnp.max(fastest), (8, LANES))

    zero = jnp.zeros((8, LANES), jnp.float32)
    stored = state + [zero] * 5 + [covered]
    for n in range(COUNT):
        inner_ref[n] = stored[n]

    own = pos_ref[0]
    far = [pos_ref[3 + d] for d in range(3)]
    for t in range(8):
        send_ref[t, 0, FACE - 1 : FACE, :] = fastest[:1]

    def taken(n, at, deep_at):
        return (stored[n - 5], deep_at) if is_deep(n) else (stored[n], at)

    for side, at, deep_at in ((0, 7, 6), (1, 0, 1)):
        for n in range(COUNT):
            value, where = taken(n, at, deep_at)
            target = side * 64 + (n if n < PAIRED else n - PAIRED + 32)
            scr_x[target : target + 1, :] = value[where : where + 1, :]
    dense = place(scr_x[...], dense_ref[...])
    left4 = lax.broadcasted_iota(jnp.int32, (32, LANES), 1) < 64
    row32 = lax.broadcasted_iota(jnp.int32, (32, LANES), 0)
    for side in range(2):
        packed = jnp.where(left4, dense[side * 64 : side * 64 + 32], roll(dense[side * 64 + 32 : side * 64 + 64], 64, 1))
        packed = jnp.where(row32 >= PAIRED, jnp.concatenate([fastest] * 4, axis=0), packed)
        send_ref[own ^ 1, far[0] if side == 0 else 1 - far[0]] = packed

    slots = lane - ((lane * 205) >> 11) * PITCH
    corners_xy, corners_xz, corners = [], [], zero
    for side, at, deep_at in ((0, 7, 6), (1, 0, 1)):
        near = 1 - side
        order = y_order(near)
        blocks = []
        for names in order:
            packed = fastest
            for s, n in enumerate(names):
                value, where = taken(n, at, deep_at)
                packed = jnp.where((lane >> 3) == s, roll(value, s * 8 - where * PITCH, 1), packed)
            blocks.append(packed)
        width = len(order[3]) * 8
        second = (lane >= width) & (lane < 2 * width)
        blocks[3] = jnp.where(second, roll(roll(blocks[3], width, 1), 4, 0), blocks[3])
        part = far[1] if side == 0 else 1 - far[1]
        for block in range(3):
            send_ref[own ^ 2, part, block * 8 : block * 8 + 8, :] = blocks[block]
        send_ref[own ^ 2, part, 24:FACE, :] = blocks[3][:4]
        corners_xy.append((blocks[0][7:8], jnp.where(lane < 80, blocks[1], blocks[0])[0:1]))

        blocks = []
        for block, (names, halves) in enumerate(z_order(near)):
            packed = fastest
            for s, n in enumerate(names):
                value, where = taken(n, at, deep_at)
                packed = jnp.where((slots == s) & (lane < 80), roll(value, s - where, 1), packed)
            if block < 3:
                extra = fastest
                for s, n in enumerate(halves):
                    value, where = taken(n, at, deep_at)
                    extra = jnp.where(slots == s, roll(value, s - where, 1), extra)
                extra = jnp.where(slots < 5, roll(extra, 80, 1), roll(extra, 45, 1))
                packed = jnp.where((lane >= 80) & (lane < MAX_LANE), extra, packed)
            else:
                second = (slots >= 5) & (lane < 80)
                packed = jnp.where(second, roll(roll(packed, 5, 1), 4, 0), packed)
                value = stored[halves[0]]
                lower = roll(value, 4, 0)
                pieces = [roll(value, 80 - at, 1), roll(value, 41 - at, 1), roll(lower, 82 - at, 1), roll(lower, 43 - at, 1)]
                for s, piece in enumerate(pieces):
                    packed = jnp.where((slots == s) & (lane >= 80) & (lane < MAX_LANE), piece, packed)
            blocks.append(packed)
        part = far[2] if side == 0 else 1 - far[2]
        for block in range(3):
            send_ref[own ^ 4, part, block * 8 : block * 8 + 8, :] = blocks[block]
        send_ref[own ^ 4, part, 24:FACE, :] = blocks[3][:4]
        corners_xz.append((blocks[0][7:8], jnp.where(lane < 80, blocks[1], blocks[0])[0:1]))
        for end, first, first_coarse in ((0, 75, 115), (1, 0, 80)):
            to = (side * 2 + end) * 16
            for start, source, i in ((first, blocks[0], 0), (first, blocks[1], 5), (first_coarse, blocks[0], 10)):
                here = (lane >= to + i) & (lane < to + i + 5)
                corners = jnp.where(here, roll(source, to + i - start, 1), corners)
    corners = block_transpose(corners)

    edges = [
        [[corners_xy[e][d] for e in range(2)] for d in range(2)],
        [[corners_xz[e][d] for e in range(2)] for d in range(2)],
        [[corners[e * 2 + d : e * 2 + d + 1] for e in range(2)] for d in range(2)],
    ]
    for (d, e), edge in zip(PAIRS, edges):
        upper, lower = [swapped(far[e] == 1, *half) for half in edge]
        near_near, far_near = swapped(far[d] == 1, upper[0], lower[0])
        near_far, far_far = swapped(far[d] == 1, upper[1], lower[1])
        for r, value in enumerate((near_near, near_far, far_near, far_far)):
            send_ref[own ^ (1 << d) ^ (1 << e), 0, r : r + 1, :] = value


def others(d):
    return [e for e in range(3) if e != d]


def pair(d, e):
    return (1 << d) ^ (1 << e)


def running_maximum(rows):
    fastest = functools.reduce(jnp.maximum, rows)
    lane = lax.broadcasted_iota(jnp.int32, fastest.shape, 1)
    fastest = jnp.where(lane >= MAX_LANE, fastest, 0.0)
    return jnp.broadcast_to(jnp.max(fastest), (1, LANES))


def pass_on(send_ref, own, fastest, faces, edges, corners):
    lane = lax.broadcasted_iota(jnp.int32, (1, LANES), 1)
    for t in range(8):
        send_ref[t, FACE - 1 : FACE, :] = fastest
    for d in range(3):
        slot = own ^ (1 << d)
        send_ref[slot, : FACE - 1, :] = faces[d](0, FACE - 1)
        last = faces[d](FACE - 1, FACE)
        send_ref[slot, FACE - 1 : FACE, :] = jnp.where(lane >= MAX_LANE, fastest, last)
        for r, value in enumerate(edges[d]):
            send_ref[slot, FACE + r : FACE + r + 1, :] = value
    for (d, e), value in zip(PAIRS, corners):
        send_ref[own ^ pair(d, e), 0:1, :] = value


def carry_once(pos_ref, got_ref, send_ref):
    own, to = pos_ref[0], pos_ref[1]
    fastest = running_maximum([got_ref[t, 0, FACE - 1 : FACE, :] for t in range(8)])
    faces = [lambda i, j, d=d: got_ref[own ^ (1 << d), 1, i:j, :] for d in range(3)]

    def edge(d, e, r):
        return got_ref[own ^ pair(d, e), 0, r : r + 1, :]

    edges = [[edge(d, e, 1 if e < d else 2) for e in others(d)] for d in range(3)]
    pass_on(send_ref, to, fastest, faces, edges, [edge(d, e, 3) for d, e in PAIRS])


def carry_twice(pos_ref, got_ref, send_ref):
    own, to = pos_ref[1], pos_ref[2]
    fastest = running_maximum([got_ref[t, FACE - 1 : FACE, :] for t in range(8)])
    faces = [lambda i, j, d=d: got_ref[own ^ (1 << d), i:j, :] for d in range(3)]

    def far_far(d, e):
        return got_ref[own ^ pair(d, e), 0:1, :]

    edges = []
    for d in range(3):
        passed = [got_ref[own ^ (1 << d), FACE + r : FACE + r + 1, :] for r in range(2)]
        edges.append(passed + [far_far(d, e) for e in others(d)])
    pass_on(send_ref, to, fastest, faces, edges, [far_far(d, e) for d, e in PAIRS])


def arrived(pos_ref, got0, got1, got2):
    own = [pos_ref[i] for i in range(3)]
    upper_far = [pos_ref[3 + d] == 1 for d in range(3)]
    twice = [pos_ref[6 + d] == 1 for d in range(3)]
    faces = []
    for d in range(3):
        near = got0[own[0] ^ (1 << d), 0]
        far = jnp.where(twice[d], got2[own[2] ^ (1 << d)], got1[own[1] ^ (1 << d)])
        faces.append(swapped(upper_far[d], near, far))

    def once(d, r):
        return got1[own[1] ^ (1 << d), FACE + r : FACE + r + 1, :]

    def again(d, r):
        return got2[own[2] ^ (1 << d), FACE + r : FACE + r + 1, :]

    edges = []
    for d, e in PAIRS:
        of_e, of_d = others(d).index(e), others(e).index(d)
        near_near = got0[own[0] ^ pair(d, e), 0, 0:1, :]
        near_far = jnp.where(twice[e], again(e, of_d), once(e, of_d))
        far_near = jnp.where(twice[d], again(d, of_e), once(d, of_e))
        both = jnp.where(twice[e], got2[own[2] ^ pair(d, e), 0:1, :], again(d, 2 + of_e))
        neither = jnp.where(twice[e], again(e, 2 + of_d), got1[own[1] ^ pair(d, e), 0:1, :])
        far_far = jnp.where(twice[d], both, neither)
        near, far = [swapped(upper_far[e], *half) for half in ((near_near, near_far), (far_near, far_far))]
        above, below = zip(*[swapped(upper_far[d], n, f) for n, f in zip(near, far)])
        edges.append((above, below))
    return faces, edges


def surround(faces, edges, inner_ref, spread_ref, scr_x):
    lane, x, y, z = positions(8)
    row = lax.broadcasted_iota(jnp.int32, (8, LANES), 0)
    left4 = lax.broadcasted_iota(jnp.int32, (32, LANES), 1) < 64
    inner = [inner_ref[n] for n in range(COUNT)]
    rows = []
    for side in range(2):
        value = faces[0][side]
        rows += [jnp.where(left4, value, 0.0), jnp.where(left4, roll(value, 64, 1), 0.0)]
    scr_x[...] = place(jnp.concatenate(rows, axis=0), spread_ref[...])
    outer = []
    for n in range(COUNT):
        at = n if n < PAIRED else n - PAIRED + 32
        above = jnp.broadcast_to(scr_x[at : at + 1, :], (8, LANES))
        below = jnp.broadcast_to(scr_x[at + 64 : at + 65, :], (8, LANES))
        outer.append(jnp.where(row == 0, above, below))

    def doubled(value):
        return jnp.concatenate([value[24:28], value[24:28]], axis=0)

    for side, (near, at) in enumerate(SIDES):
        blocks = [faces[1][side][block * 8 : block * 8 + 8] for block in range(3)]
        order = y_order(near)
        first = at * PITCH % LANES
        here = (lane >= first) & (lane < first + 8)
        for block, names in zip(blocks, order):
            for s, n in enumerate(names):
                inner[n] = jnp.where(here, roll(block, first - s * 8, 1), inner[n])
        last = doubled(faces[1][side])
        for s, n in enumerate(order[3]):
            value = jnp.where(row < 4, roll(last, first - s * 8, 1), roll(last, first - (s + len(order[3])) * 8, 1))
            inner[n] = jnp.where(here, value, inner[n])
        above, below = [jnp.broadcast_to(edges[0][end][side], (8, LANES)) for end in range(2)]
        edge = jnp.where(row == 0, above, below)
        for s in range(15):
            value = roll(edge, first - s * 8, 1)
            for n in (order[0][s], order[1][s]) if s < 10 else (order[0][s],):
                outer[n] = jnp.where(here, value, outer[n])

    columns = jnp.concatenate([edges[2][end][side] for side in range(2) for end in range(2)] * 2, axis=0)
    columns = block_transpose(columns)
    for side, (near, at) in enumerate(SIDES):
        blocks = [faces[2][side][block * 8 : block * 8 + 8] for block in range(3)]
        order = z_order(near)
        here = (z == at) & (y < 9)
        low_y = y < 4
        above, below = side * 32, side * 32 + 16

        def joined(block):
            return jnp.where(lane < 40, roll(block, -80, 1), roll(block, -45, 1))

        def ended(block, i, below_lane):
            block = jnp.where(lane < 80, block, roll(columns, 80 - above - i, 1))
            return jnp.where(lane >= below_lane, roll(columns, below_lane - below - i, 1), block)

        mains = [ended(blocks[0], 0, 123), ended(blocks[1], 5, 123), blocks[2]]
        halves = [ended(joined(blocks[0]), 10, 118), joined(blocks[1]), joined(blocks[2])]
        for block in range(3):
            for source, names in ((mains[block], order[block][0]), (halves[block], order[block][1])):
                for s, n in enumerate(names):
                    inner[n] = jnp.where(here, roll(source, at - s, 1), inner[n])
        last = doubled(faces[2][side])
        for s, n in enumerate(order[3][0]):
            value = jnp.where(row < 4, roll(last, at - s, 1), roll(last, at - 5 - s, 1))
            inner[n] = jnp.where(here, value, inner[n])
        upper_rows = jnp.where(low_y, roll(last, at - 80, 1), roll(last, at - 41, 1))
        lower_rows = jnp.where(low_y, roll(last, at - 82, 1), roll(last, at - 43, 1))
        n = order[3][1][0]
        inner[n] = jnp.where(here, jnp.where(row < 4, upper_rows, lower_rows), inner[n])

        above, below = [jnp.broadcast_to(edges[1][end][side], (8, LANES)) for end in range(2)]
        edge = jnp.where(row == 0, above, below)
        for s in range(10):
            value = roll(edge, at - s, 1)
            for n in (order[0][0][s], order[1][0][s]):
                outer[n] = jnp.where(here & inside(y), value, outer[n])
        edge = joined(edge)
        for s in range(5):
            n = COARSE + s
            outer[n] = jnp.where(here & inside(y), roll(edge, at - s, 1), outer[n])
    return [jnp.concatenate([i, o], axis=0) for i, o in zip(inner, outer)]


def advance(
    pos_ref, got0, got1, got2, inner_ref, spread_ref, back_ref, back_coarse_ref, coarse_out, fine_out, scr, scr_x
):
    lane, x, y, z = positions(16)
    fastest = running_maximum([got2[t, FACE - 1 : FACE, :] for t in range(8)])
    half16 = 0.5 * (courant / jnp.broadcast_to(fastest, (16, LANES)))
    half = half16[:8]
    faces, edges = arrived(pos_ref, got0, got1, got2)
    state = surround(faces, edges, inner_ref, spread_ref, scr_x)
    covered = state[COVER] > 0.5
    fine0 = [[state[f * 8 + q] for f in range(5)] for q in range(8)]
    coarse0 = state[COARSE:DEEP]

    net = coarse_net(coarse0, state[DEEP:COVER], (x, y, z))
    coarse1 = [u - 0.5 * half16 * n for u, n in zip(coarse0, net)]
    net = fine_net(fine0, False)
    fine1 = [
        [jnp.where(covered, fine0[q][f] - half16 * net[q][f], coarse1[f]) for f in range(5)] for q in range(8)
    ]
    net = coarse_net(coarse1, None, None)
    coarse2 = [0.5 * c0[:8] + 0.5 * (c1[:8] - 0.5 * half * n[:8]) for c0, c1, n in zip(coarse0, coarse1, net)]
    net = fine_net(fine1, True)
    mine = inside(y[:8]) & inside(z[:8])
    refined = mine & covered[:8]
    fine2 = [
        [
            jnp.where(refined, 0.5 * fine0[q][f][:8] + 0.5 * (fine1[q][f][:8] - half * net[q][f]), 0.0)
            for f in range(5)
        ]
        for q in range(8)
    ]
    coarse = []
    for f in range(5):
        total = functools.reduce(jnp.add, [fine2[q][f] for q in range(8)])
        coarse.append(jnp.where(mine, jnp.where(refined, 0.125 * total, coarse2[f]), 0.0))

    left_half = lane[:8] < 64
    rows = [jnp.concatenate([fine2[a * 4 + q][f] for q in range(4)], axis=1) for a in range(2) for f in range(5)]
    back = place(jnp.concatenate(rows, axis=0), back_ref[...])
    for f in range(5):
        for h in range(2):
            even = back[f * 8 : f * 8 + 8, h * 128 : h * 128 + 128]
            odd = back[40 + f * 8 : 48 + f * 8, h * 128 : h * 128 + 128]
            scr[f, h * 16 : h * 16 + 8, :] = jnp.where(left_half, even, roll(odd, 64, 1))
            scr[f, h * 16 + 8 : h * 16 + 16, :] = jnp.where(left_half, roll(even, 64, 1), odd)
        for q in range(4):
            for ox in range(2):
                tile = scr[f, pl.ds(ox * 4 + q, 4, stride=8), :]
                fine_out[f, ox * 4 : ox * 4 + 4, q * 128 : q * 128 + 128] = tile
    back = place(jnp.concatenate(coarse, axis=0), back_coarse_ref[...])
    for f in range(5):
        value = back[f * 8 : f * 8 + 8]
        value = jnp.where(left_half, value, roll(roll(value, 64, 1), -1, 0))
        for q in range(4):
            coarse_out[f, :, q * 128 : q * 128 + 128] = value[2 * q : 2 * q + 1]


def shape(*dims):
    return jax.ShapeDtypeStruct(dims, jnp.float32)


def call(kernel, kinds, outs, scratch, args):
    spaces = {"s": pltpu.SMEM, "v": pltpu.VMEM}
    return pl.pallas_call(
        kernel,
        out_shape=outs,
        in_specs=[pl.BlockSpec(memory_space=spaces[k]) for k in kinds],
        out_specs=[pl.BlockSpec(memory_space=pltpu.VMEM)] * len(outs),
        scratch_shapes=[pltpu.VMEM(dims, jnp.float32) for dims in scratch],
        compiler_params=pltpu.CompilerParams(vmem_limit_bytes=32 * 1024 * 1024),
    )(*args)


def swap(block, level):
    count = lax.axis_size("boxes")
    mask = 7 << (3 * level)
    groups = {}
    for device in range(count):
        groups.setdefault(device & ~mask, []).append(device)
    return lax.all_to_all(block, "boxes", 0, 0, axis_index_groups=list(groups.values()))


def local(coarse_state, fine_state, refined):
    fine_place, coarse_place = placement()
    as_matrix = lambda m: jnp.asarray(np.ascontiguousarray(m).astype(ml_dtypes.bfloat16))
    device = lax.axis_index("boxes")
    levels = [(device >> (3 * level)) & 7 for level in range(3)]
    bits = [[(level >> d) & 1 for d in range(3)] for level in levels]
    twice = [(bits[0][d] == bits[1][d]).astype(jnp.int32) for d in range(3)]
    pos = jnp.stack(levels + bits[0] + twice).astype(jnp.int32)
    spread, dense = as_matrix(coarse_place), as_matrix(coarse_place.T)

    inner, send = call(
        prepare,
        "ssvvvvv",
        [shape(COUNT, 8, LANES), shape(8, 2, ROWS, LANES)],
        [(5, 32, LANES), (5, 8, LANES), (128, LANES)],
        (
            pos,
            refined[0],
            jnp.swapaxes(coarse_state, 0, 1),
            jnp.swapaxes(fine_state[0], 0, 1),
            as_matrix(fine_place),
            spread,
            dense,
        ),
    )
    got0 = swap(send, 0)
    got1 = swap(call(carry_once, "sv", [shape(8, ROWS, LANES)], [], (pos, got0))[0], 1)
    got2 = swap(call(carry_twice, "sv", [shape(8, ROWS, LANES)], [], (pos, got1))[0], 2)
    coarse_out, fine_out = call(
        advance,
        "svvvvvvv",
        [shape(5, 1, 512), shape(5, 8, 512)],
        [(5, 32, LANES), (128, LANES)],
        (pos, got0, got1, got2, inner, spread, as_matrix(fine_place.T), dense),
    )
    return jnp.swapaxes(coarse_out, 0, 1), jnp.swapaxes(fine_out, 0, 1)[None]


def solution(mesh):
    in_specs = (P("boxes", None, None), P("boxes", None, None, None), P("boxes", None))
    out_specs = (P("boxes", None, None), P("boxes", None, None, None))
    return jax.shard_map(local, mesh=mesh, in_specs=in_specs, out_specs=out_specs, check_vma=False)
```

```python
import functools

import jax
import jax.numpy as jnp
import ml_dtypes
import numpy as np
from jax import lax
from jax.experimental import pallas as pl
from jax.experimental.pallas import tpu as pltpu
from jax.sharding import PartitionSpec as P

PITCH = 10
LANES = 128
FINE = 40
COARSE = FINE
DEEP = COARSE + 5
COVER = DEEP + 5
COUNT = COVER + 1
FACE = 28
ROWS = 32
MAX_LANE = 120
PAIRED = 26
LEAD = (1, 4, 4)
SIDES = ((0, 8), (1, -1))
PAIRS = ((0, 1), (0, 2), (1, 2))
gamma_gas = 1.4
courant = 0.4


def placement():
    fine = np.zeros((256, 512), np.float32)
    coarse = np.zeros((128, 128), np.float32)
    for oy in range(2):
        for oz in range(2):
            for j in range(8):
                for k in range(8):
                    row = oy * 128 + oz * 64 + j * 8 + k
                    lane = (oy * 4 + j // 2) * PITCH + oz * 4 + k // 2
                    fine[row, (j % 2 * 2 + k % 2) * 128 + lane] = 1
    for j in range(8):
        for k in range(8):
            coarse[j * 8 + k, j * PITCH + k] = 1
    return fine, coarse


def place(values, matrix):
    high = values.astype(jnp.bfloat16)
    rest = values - high.astype(jnp.float32)
    middle = rest.astype(jnp.bfloat16)
    low = (rest - middle.astype(jnp.float32)).astype(jnp.bfloat16)
    rows = values.shape[0]
    parts = jnp.concatenate([high, middle, low], axis=0)
    out = jnp.dot(parts, matrix, preferred_element_type=jnp.float32)
    return out[:rows] + out[rows : 2 * rows] + out[2 * rows :]


def roll(x, shift, axis):
    shift = shift % x.shape[axis]
    return pltpu.roll(x, shift, axis) if shift else x


def positions(rows):
    row = lax.broadcasted_iota(jnp.int32, (rows, LANES), 0)
    lane = lax.broadcasted_iota(jnp.int32, (rows, LANES), 1)
    x = jnp.where(row > 8, row - 16, row)
    along = (lane + PITCH + 1) & (LANES - 1)
    y1 = (along * 205) >> 11
    return lane, x, y1 - 1, along - y1 * PITCH - 1


def inside(pos):
    return (pos >= 0) & (pos < 8)


def primitive(u):
    inverse = 1.0 / u[0]
    v = [u[1 + d] * inverse for d in range(3)]
    pressure = 0.4 * (u[4] - 0.5 * (u[1] * v[0] + u[2] * v[1] + u[3] * v[2]))
    sound = jnp.sqrt(gamma_gas * pressure * inverse)
    return v, pressure, sound


def cell_flux(u, prim, d):
    v, pressure, sound = prim
    flux = [u[1 + d]] + [u[1 + e] * v[d] for e in range(3)] + [(u[4] + pressure) * v[d]]
    flux[1 + d] = flux[1 + d] + pressure
    return list(u) + flux + [jnp.abs(v[d]) + sound]


def face(left, right):
    speed = jnp.maximum(left[10], right[10])
    return [(left[5 + f] + right[5 + f]) - speed * (right[f] - left[f]) for f in range(5)]


def ahead(x, d):
    return roll(x, -1, 0) if d == 0 else roll(x, -PITCH if d == 1 else -1, 1)


def behind(x, d):
    return roll(x, 1, 0) if d == 0 else roll(x, PITCH if d == 1 else 1, 1)


def fine_net(u, inner):
    prims = [primitive(u[q]) for q in range(8)]
    total = [None] * 8
    for d in range(3):
        bit = 4 >> d
        cut = (lambda x: x[:8]) if inner and d > 0 else (lambda x: x)
        keep = (lambda x: x[:8]) if inner else (lambda x: x)
        for low in range(8):
            if low & bit:
                continue
            high = low | bit
            cells = []
            for q in (low, high):
                v, pressure, sound = prims[q]
                cells.append(cell_flux([cut(x) for x in u[q]], ([cut(x) for x in v], cut(pressure), cut(sound)), d))
            middle = face(cells[0], cells[1])
            after = face(cells[1], [ahead(x, d) for x in cells[0]])
            net_low = [keep(middle[f] - behind(after[f], d)) for f in range(5)]
            net_high = [keep(after[f] - middle[f]) for f in range(5)]
            for q, net in ((low, net_low), (high, net_high)):
                total[q] = net if total[q] is None else [s + n for s, n in zip(total[q], net)]
    return total


def coarse_net(u, deep, pos):
    prim = primitive(u)
    prim_deep = None if deep is None else primitive(deep)
    total = None
    for d in range(3):
        cell = cell_flux(u, prim, d)
        right = [ahead(x, d) for x in cell]
        if deep is not None:
            outer = cell_flux(deep, prim_deep, d)
            last, first = pos[d] == 8, pos[d] == -1
            right = [jnp.where(last, o, r) for o, r in zip(outer, right)]
        after = face(cell, right)
        before = [behind(x, d) for x in after]
        if deep is not None:
            before = [jnp.where(first, o, b) for o, b in zip(face(outer, cell), before)]
        net = [a - b for a, b in zip(after, before)]
        total = net if total is None else [s + n for s, n in zip(total, net)]
    return total


def is_deep(n):
    return DEEP <= n < COVER


def fine_index(f, a, b, c):
    return f * 8 + a * 4 + b * 2 + c


def y_order(near):
    rest = [fine_index(f, a, 1 - near, c) for f in range(5) for a in range(2) for c in range(2)]
    first = [fine_index(f, 1, near, c) for c in range(2) for f in range(5)]
    second = [fine_index(f, 0, near, c) for c in range(2) for f in range(5)]
    return (
        first + [COARSE + f for f in range(5)] + rest[:1],
        second + [DEEP + f for f in range(5)] + [COVER],
        rest[1:17],
        rest[17:],
    )


def z_order(near):
    rest = [fine_index(f, a, b, 1 - near) for f in range(5) for a in range(2) for b in range(2)]
    first = [fine_index(f, 1, b, near) for b in range(2) for f in range(5)]
    second = [fine_index(f, 0, b, near) for b in range(2) for f in range(5)]
    return (
        (first, [COARSE + f for f in range(5)]),
        (second, [DEEP + f for f in range(5)]),
        (rest[:10], [COVER] + rest[10:14]),
        (rest[14:19], rest[19:]),
    )


def block_transpose(value):
    row = lax.broadcasted_iota(jnp.int32, (8, LANES), 0)
    group = lax.broadcasted_iota(jnp.int32, (8, LANES), 1) >> 4
    out = value
    for step in range(1, 8):
        moved = roll(roll(value, -16 * step, 1), step, 0)
        out = jnp.where(((row - group) & 7) == step, moved, out)
    return out


def swapped(flag, first, second):
    return jnp.where(flag, second, first), jnp.where(flag, first, second)


def prepare(
    pos_ref, refined_ref, coarse_ref, fine_ref, place_ref, place_coarse_ref, dense_ref, inner_ref, send_ref, scr, scr_c, scr_x
):
    lane, x, y, z = positions(8)
    row = lax.broadcasted_iota(jnp.int32, (8, LANES), 0)
    left_half = lane < 64
    for f in range(5):
        for q in range(4):
            tile = fine_ref[f, :, q * 128 : q * 128 + 128]
            for ox in range(2):
                scr[f, pl.ds(ox * 4 + q, 4, stride=8), :] = tile[ox * 4 : ox * 4 + 4]
            part = coarse_ref[f, :, q * 128 : q * 128 + 128]
            scr_c[f, 2 * q : 2 * q + 1, :] = part
            scr_c[f, 2 * q + 1 : 2 * q + 2, :] = part
    sides = [[], []]
    rows = []
    for f in range(5):
        tile = [scr[f, c * 8 : c * 8 + 8, :] for c in range(4)]
        sides[0].append(
            jnp.concatenate([jnp.where(left_half, tile[2 * h], roll(tile[2 * h + 1], 64, 1)) for h in range(2)], axis=1)
        )
        sides[1].append(
            jnp.concatenate([jnp.where(left_half, roll(tile[2 * h], 64, 1), tile[2 * h + 1]) for h in range(2)], axis=1)
        )
        value = scr_c[f]
        rows.append(jnp.where((row & 1) == 1, roll(value, 64, 1), value))
    fine = place(jnp.concatenate(sides[0] + sides[1], axis=0), place_ref[...])
    coarse = place(jnp.concatenate(rows, axis=0), place_coarse_ref[...])
    coarse = [coarse[f * 8 : f * 8 + 8] for f in range(5)]

    covered = jnp.zeros((8, LANES), jnp.float32)
    for o in range(8):
        here = ((x >= 4) == (o >= 4)) & ((y >= 4) == (o % 4 >= 2)) & ((z >= 4) == (o % 2 == 1))
        covered = jnp.where(here, (refined_ref[o] > 0).astype(jnp.float32), covered)
    state = []
    for f in range(5):
        for q in range(8):
            first = (q // 4 * 5 + f) * 8
            part = fine[first : first + 8, q % 4 * 128 : q % 4 * 128 + 128]
            state.append(jnp.where(covered > 0.5, part, coarse[f]))
    state += coarse
    fastest = None
    for u in [[state[f * 8 + q] for f in range(5)] for q in range(8)] + [coarse]:
        v, pressure, sound = primitive(u)
        speed = jnp.abs(v[0]) + jnp.abs(v[1]) + jnp.abs(v[2]) + 3.0 * sound
        fastest = speed if fastest is None else jnp.maximum(fastest, speed)
    fastest = jnp.where(inside(y) & inside(z), fastest, 0.0)
    fastest = jnp.broadcast_to(jnp.max(fastest), (8, LANES))

    zero = jnp.zeros((8, LANES), jnp.float32)
    stored = state + [zero] * 5 + [covered]
    for n in range(COUNT):
        inner_ref[n] = stored[n]

    own = pos_ref[0]
    far = [pos_ref[3 + d] for d in range(3)]
    for t in range(8):
        send_ref[t, 0, FACE - 1 : FACE, :] = fastest[:1]

    def taken(n, at, deep_at):
        return (stored[n - 5], deep_at) if is_deep(n) else (stored[n], at)

    for side, at, deep_at in ((0, 7, 6), (1, 0, 1)):
        for n in range(COUNT):
            value, where = taken(n, at, deep_at)
            target = side * 64 + (n if n < PAIRED else n - PAIRED + 32)
            scr_x[target : target + 1, :] = value[where : where + 1, :]
    dense = place(scr_x[...], dense_ref[...])
    left4 = lax.broadcasted_iota(jnp.int32, (32, LANES), 1) < 64
    row32 = lax.broadcasted_iota(jnp.int32, (32, LANES), 0)
    for side in range(2):
        packed = jnp.where(left4, dense[side * 64 : side * 64 + 32], roll(dense[side * 64 + 32 : side * 64 + 64], 64, 1))
        packed = jnp.where(row32 >= PAIRED, jnp.concatenate([fastest] * 4, axis=0), packed)
        send_ref[own ^ 1, far[0] if side == 0 else 1 - far[0]] = packed

    slots = lane - ((lane * 205) >> 11) * PITCH
    corners_xy, corners_xz, corners = [], [], zero
    for side, at, deep_at in ((0, 7, 6), (1, 0, 1)):
        near = 1 - side
        order = y_order(near)
        blocks = []
        for names in order:
            packed = fastest
            for s, n in enumerate(names):
                value, where = taken(n, at, deep_at)
                packed = jnp.where((lane >> 3) == s, roll(value, s * 8 - where * PITCH, 1), packed)
            blocks.append(packed)
        width = len(order[3]) * 8
        second = (lane >= width) & (lane < 2 * width)
        blocks[3] = jnp.where(second, roll(roll(blocks[3], width, 1), 4, 0), blocks[3])
        part = far[1] if side == 0 else 1 - far[1]
        for block in range(3):
            send_ref[own ^ 2, part, block * 8 : block * 8 + 8, :] = blocks[block]
        send_ref[own ^ 2, part, 24:FACE, :] = blocks[3][:4]
        corners_xy.append((blocks[0][7:8], jnp.where(lane < 80, blocks[1], blocks[0])[0:1]))

        blocks = []
        for block, (names, halves) in enumerate(z_order(near)):
            packed = fastest
            for s, n in enumerate(names):
                value, where = taken(n, at, deep_at)
                packed = jnp.where((slots == s) & (lane < 80), roll(value, s - where, 1), packed)
            if block < 3:
                extra = fastest
                for s, n in enumerate(halves):
                    value, where = taken(n, at, deep_at)
                    extra = jnp.where(slots == s, roll(value, s - where, 1), extra)
                extra = jnp.where(slots < 5, roll(extra, 80, 1), roll(extra, 45, 1))
                packed = jnp.where((lane >= 80) & (lane < MAX_LANE), extra, packed)
            else:
                second = (slots >= 5) & (lane < 80)
                packed = jnp.where(second, roll(roll(packed, 5, 1), 4, 0), packed)
                value = stored[halves[0]]
                lower = roll(value, 4, 0)
                pieces = [roll(value, 80 - at, 1), roll(value, 41 - at, 1), roll(lower, 82 - at, 1), roll(lower, 43 - at, 1)]
                for s, piece in enumerate(pieces):
                    packed = jnp.where((slots == s) & (lane >= 80) & (lane < MAX_LANE), piece, packed)
            blocks.append(packed)
        part = far[2] if side == 0 else 1 - far[2]
        for block in range(3):
            send_ref[own ^ 4, part, block * 8 : block * 8 + 8, :] = blocks[block]
        send_ref[own ^ 4, part, 24:FACE, :] = blocks[3][:4]
        corners_xz.append((blocks[0][7:8], jnp.where(lane < 80, blocks[1], blocks[0])[0:1]))
        for end, first, first_coarse in ((0, 75, 115), (1, 0, 80)):
            to = (side * 2 + end) * 16
            for start, source, i in ((first, blocks[0], 0), (first, blocks[1], 5), (first_coarse, blocks[0], 10)):
                here = (lane >= to + i) & (lane < to + i + 5)
                corners = jnp.where(here, roll(source, to + i - start, 1), corners)
    corners = block_transpose(corners)

    edges = [
        [[corners_xy[e][d] for e in range(2)] for d in range(2)],
        [[corners_xz[e][d] for e in range(2)] for d in range(2)],
        [[corners[e * 2 + d : e * 2 + d + 1] for e in range(2)] for d in range(2)],
    ]
    for (d, e), edge in zip(PAIRS, edges):
        upper, lower = [swapped(far[e] == 1, *half) for half in edge]
        near_near, far_near = swapped(far[d] == 1, upper[0], lower[0])
        near_far, far_far = swapped(far[d] == 1, upper[1], lower[1])
        for r, value in enumerate((near_near, near_far, far_near, far_far)):
            send_ref[own ^ (1 << d) ^ (1 << e), 0, r : r + 1, :] = value


def others(d):
    return [e for e in range(3) if e != d]


def pair(d, e):
    return (1 << d) ^ (1 << e)


def running_maximum(rows):
    fastest = functools.reduce(jnp.maximum, rows)
    lane = lax.broadcasted_iota(jnp.int32, fastest.shape, 1)
    fastest = jnp.where(lane >= MAX_LANE, fastest, 0.0)
    return jnp.broadcast_to(jnp.max(fastest), (1, LANES))


def pass_on(send_ref, own, fastest, faces, edges, corners):
    lane = lax.broadcasted_iota(jnp.int32, (1, LANES), 1)
    for t in range(8):
        send_ref[t, FACE - 1 : FACE, :] = fastest
    for d in range(3):
        slot = own ^ (1 << d)
        send_ref[slot, : FACE - 1, :] = faces[d](0, FACE - 1)
        last = faces[d](FACE - 1, FACE)
        send_ref[slot, FACE - 1 : FACE, :] = jnp.where(lane >= MAX_LANE, fastest, last)
        for r, value in enumerate(edges[d]):
            send_ref[slot, FACE + r : FACE + r + 1, :] = value
    for (d, e), value in zip(PAIRS, corners):
        send_ref[own ^ pair(d, e), 0:1, :] = value


def carry_once(pos_ref, got_ref, send_ref):
    own, to = pos_ref[0], pos_ref[1]
    fastest = running_maximum([got_ref[t, 0, FACE - 1 : FACE, :] for t in range(8)])
    faces = [lambda i, j, d=d: got_ref[own ^ (1 << d), 1, i:j, :] for d in range(3)]

    def edge(d, e, r):
        return got_ref[own ^ pair(d, e), 0, r : r + 1, :]

    edges = [[edge(d, e, 1 if e < d else 2) for e in others(d)] for d in range(3)]
    pass_on(send_ref, to, fastest, faces, edges, [edge(d, e, 3) for d, e in PAIRS])


def carry_twice(pos_ref, got_ref, send_ref):
    own, to = pos_ref[1], pos_ref[2]
    fastest = running_maximum([got_ref[t, FACE - 1 : FACE, :] for t in range(8)])
    faces = [lambda i, j, d=d: got_ref[own ^ (1 << d), i:j, :] for d in range(3)]

    def far_far(d, e):
        return got_ref[own ^ pair(d, e), 0:1, :]

    edges = []
    for d in range(3):
        passed = [got_ref[own ^ (1 << d), FACE + r : FACE + r + 1, :] for r in range(2)]
        edges.append(passed + [far_far(d, e) for e in others(d)])
    pass_on(send_ref, to, fastest, faces, edges, [far_far(d, e) for d, e in PAIRS])


def arrived(pos_ref, got0, got1, got2):
    own = [pos_ref[i] for i in range(3)]
    upper_far = [pos_ref[3 + d] == 1 for d in range(3)]
    twice = [pos_ref[6 + d] == 1 for d in range(3)]
    faces = []
    for d in range(3):
        near = got0[own[0] ^ (1 << d), 0]
        far = jnp.where(twice[d], got2[own[2] ^ (1 << d)], got1[own[1] ^ (1 << d)])
        faces.append(swapped(upper_far[d], near, far))

    def once(d, r):
        return got1[own[1] ^ (1 << d), FACE + r : FACE + r + 1, :]

    def again(d, r):
        return got2[own[2] ^ (1 << d), FACE + r : FACE + r + 1, :]

    edges = []
    for d, e in PAIRS:
        of_e, of_d = others(d).index(e), others(e).index(d)
        near_near = got0[own[0] ^ pair(d, e), 0, 0:1, :]
        near_far = jnp.where(twice[e], again(e, of_d), once(e, of_d))
        far_near = jnp.where(twice[d], again(d, of_e), once(d, of_e))
        both = jnp.where(twice[e], got2[own[2] ^ pair(d, e), 0:1, :], again(d, 2 + of_e))
        neither = jnp.where(twice[e], again(e, 2 + of_d), got1[own[1] ^ pair(d, e), 0:1, :])
        far_far = jnp.where(twice[d], both, neither)
        near, far = [swapped(upper_far[e], *half) for half in ((near_near, near_far), (far_near, far_far))]
        above, below = zip(*[swapped(upper_far[d], n, f) for n, f in zip(near, far)])
        edges.append((above, below))
    return faces, edges


def surround(faces, edges, inner_ref, spread_ref, scr_x):
    lane, x, y, z = positions(8)
    row = lax.broadcasted_iota(jnp.int32, (8, LANES), 0)
    left4 = lax.broadcasted_iota(jnp.int32, (32, LANES), 1) < 64
    inner = [inner_ref[n] for n in range(COUNT)]
    rows = []
    for side in range(2):
        value = faces[0][side]
        rows += [jnp.where(left4, value, 0.0), jnp.where(left4, roll(value, 64, 1), 0.0)]
    scr_x[...] = place(jnp.concatenate(rows, axis=0), spread_ref[...])
    outer = []
    for n in range(COUNT):
        at = n if n < PAIRED else n - PAIRED + 32
        above = jnp.broadcast_to(scr_x[at : at + 1, :], (8, LANES))
        below = jnp.broadcast_to(scr_x[at + 64 : at + 65, :], (8, LANES))
        outer.append(jnp.where(row == 0, above, below))

    def doubled(value):
        return jnp.concatenate([value[24:28], value[24:28]], axis=0)

    for side, (near, at) in enumerate(SIDES):
        blocks = [faces[1][side][block * 8 : block * 8 + 8] for block in range(3)]
        order = y_order(near)
        first = at * PITCH % LANES
        here = (lane >= first) & (lane < first + 8)
        for block, names in zip(blocks, order):
            for s, n in enumerate(names):
                inner[n] = jnp.where(here, roll(block, first - s * 8, 1), inner[n])
        last = doubled(faces[1][side])
        for s, n in enumerate(order[3]):
            value = jnp.where(row < 4, roll(last, first - s * 8, 1), roll(last, first - (s + len(order[3])) * 8, 1))
            inner[n] = jnp.where(here, value, inner[n])
        above, below = [jnp.broadcast_to(edges[0][end][side], (8, LANES)) for end in range(2)]
        edge = jnp.where(row == 0, above, below)
        for s in range(15):
            value = roll(edge, first - s * 8, 1)
            for n in (order[0][s], order[1][s]) if s < 10 else (order[0][s],):
                outer[n] = jnp.where(here, value, outer[n])

    columns = jnp.concatenate([edges[2][end][side] for side in range(2) for end in range(2)] * 2, axis=0)
    columns = block_transpose(columns)
    for side, (near, at) in enumerate(SIDES):
        blocks = [faces[2][side][block * 8 : block * 8 + 8] for block in range(3)]
        order = z_order(near)
        here = (z == at) & (y < 9)
        low_y = y < 4
        above, below = side * 32, side * 32 + 16

        def joined(block):
            return jnp.where(lane < 40, roll(block, -80, 1), roll(block, -45, 1))

        def ended(block, i, below_lane):
            block = jnp.where(lane < 80, block, roll(columns, 80 - above - i, 1))
            return jnp.where(lane >= below_lane, roll(columns, below_lane - below - i, 1), block)

        mains = [ended(blocks[0], 0, 123), ended(blocks[1], 5, 123), blocks[2]]
        halves = [ended(joined(blocks[0]), 10, 118), joined(blocks[1]), joined(blocks[2])]
        for block in range(3):
            for source, names in ((mains[block], order[block][0]), (halves[block], order[block][1])):
                for s, n in enumerate(names):
                    inner[n] = jnp.where(here, roll(source, at - s, 1), inner[n])
        last = doubled(faces[2][side])
        for s, n in enumerate(order[3][0]):
            value = jnp.where(row < 4, roll(last, at - s, 1), roll(last, at - 5 - s, 1))
            inner[n] = jnp.where(here, value, inner[n])
        upper_rows = jnp.where(low_y, roll(last, at - 80, 1), roll(last, at - 41, 1))
        lower_rows = jnp.where(low_y, roll(last, at - 82, 1), roll(last, at - 43, 1))
        n = order[3][1][0]
        inner[n] = jnp.where(here, jnp.where(row < 4, upper_rows, lower_rows), inner[n])

        above, below = [jnp.broadcast_to(edges[1][end][side], (8, LANES)) for end in range(2)]
        edge = jnp.where(row == 0, above, below)
        for s in range(10):
            value = roll(edge, at - s, 1)
            for n in (order[0][0][s], order[1][0][s]):
                outer[n] = jnp.where(here & inside(y), value, outer[n])
        edge = joined(edge)
        for s in range(5):
            n = COARSE + s
            outer[n] = jnp.where(here & inside(y), roll(edge, at - s, 1), outer[n])
    return [jnp.concatenate([i, o], axis=0) for i, o in zip(inner, outer)]


def advance(
    pos_ref, got0, got1, got2, inner_ref, spread_ref, back_ref, back_coarse_ref, coarse_out, fine_out, scr, scr_x
):
    lane, x, y, z = positions(16)
    fastest = running_maximum([got2[t, FACE - 1 : FACE, :] for t in range(8)])
    half16 = 0.5 * (courant / jnp.broadcast_to(fastest, (16, LANES)))
    half = half16[:8]
    faces, edges = arrived(pos_ref, got0, got1, got2)
    state = surround(faces, edges, inner_ref, spread_ref, scr_x)
    covered = state[COVER] > 0.5
    fine0 = [[state[f * 8 + q] for f in range(5)] for q in range(8)]
    coarse0 = state[COARSE:DEEP]

    net = coarse_net(coarse0, state[DEEP:COVER], (x, y, z))
    coarse1 = [u - 0.5 * half16 * n for u, n in zip(coarse0, net)]
    net = fine_net(fine0, False)
    fine1 = [
        [jnp.where(covered, fine0[q][f] - half16 * net[q][f], coarse1[f]) for f in range(5)] for q in range(8)
    ]
    net = coarse_net(coarse1, None, None)
    coarse2 = [0.5 * c0[:8] + 0.5 * (c1[:8] - 0.5 * half * n[:8]) for c0, c1, n in zip(coarse0, coarse1, net)]
    net = fine_net(fine1, True)
    mine = inside(y[:8]) & inside(z[:8])
    refined = mine & covered[:8]
    fine2 = [
        [
            jnp.where(refined, 0.5 * fine0[q][f][:8] + 0.5 * (fine1[q][f][:8] - half * net[q][f]), 0.0)
            for f in range(5)
        ]
        for q in range(8)
    ]
    coarse = []
    for f in range(5):
        total = functools.reduce(jnp.add, [fine2[q][f] for q in range(8)])
        coarse.append(jnp.where(mine, jnp.where(refined, 0.125 * total, coarse2[f]), 0.0))

    left_half = lane[:8] < 64
    rows = [jnp.concatenate([fine2[a * 4 + q][f] for q in range(4)], axis=1) for a in range(2) for f in range(5)]
    back = place(jnp.concatenate(rows, axis=0), back_ref[...])
    for f in range(5):
        for h in range(2):
            even = back[f * 8 : f * 8 + 8, h * 128 : h * 128 + 128]
            odd = back[40 + f * 8 : 48 + f * 8, h * 128 : h * 128 + 128]
            scr[f, h * 16 : h * 16 + 8, :] = jnp.where(left_half, even, roll(odd, 64, 1))
            scr[f, h * 16 + 8 : h * 16 + 16, :] = jnp.where(left_half, roll(even, 64, 1), odd)
        for q in range(4):
            for ox in range(2):
                tile = scr[f, pl.ds(ox * 4 + q, 4, stride=8), :]
                fine_out[f, ox * 4 : ox * 4 + 4, q * 128 : q * 128 + 128] = tile
    back = place(jnp.concatenate(coarse, axis=0), back_coarse_ref[...])
    for f in range(5):
        value = back[f * 8 : f * 8 + 8]
        value = jnp.where(left_half, value, roll(roll(value, 64, 1), -1, 0))
        for q in range(4):
            coarse_out[f, :, q * 128 : q * 128 + 128] = value[2 * q : 2 * q + 1]


def shape(*dims):
    return jax.ShapeDtypeStruct(dims, jnp.float32)


def call(kernel, kinds, outs, scratch, args):
    spaces = {"s": pltpu.SMEM, "v": pltpu.VMEM}
    return pl.pallas_call(
        kernel,
        out_shape=outs,
        in_specs=[pl.BlockSpec(memory_space=spaces[k]) for k in kinds],
        out_specs=[pl.BlockSpec(memory_space=pltpu.VMEM)] * len(outs),
        scratch_shapes=[pltpu.VMEM(dims, jnp.float32) for dims in scratch],
        compiler_params=pltpu.CompilerParams(vmem_limit_bytes=32 * 1024 * 1024),
    )(*args)


def swap(block, level):
    count = lax.axis_size("boxes")
    low = 3 * level
    first = [device for device in range(count) if not (device >> low) & 7]
    groups = [[device | (slot ^ LEAD[level]) << low for slot in range(8)] for device in first]
    return lax.all_to_all(block, "boxes", 0, 0, axis_index_groups=groups)


def local(coarse_state, fine_state, refined):
    fine_place, coarse_place = placement()
    as_matrix = lambda m: jnp.asarray(np.ascontiguousarray(m).astype(ml_dtypes.bfloat16))
    device = lax.axis_index("boxes")
    levels = [(device >> (3 * level)) & 7 for level in range(3)]
    bits = [[(level >> d) & 1 for d in range(3)] for level in levels]
    levels = [level ^ lead for level, lead in zip(levels, LEAD)]
    twice = [(bits[0][d] == bits[1][d]).astype(jnp.int32) for d in range(3)]
    pos = jnp.stack(levels + bits[0] + twice).astype(jnp.int32)
    spread, dense = as_matrix(coarse_place), as_matrix(coarse_place.T)

    inner, send = call(
        prepare,
        "ssvvvvv",
        [shape(COUNT, 8, LANES), shape(8, 2, ROWS, LANES)],
        [(5, 32, LANES), (5, 8, LANES), (128, LANES)],
        (
            pos,
            refined[0],
            jnp.swapaxes(coarse_state, 0, 1),
            jnp.swapaxes(fine_state[0], 0, 1),
            as_matrix(fine_place),
            spread,
            dense,
        ),
    )
    got0 = swap(send, 0)
    got1 = swap(call(carry_once, "sv", [shape(8, ROWS, LANES)], [], (pos, got0))[0], 1)
    got2 = swap(call(carry_twice, "sv", [shape(8, ROWS, LANES)], [], (pos, got1))[0], 2)
    coarse_out, fine_out = call(
        advance,
        "svvvvvvv",
        [shape(5, 1, 512), shape(5, 8, 512)],
        [(5, 32, LANES), (128, LANES)],
        (pos, got0, got1, got2, inner, spread, as_matrix(fine_place.T), dense),
    )
    return jnp.swapaxes(coarse_out, 0, 1), jnp.swapaxes(fine_out, 0, 1)[None]


def solution(mesh):
    in_specs = (P("boxes", None, None), P("boxes", None, None, None), P("boxes", None))
    out_specs = (P("boxes", None, None), P("boxes", None, None, None))
    return jax.shard_map(local, mesh=mesh, in_specs=in_specs, out_specs=out_specs, check_vma=False)
```

```python
import functools

import jax
import jax.numpy as jnp
import ml_dtypes
import numpy as np
from jax import lax
from jax.experimental import pallas as pl
from jax.experimental.pallas import tpu as pltpu
from jax.sharding import PartitionSpec as P

PITCH = 10
LANES = 128
FINE = 40
COARSE = FINE
DEEP = COARSE + 5
COVER = DEEP + 5
COUNT = COVER + 1
FACE = 28
ROWS = 32
MAX_LANE = 120
PAIRED = 26
LEAD = (1, 4, 4)
SIDES = ((0, 8), (1, -1))
PAIRS = ((0, 1), (0, 2), (1, 2))
gamma_gas = 1.4
courant = 0.4


def back_matrix():
    back = np.zeros((512, 256), np.float32)
    for y in range(16):
        for z in range(16):
            row = (y // 8 * 2 + z // 8) * 64 + y % 8 * 8 + z % 8
            back[(y % 2 * 2 + z % 2) * 128 + y // 2 * PITCH + z // 2, row] = 1
    return back


def place(values, matrix):
    high = values.astype(jnp.bfloat16)
    rest = values - high.astype(jnp.float32)
    middle = rest.astype(jnp.bfloat16)
    low = (rest - middle.astype(jnp.float32)).astype(jnp.bfloat16)
    rows = values.shape[0]
    parts = jnp.concatenate([high, middle, low], axis=0)
    out = jnp.dot(parts, matrix, preferred_element_type=jnp.float32)
    return out[:rows] + out[rows : 2 * rows] + out[2 * rows :]


def roll(x, shift, axis):
    shift = shift % x.shape[axis]
    return pltpu.roll(x, shift, axis) if shift else x


def positions(rows):
    row = lax.broadcasted_iota(jnp.int32, (rows, LANES), 0)
    lane = lax.broadcasted_iota(jnp.int32, (rows, LANES), 1)
    x = jnp.where(row > 8, row - 16, row)
    along = (lane + PITCH + 1) & (LANES - 1)
    y1 = (along * 205) >> 11
    return lane, x, y1 - 1, along - y1 * PITCH - 1


def inside(pos):
    return (pos >= 0) & (pos < 8)


def primitive(u):
    inverse = 1.0 / u[0]
    v = [u[1 + d] * inverse for d in range(3)]
    pressure = 0.4 * (u[4] - 0.5 * (u[1] * v[0] + u[2] * v[1] + u[3] * v[2]))
    sound = jnp.sqrt(gamma_gas * pressure * inverse)
    return v, pressure, sound


def cell_flux(u, prim, d):
    v, pressure, sound = prim
    flux = [u[1 + d]] + [u[1 + e] * v[d] for e in range(3)] + [(u[4] + pressure) * v[d]]
    flux[1 + d] = flux[1 + d] + pressure
    return list(u) + flux + [jnp.abs(v[d]) + sound]


def face(left, right):
    speed = jnp.maximum(left[10], right[10])
    return [(left[5 + f] + right[5 + f]) - speed * (right[f] - left[f]) for f in range(5)]


def ahead(x, d):
    return roll(x, -1, 0) if d == 0 else roll(x, -PITCH if d == 1 else -1, 1)


def behind(x, d):
    return roll(x, 1, 0) if d == 0 else roll(x, PITCH if d == 1 else 1, 1)


def fine_net(u, inner):
    prims = [primitive(u[q]) for q in range(8)]
    total = [None] * 8
    for d in range(3):
        bit = 4 >> d
        cut = (lambda x: x[:8]) if inner and d > 0 else (lambda x: x)
        keep = (lambda x: x[:8]) if inner else (lambda x: x)
        for low in range(8):
            if low & bit:
                continue
            high = low | bit
            cells = []
            for q in (low, high):
                v, pressure, sound = prims[q]
                cells.append(cell_flux([cut(x) for x in u[q]], ([cut(x) for x in v], cut(pressure), cut(sound)), d))
            middle = face(cells[0], cells[1])
            after = face(cells[1], [ahead(x, d) for x in cells[0]])
            net_low = [keep(middle[f] - behind(after[f], d)) for f in range(5)]
            net_high = [keep(after[f] - middle[f]) for f in range(5)]
            for q, net in ((low, net_low), (high, net_high)):
                total[q] = net if total[q] is None else [s + n for s, n in zip(total[q], net)]
    return total


def coarse_net(u, deep, pos):
    prim = primitive(u)
    prim_deep = None if deep is None else primitive(deep)
    total = None
    for d in range(3):
        cell = cell_flux(u, prim, d)
        right = [ahead(x, d) for x in cell]
        if deep is not None:
            outer = cell_flux(deep, prim_deep, d)
            last, first = pos[d] == 8, pos[d] == -1
            right = [jnp.where(last, o, r) for o, r in zip(outer, right)]
        after = face(cell, right)
        before = [behind(x, d) for x in after]
        if deep is not None:
            before = [jnp.where(first, o, b) for o, b in zip(face(outer, cell), before)]
        net = [a - b for a, b in zip(after, before)]
        total = net if total is None else [s + n for s, n in zip(total, net)]
    return total


def is_deep(n):
    return DEEP <= n < COVER


def fine_index(f, a, b, c):
    return f * 8 + a * 4 + b * 2 + c


def y_order(near):
    rest = [fine_index(f, a, 1 - near, c) for f in range(5) for a in range(2) for c in range(2)]
    first = [fine_index(f, 1, near, c) for c in range(2) for f in range(5)]
    second = [fine_index(f, 0, near, c) for c in range(2) for f in range(5)]
    return (
        first + [COARSE + f for f in range(5)] + rest[:1],
        second + [DEEP + f for f in range(5)] + [COVER],
        rest[1:17],
        rest[17:],
    )


def z_order(near):
    rest = [fine_index(f, a, b, 1 - near) for f in range(5) for a in range(2) for b in range(2)]
    first = [fine_index(f, 1, b, near) for b in range(2) for f in range(5)]
    second = [fine_index(f, 0, b, near) for b in range(2) for f in range(5)]
    return (
        (first, [COARSE + f for f in range(5)]),
        (second, [DEEP + f for f in range(5)]),
        (rest[:10], [COVER] + rest[10:14]),
        (rest[14:19], rest[19:]),
    )


def block_transpose(value):
    row = lax.broadcasted_iota(jnp.int32, (8, LANES), 0)
    group = lax.broadcasted_iota(jnp.int32, (8, LANES), 1) >> 4
    out = value
    for step in range(1, 8):
        moved = roll(roll(value, -16 * step, 1), step, 0)
        out = jnp.where(((row - group) & 7) == step, moved, out)
    return out


def swapped(flag, first, second):
    return jnp.where(flag, second, first), jnp.where(flag, first, second)


def whereabouts():
    device = lax.axis_index("boxes")
    own = [((device >> (3 * level)) & 7) ^ lead for level, lead in enumerate(LEAD)]
    first = [(device >> d) & 1 for d in range(3)]
    second = [(device >> (3 + d)) & 1 for d in range(3)]
    return own, first, [a == b for a, b in zip(first, second)]


def fine_matrix():
    row = lax.broadcasted_iota(jnp.int32, (256, LANES), 0)
    lane = lax.broadcasted_iota(jnp.int32, (256, LANES), 1)
    y = ((row >> 7) << 2) + ((row >> 4) & 3)
    z = (((row >> 6) & 1) << 2) + ((row >> 1) & 3)
    hit = lane == y * PITCH + z
    parity = ((row >> 2) & 2) + (row & 1)
    return [jnp.where(hit & (parity == q), 1.0, 0.0).astype(jnp.bfloat16) for q in range(4)]


def coarse_matrices():
    row = lax.broadcasted_iota(jnp.int32, (LANES, LANES), 0)
    lane = lax.broadcasted_iota(jnp.int32, (LANES, LANES), 1)
    spread = (row < 64) & (lane == (row >> 3) * PITCH + (row & 7))
    dense = (lane < 64) & (row == (lane >> 3) * PITCH + (lane & 7))
    return [jnp.where(hit, 1.0, 0.0).astype(jnp.bfloat16) for hit in (spread, dense)]


def matrices(place_ref, spread_ref, dense_ref):
    for q, part in enumerate(fine_matrix()):
        place_ref[:, q * LANES : (q + 1) * LANES] = part
    spread_ref[...], dense_ref[...] = coarse_matrices()


def prepare(
    refined_ref, coarse_ref, fine_ref, place_ref, spread_ref, dense_ref, inner_ref, send_ref, scr, scr_c, scr_x
):
    places, far, _ = whereabouts()
    own = places[0]
    lane, x, y, z = positions(8)
    row = lax.broadcasted_iota(jnp.int32, (8, LANES), 0)
    left_half = lane < 64
    for f in range(5):
        for q in range(4):
            tile = fine_ref[f, :, q * 128 : q * 128 + 128]
            for ox in range(2):
                scr[f, pl.ds(ox * 4 + q, 4, stride=8), :] = tile[ox * 4 : ox * 4 + 4]
            part = coarse_ref[f, :, q * 128 : q * 128 + 128]
            scr_c[f, 2 * q : 2 * q + 1, :] = part
            scr_c[f, 2 * q + 1 : 2 * q + 2, :] = part
    sides = [[], []]
    rows = []
    for f in range(5):
        tile = [scr[f, c * 8 : c * 8 + 8, :] for c in range(4)]
        sides[0].append(
            jnp.concatenate([jnp.where(left_half, tile[2 * h], roll(tile[2 * h + 1], 64, 1)) for h in range(2)], axis=1)
        )
        sides[1].append(
            jnp.concatenate([jnp.where(left_half, roll(tile[2 * h], 64, 1), tile[2 * h + 1]) for h in range(2)], axis=1)
        )
        value = scr_c[f]
        rows.append(jnp.where((row & 1) == 1, roll(value, 64, 1), value))
    fine = place(jnp.concatenate(sides[0] + sides[1], axis=0), place_ref[...])
    coarse = place(jnp.concatenate(rows, axis=0), spread_ref[...])
    coarse = [coarse[f * 8 : f * 8 + 8] for f in range(5)]

    covered = jnp.zeros((8, LANES), jnp.float32)
    for o in range(8):
        here = ((x >= 4) == (o >= 4)) & ((y >= 4) == (o % 4 >= 2)) & ((z >= 4) == (o % 2 == 1))
        flag = jnp.broadcast_to(refined_ref[:, o : o + 1], (8, LANES))
        covered = jnp.where(here & (flag > 0), 1.0, covered)
    state = []
    for f in range(5):
        for q in range(8):
            first = (q // 4 * 5 + f) * 8
            part = fine[first : first + 8, q % 4 * 128 : q % 4 * 128 + 128]
            state.append(jnp.where(covered > 0.5, part, coarse[f]))
    state += coarse
    fastest = None
    for u in [[state[f * 8 + q] for f in range(5)] for q in range(8)] + [coarse]:
        v, pressure, sound = primitive(u)
        speed = jnp.abs(v[0]) + jnp.abs(v[1]) + jnp.abs(v[2]) + 3.0 * sound
        fastest = speed if fastest is None else jnp.maximum(fastest, speed)
    fastest = jnp.where(inside(y) & inside(z), fastest, 0.0)
    fastest = jnp.broadcast_to(jnp.max(fastest), (8, LANES))

    zero = jnp.zeros((8, LANES), jnp.float32)
    stored = state + [zero] * 5 + [covered]
    for n in range(COUNT):
        inner_ref[n] = stored[n]

    for t in range(8):
        send_ref[t, 0, FACE - 1 : FACE, :] = fastest[:1]

    def taken(n, at, deep_at):
        return (stored[n - 5], deep_at) if is_deep(n) else (stored[n], at)

    for side, at, deep_at in ((0, 7, 6), (1, 0, 1)):
        for n in range(COUNT):
            value, where = taken(n, at, deep_at)
            target = side * 64 + (n if n < PAIRED else n - PAIRED + 32)
            scr_x[target : target + 1, :] = value[where : where + 1, :]
    dense = place(scr_x[...], dense_ref[...])
    left4 = lax.broadcasted_iota(jnp.int32, (32, LANES), 1) < 64
    row32 = lax.broadcasted_iota(jnp.int32, (32, LANES), 0)
    for side in range(2):
        packed = jnp.where(left4, dense[side * 64 : side * 64 + 32], roll(dense[side * 64 + 32 : side * 64 + 64], 64, 1))
        packed = jnp.where(row32 >= PAIRED, jnp.concatenate([fastest] * 4, axis=0), packed)
        send_ref[own ^ 1, far[0] if side == 0 else 1 - far[0]] = packed

    slots = lane - ((lane * 205) >> 11) * PITCH
    corners_xy, corners_xz, corners = [], [], zero
    for side, at, deep_at in ((0, 7, 6), (1, 0, 1)):
        near = 1 - side
        order = y_order(near)
        blocks = []
        for names in order:
            packed = fastest
            for s, n in enumerate(names):
                value, where = taken(n, at, deep_at)
                packed = jnp.where((lane >> 3) == s, roll(value, s * 8 - where * PITCH, 1), packed)
            blocks.append(packed)
        width = len(order[3]) * 8
        second = (lane >= width) & (lane < 2 * width)
        blocks[3] = jnp.where(second, roll(roll(blocks[3], width, 1), 4, 0), blocks[3])
        part = far[1] if side == 0 else 1 - far[1]
        for block in range(3):
            send_ref[own ^ 2, part, block * 8 : block * 8 + 8, :] = blocks[block]
        send_ref[own ^ 2, part, 24:FACE, :] = blocks[3][:4]
        corners_xy.append((blocks[0][7:8], jnp.where(lane < 80, blocks[1], blocks[0])[0:1]))

        blocks = []
        for block, (names, halves) in enumerate(z_order(near)):
            packed = fastest
            for s, n in enumerate(names):
                value, where = taken(n, at, deep_at)
                packed = jnp.where((slots == s) & (lane < 80), roll(value, s - where, 1), packed)
            if block < 3:
                extra = fastest
                for s, n in enumerate(halves):
                    value, where = taken(n, at, deep_at)
                    extra = jnp.where(slots == s, roll(value, s - where, 1), extra)
                extra = jnp.where(slots < 5, roll(extra, 80, 1), roll(extra, 45, 1))
                packed = jnp.where((lane >= 80) & (lane < MAX_LANE), extra, packed)
            else:
                second = (slots >= 5) & (lane < 80)
                packed = jnp.where(second, roll(roll(packed, 5, 1), 4, 0), packed)
                value = stored[halves[0]]
                lower = roll(value, 4, 0)
                pieces = [roll(value, 80 - at, 1), roll(value, 41 - at, 1), roll(lower, 82 - at, 1), roll(lower, 43 - at, 1)]
                for s, piece in enumerate(pieces):
                    packed = jnp.where((slots == s) & (lane >= 80) & (lane < MAX_LANE), piece, packed)
            blocks.append(packed)
        part = far[2] if side == 0 else 1 - far[2]
        for block in range(3):
            send_ref[own ^ 4, part, block * 8 : block * 8 + 8, :] = blocks[block]
        send_ref[own ^ 4, part, 24:FACE, :] = blocks[3][:4]
        corners_xz.append((blocks[0][7:8], jnp.where(lane < 80, blocks[1], blocks[0])[0:1]))
        for end, first, first_coarse in ((0, 75, 115), (1, 0, 80)):
            to = (side * 2 + end) * 16
            for start, source, i in ((first, blocks[0], 0), (first, blocks[1], 5), (first_coarse, blocks[0], 10)):
                here = (lane >= to + i) & (lane < to + i + 5)
                corners = jnp.where(here, roll(source, to + i - start, 1), corners)
    corners = block_transpose(corners)

    edges = [
        [[corners_xy[e][d] for e in range(2)] for d in range(2)],
        [[corners_xz[e][d] for e in range(2)] for d in range(2)],
        [[corners[e * 2 + d : e * 2 + d + 1] for e in range(2)] for d in range(2)],
    ]
    for (d, e), edge in zip(PAIRS, edges):
        upper, lower = [swapped(far[e] == 1, *half) for half in edge]
        near_near, far_near = swapped(far[d] == 1, upper[0], lower[0])
        near_far, far_far = swapped(far[d] == 1, upper[1], lower[1])
        for r, value in enumerate((near_near, near_far, far_near, far_far)):
            send_ref[own ^ (1 << d) ^ (1 << e), 0, r : r + 1, :] = value


def others(d):
    return [e for e in range(3) if e != d]


def pair(d, e):
    return (1 << d) ^ (1 << e)


def running_maximum(rows):
    fastest = functools.reduce(jnp.maximum, rows)
    lane = lax.broadcasted_iota(jnp.int32, fastest.shape, 1)
    fastest = jnp.where(lane >= MAX_LANE, fastest, 0.0)
    return jnp.broadcast_to(jnp.max(fastest), (1, LANES))


def pass_on(send_ref, own, fastest, faces, edges, corners):
    lane = lax.broadcasted_iota(jnp.int32, (1, LANES), 1)
    for t in range(8):
        send_ref[t, FACE - 1 : FACE, :] = fastest
    for d in range(3):
        slot = own ^ (1 << d)
        send_ref[slot, : FACE - 1, :] = faces[d](0, FACE - 1)
        last = faces[d](FACE - 1, FACE)
        send_ref[slot, FACE - 1 : FACE, :] = jnp.where(lane >= MAX_LANE, fastest, last)
        for r, value in enumerate(edges[d]):
            send_ref[slot, FACE + r : FACE + r + 1, :] = value
    for (d, e), value in zip(PAIRS, corners):
        send_ref[own ^ pair(d, e), 0:1, :] = value


def carry_once(got_ref, send_ref):
    own, to, _ = whereabouts()[0]
    fastest = running_maximum([got_ref[t, 0, FACE - 1 : FACE, :] for t in range(8)])
    faces = [lambda i, j, d=d: got_ref[own ^ (1 << d), 1, i:j, :] for d in range(3)]

    def edge(d, e, r):
        return got_ref[own ^ pair(d, e), 0, r : r + 1, :]

    edges = [[edge(d, e, 1 if e < d else 2) for e in others(d)] for d in range(3)]
    pass_on(send_ref, to, fastest, faces, edges, [edge(d, e, 3) for d, e in PAIRS])


def carry_twice(got_ref, send_ref):
    _, own, to = whereabouts()[0]
    fastest = running_maximum([got_ref[t, FACE - 1 : FACE, :] for t in range(8)])
    faces = [lambda i, j, d=d: got_ref[own ^ (1 << d), i:j, :] for d in range(3)]

    def far_far(d, e):
        return got_ref[own ^ pair(d, e), 0:1, :]

    edges = []
    for d in range(3):
        passed = [got_ref[own ^ (1 << d), FACE + r : FACE + r + 1, :] for r in range(2)]
        edges.append(passed + [far_far(d, e) for e in others(d)])
    pass_on(send_ref, to, fastest, faces, edges, [far_far(d, e) for d, e in PAIRS])


def arrived(got0, got1, got2):
    own, first, twice = whereabouts()
    upper_far = [bit == 1 for bit in first]
    faces = []
    for d in range(3):
        near = got0[own[0] ^ (1 << d), 0]
        far = jnp.where(twice[d], got2[own[2] ^ (1 << d)], got1[own[1] ^ (1 << d)])
        faces.append(swapped(upper_far[d], near, far))

    def once(d, r):
        return got1[own[1] ^ (1 << d), FACE + r : FACE + r + 1, :]

    def again(d, r):
        return got2[own[2] ^ (1 << d), FACE + r : FACE + r + 1, :]

    edges = []
    for d, e in PAIRS:
        of_e, of_d = others(d).index(e), others(e).index(d)
        near_near = got0[own[0] ^ pair(d, e), 0, 0:1, :]
        near_far = jnp.where(twice[e], again(e, of_d), once(e, of_d))
        far_near = jnp.where(twice[d], again(d, of_e), once(d, of_e))
        both = jnp.where(twice[e], got2[own[2] ^ pair(d, e), 0:1, :], again(d, 2 + of_e))
        neither = jnp.where(twice[e], again(e, 2 + of_d), got1[own[1] ^ pair(d, e), 0:1, :])
        far_far = jnp.where(twice[d], both, neither)
        near, far = [swapped(upper_far[e], *half) for half in ((near_near, near_far), (far_near, far_far))]
        above, below = zip(*[swapped(upper_far[d], n, f) for n, f in zip(near, far)])
        edges.append((above, below))
    return faces, edges


def surround(faces, edges, inner_ref, spread, scr_x):
    lane, x, y, z = positions(8)
    row = lax.broadcasted_iota(jnp.int32, (8, LANES), 0)
    left4 = lax.broadcasted_iota(jnp.int32, (32, LANES), 1) < 64
    inner = [inner_ref[n] for n in range(COUNT)]
    rows = []
    for side in range(2):
        value = faces[0][side]
        rows += [jnp.where(left4, value, 0.0), jnp.where(left4, roll(value, 64, 1), 0.0)]
    scr_x[...] = place(jnp.concatenate(rows, axis=0), spread)
    outer = []
    for n in range(COUNT):
        at = n if n < PAIRED else n - PAIRED + 32
        above = jnp.broadcast_to(scr_x[at : at + 1, :], (8, LANES))
        below = jnp.broadcast_to(scr_x[at + 64 : at + 65, :], (8, LANES))
        outer.append(jnp.where(row == 0, above, below))

    def doubled(value):
        return jnp.concatenate([value[24:28], value[24:28]], axis=0)

    for side, (near, at) in enumerate(SIDES):
        blocks = [faces[1][side][block * 8 : block * 8 + 8] for block in range(3)]
        order = y_order(near)
        first = at * PITCH % LANES
        here = (lane >= first) & (lane < first + 8)
        for block, names in zip(blocks, order):
            for s, n in enumerate(names):
                inner[n] = jnp.where(here, roll(block, first - s * 8, 1), inner[n])
        last = doubled(faces[1][side])
        for s, n in enumerate(order[3]):
            value = jnp.where(row < 4, roll(last, first - s * 8, 1), roll(last, first - (s + len(order[3])) * 8, 1))
            inner[n] = jnp.where(here, value, inner[n])
        above, below = [jnp.broadcast_to(edges[0][end][side], (8, LANES)) for end in range(2)]
        edge = jnp.where(row == 0, above, below)
        for s in range(15):
            value = roll(edge, first - s * 8, 1)
            for n in (order[0][s], order[1][s]) if s < 10 else (order[0][s],):
                outer[n] = jnp.where(here, value, outer[n])

    columns = jnp.concatenate([edges[2][end][side] for side in range(2) for end in range(2)] * 2, axis=0)
    columns = block_transpose(columns)
    for side, (near, at) in enumerate(SIDES):
        blocks = [faces[2][side][block * 8 : block * 8 + 8] for block in range(3)]
        order = z_order(near)
        here = (z == at) & (y < 9)
        low_y = y < 4
        above, below = side * 32, side * 32 + 16

        def joined(block):
            return jnp.where(lane < 40, roll(block, -80, 1), roll(block, -45, 1))

        def ended(block, i, below_lane):
            block = jnp.where(lane < 80, block, roll(columns, 80 - above - i, 1))
            return jnp.where(lane >= below_lane, roll(columns, below_lane - below - i, 1), block)

        mains = [ended(blocks[0], 0, 123), ended(blocks[1], 5, 123), blocks[2]]
        halves = [ended(joined(blocks[0]), 10, 118), joined(blocks[1]), joined(blocks[2])]
        for block in range(3):
            for source, names in ((mains[block], order[block][0]), (halves[block], order[block][1])):
                for s, n in enumerate(names):
                    inner[n] = jnp.where(here, roll(source, at - s, 1), inner[n])
        last = doubled(faces[2][side])
        for s, n in enumerate(order[3][0]):
            value = jnp.where(row < 4, roll(last, at - s, 1), roll(last, at - 5 - s, 1))
            inner[n] = jnp.where(here, value, inner[n])
        upper_rows = jnp.where(low_y, roll(last, at - 80, 1), roll(last, at - 41, 1))
        lower_rows = jnp.where(low_y, roll(last, at - 82, 1), roll(last, at - 43, 1))
        n = order[3][1][0]
        inner[n] = jnp.where(here, jnp.where(row < 4, upper_rows, lower_rows), inner[n])

        above, below = [jnp.broadcast_to(edges[1][end][side], (8, LANES)) for end in range(2)]
        edge = jnp.where(row == 0, above, below)
        for s in range(10):
            value = roll(edge, at - s, 1)
            for n in (order[0][0][s], order[1][0][s]):
                outer[n] = jnp.where(here & inside(y), value, outer[n])
        edge = joined(edge)
        for s in range(5):
            n = COARSE + s
            outer[n] = jnp.where(here & inside(y), roll(edge, at - s, 1), outer[n])
    return [jnp.concatenate([i, o], axis=0) for i, o in zip(inner, outer)]


def advance(got0, got1, got2, inner_ref, back_ref, spread_ref, dense_ref, coarse_out, fine_out, scr, scr_x):
    lane, x, y, z = positions(16)
    fastest = running_maximum([got2[t, FACE - 1 : FACE, :] for t in range(8)])
    half16 = 0.5 * (courant / jnp.broadcast_to(fastest, (16, LANES)))
    half = half16[:8]
    faces, edges = arrived(got0, got1, got2)
    state = surround(faces, edges, inner_ref, spread_ref[...], scr_x)
    covered = state[COVER] > 0.5
    fine0 = [[state[f * 8 + q] for f in range(5)] for q in range(8)]
    coarse0 = state[COARSE:DEEP]

    net = coarse_net(coarse0, state[DEEP:COVER], (x, y, z))
    coarse1 = [u - 0.5 * half16 * n for u, n in zip(coarse0, net)]
    net = fine_net(fine0, False)
    fine1 = [
        [jnp.where(covered, fine0[q][f] - half16 * net[q][f], coarse1[f]) for f in range(5)] for q in range(8)
    ]
    net = coarse_net(coarse1, None, None)
    coarse2 = [0.5 * c0[:8] + 0.5 * (c1[:8] - 0.5 * half * n[:8]) for c0, c1, n in zip(coarse0, coarse1, net)]
    net = fine_net(fine1, True)
    mine = inside(y[:8]) & inside(z[:8])
    refined = mine & covered[:8]
    fine2 = [
        [
            jnp.where(refined, 0.5 * fine0[q][f][:8] + 0.5 * (fine1[q][f][:8] - half * net[q][f]), 0.0)
            for f in range(5)
        ]
        for q in range(8)
    ]
    coarse = []
    for f in range(5):
        total = functools.reduce(jnp.add, [fine2[q][f] for q in range(8)])
        coarse.append(jnp.where(mine, jnp.where(refined, 0.125 * total, coarse2[f]), 0.0))

    left_half = lane[:8] < 64
    rows = [jnp.concatenate([fine2[a * 4 + q][f] for q in range(4)], axis=1) for a in range(2) for f in range(5)]
    back = place(jnp.concatenate(rows, axis=0), back_ref[...])
    for f in range(5):
        for h in range(2):
            even = back[f * 8 : f * 8 + 8, h * 128 : h * 128 + 128]
            odd = back[40 + f * 8 : 48 + f * 8, h * 128 : h * 128 + 128]
            scr[f, h * 16 : h * 16 + 8, :] = jnp.where(left_half, even, roll(odd, 64, 1))
            scr[f, h * 16 + 8 : h * 16 + 16, :] = jnp.where(left_half, roll(even, 64, 1), odd)
        for q in range(4):
            for ox in range(2):
                tile = scr[f, pl.ds(ox * 4 + q, 4, stride=8), :]
                fine_out[f, ox * 4 : ox * 4 + 4, q * 128 : q * 128 + 128] = tile
    back = place(jnp.concatenate(coarse, axis=0), dense_ref[...])
    for f in range(5):
        value = back[f * 8 : f * 8 + 8]
        value = jnp.where(left_half, value, roll(roll(value, 64, 1), -1, 0))
        for q in range(4):
            coarse_out[f, :, q * 128 : q * 128 + 128] = value[2 * q : 2 * q + 1]


def shape(*dims):
    return jax.ShapeDtypeStruct(dims, jnp.float32)


def call(kernel, outs, scratch, args, cost=None):
    return pl.pallas_call(
        kernel,
        out_shape=outs,
        in_specs=[pl.BlockSpec(memory_space=pltpu.VMEM)] * len(args),
        out_specs=[pl.BlockSpec(memory_space=pltpu.VMEM)] * len(outs),
        scratch_shapes=scratch,
        cost_estimate=cost,
        compiler_params=pltpu.CompilerParams(vmem_limit_bytes=32 * 1024 * 1024),
    )(*args)


def swap(block, level):
    count = lax.axis_size("boxes")
    low = 3 * level
    first = [device for device in range(count) if not (device >> low) & 7]
    groups = [[device | (slot ^ LEAD[level]) << low for slot in range(8)] for device in first]
    return lax.all_to_all(block, "boxes", 0, 0, axis_index_groups=groups)


def local(coarse_state, fine_state, refined):
    back = jnp.asarray(back_matrix().astype(ml_dtypes.bfloat16))
    fields = lambda *dims: pltpu.VMEM(dims, jnp.float32)
    matrix = lambda *dims: jax.ShapeDtypeStruct(dims, jnp.bfloat16)
    made = call(matrices, [matrix(256, 4 * LANES), matrix(LANES, LANES), matrix(LANES, LANES)], [], (), pl.CostEstimate(flops=50000000, bytes_accessed=327680, transcendentals=0))
    inner, send = call(
        prepare,
        [shape(COUNT, 8, LANES), shape(8, 2, ROWS, LANES)],
        [fields(5, 32, LANES), fields(5, 8, LANES), fields(128, LANES)],
        (refined, jnp.swapaxes(coarse_state, 0, 1), jnp.swapaxes(fine_state[0], 0, 1), *made),
    )
    got0 = swap(send, 0)
    got1 = swap(call(carry_once, [shape(8, ROWS, LANES)], [], (got0,))[0], 1)
    got2 = swap(call(carry_twice, [shape(8, ROWS, LANES)], [], (got1,))[0], 2)
    coarse_out, fine_out = call(
        advance,
        [shape(5, 1, 512), shape(5, 8, 512)],
        [fields(5, 32, LANES), fields(128, LANES)],
        (got0, got1, got2, inner, back, *made[1:]),
    )
    return jnp.swapaxes(coarse_out, 0, 1), jnp.swapaxes(fine_out, 0, 1)[None]


def solution(mesh):
    in_specs = (P("boxes", None, None), P("boxes", None, None, None), P("boxes", None))
    out_specs = (P("boxes", None, None), P("boxes", None, None, None))
    return jax.shard_map(local, mesh=mesh, in_specs=in_specs, out_specs=out_specs, check_vma=False)
```

```python
import functools

import jax
import jax.numpy as jnp
import ml_dtypes
import numpy as np
from jax import lax
from jax.experimental import pallas as pl
from jax.experimental.pallas import tpu as pltpu
from jax.sharding import PartitionSpec as P

PITCH = 10
LANES = 128
FINE = 40
COARSE = FINE
DEEP = COARSE + 5
COVER = DEEP + 5
COUNT = COVER + 1
FACE = 28
ROWS = 32
MAX_LANE = 120
PAIRED = 26
LEAD = (5, 6, 4)
SIDES = ((0, 8), (1, -1))
PAIRS = ((0, 1), (0, 2), (1, 2))
gamma_gas = 1.4
courant = 0.4


def back_matrix():
    back = np.zeros((512, 256), np.float32)
    for y in range(16):
        for z in range(16):
            row = (y // 8 * 2 + z // 8) * 64 + y % 8 * 8 + z % 8
            back[(y % 2 * 2 + z % 2) * 128 + y // 2 * PITCH + z // 2, row] = 1
    return back


def place(values, matrix):
    high = values.astype(jnp.bfloat16)
    rest = values - high.astype(jnp.float32)
    middle = rest.astype(jnp.bfloat16)
    low = (rest - middle.astype(jnp.float32)).astype(jnp.bfloat16)
    rows = values.shape[0]
    parts = jnp.concatenate([high, middle, low], axis=0)
    out = jnp.dot(parts, matrix, preferred_element_type=jnp.float32)
    return out[:rows] + out[rows : 2 * rows] + out[2 * rows :]


def roll(x, shift, axis):
    shift = shift % x.shape[axis]
    return pltpu.roll(x, shift, axis) if shift else x


def positions(rows):
    row = lax.broadcasted_iota(jnp.int32, (rows, LANES), 0)
    lane = lax.broadcasted_iota(jnp.int32, (rows, LANES), 1)
    x = jnp.where(row > 8, row - 16, row)
    along = (lane + PITCH + 1) & (LANES - 1)
    y1 = (along * 205) >> 11
    return lane, x, y1 - 1, along - y1 * PITCH - 1


def inside(pos):
    return (pos >= 0) & (pos < 8)


def primitive(u):
    inverse = 1.0 / u[0]
    v = [u[1 + d] * inverse for d in range(3)]
    pressure = 0.4 * (u[4] - 0.5 * (u[1] * v[0] + u[2] * v[1] + u[3] * v[2]))
    sound = jnp.sqrt(gamma_gas * pressure * inverse)
    return v, pressure, sound


def cell_flux(u, prim, d):
    v, pressure, sound = prim
    flux = [u[1 + d]] + [u[1 + e] * v[d] for e in range(3)] + [(u[4] + pressure) * v[d]]
    flux[1 + d] = flux[1 + d] + pressure
    return list(u) + flux + [jnp.abs(v[d]) + sound]


def face(left, right):
    speed = jnp.maximum(left[10], right[10])
    return [(left[5 + f] + right[5 + f]) - speed * (right[f] - left[f]) for f in range(5)]


def ahead(x, d):
    return roll(x, -1, 0) if d == 0 else roll(x, -PITCH if d == 1 else -1, 1)


def behind(x, d):
    return roll(x, 1, 0) if d == 0 else roll(x, PITCH if d == 1 else 1, 1)


def fine_net(u, inner):
    prims = [primitive(u[q]) for q in range(8)]
    total = [None] * 8
    for d in range(3):
        bit = 4 >> d
        cut = (lambda x: x[:8]) if inner and d > 0 else (lambda x: x)
        keep = (lambda x: x[:8]) if inner else (lambda x: x)
        for low in range(8):
            if low & bit:
                continue
            high = low | bit
            cells = []
            for q in (low, high):
                v, pressure, sound = prims[q]
                cells.append(cell_flux([cut(x) for x in u[q]], ([cut(x) for x in v], cut(pressure), cut(sound)), d))
            middle = face(cells[0], cells[1])
            after = face(cells[1], [ahead(x, d) for x in cells[0]])
            net_low = [keep(middle[f] - behind(after[f], d)) for f in range(5)]
            net_high = [keep(after[f] - middle[f]) for f in range(5)]
            for q, net in ((low, net_low), (high, net_high)):
                total[q] = net if total[q] is None else [s + n for s, n in zip(total[q], net)]
    return total


def coarse_net(u, deep, pos):
    prim = primitive(u)
    prim_deep = None if deep is None else primitive(deep)
    total = None
    for d in range(3):
        cell = cell_flux(u, prim, d)
        right = [ahead(x, d) for x in cell]
        if deep is not None:
            outer = cell_flux(deep, prim_deep, d)
            last, first = pos[d] == 8, pos[d] == -1
            right = [jnp.where(last, o, r) for o, r in zip(outer, right)]
        after = face(cell, right)
        before = [behind(x, d) for x in after]
        if deep is not None:
            before = [jnp.where(first, o, b) for o, b in zip(face(outer, cell), before)]
        net = [a - b for a, b in zip(after, before)]
        total = net if total is None else [s + n for s, n in zip(total, net)]
    return total


def is_deep(n):
    return DEEP <= n < COVER


def fine_index(f, a, b, c):
    return f * 8 + a * 4 + b * 2 + c


def y_order(near):
    rest = [fine_index(f, a, 1 - near, c) for f in range(5) for a in range(2) for c in range(2)]
    first = [fine_index(f, 1, near, c) for c in range(2) for f in range(5)]
    second = [fine_index(f, 0, near, c) for c in range(2) for f in range(5)]
    return (
        first + [COARSE + f for f in range(5)] + rest[:1],
        second + [DEEP + f for f in range(5)] + [COVER],
        rest[1:17],
        rest[17:],
    )


def z_order(near):
    rest = [fine_index(f, a, b, 1 - near) for f in range(5) for a in range(2) for b in range(2)]
    first = [fine_index(f, 1, b, near) for b in range(2) for f in range(5)]
    second = [fine_index(f, 0, b, near) for b in range(2) for f in range(5)]
    return (
        (first, [COARSE + f for f in range(5)]),
        (second, [DEEP + f for f in range(5)]),
        (rest[:10], [COVER] + rest[10:14]),
        (rest[14:19], rest[19:]),
    )


def block_transpose(value):
    row = lax.broadcasted_iota(jnp.int32, (8, LANES), 0)
    group = lax.broadcasted_iota(jnp.int32, (8, LANES), 1) >> 4
    out = value
    for step in range(1, 8):
        moved = roll(roll(value, -16 * step, 1), step, 0)
        out = jnp.where(((row - group) & 7) == step, moved, out)
    return out


def swapped(flag, first, second):
    return jnp.where(flag, second, first), jnp.where(flag, first, second)


def whereabouts():
    device = lax.axis_index("boxes")
    own = [((device >> (3 * level)) & 7) ^ lead for level, lead in enumerate(LEAD)]
    first = [(device >> d) & 1 for d in range(3)]
    second = [(device >> (3 + d)) & 1 for d in range(3)]
    return own, first, [a == b for a, b in zip(first, second)]


def fine_matrix():
    row = lax.broadcasted_iota(jnp.int32, (256, LANES), 0)
    lane = lax.broadcasted_iota(jnp.int32, (256, LANES), 1)
    y = ((row >> 7) << 2) + ((row >> 4) & 3)
    z = (((row >> 6) & 1) << 2) + ((row >> 1) & 3)
    hit = lane == y * PITCH + z
    parity = ((row >> 2) & 2) + (row & 1)
    return [jnp.where(hit & (parity == q), 1.0, 0.0).astype(jnp.bfloat16) for q in range(4)]


def coarse_matrices():
    row = lax.broadcasted_iota(jnp.int32, (LANES, LANES), 0)
    lane = lax.broadcasted_iota(jnp.int32, (LANES, LANES), 1)
    spread = (row < 64) & (lane == (row >> 3) * PITCH + (row & 7))
    dense = (lane < 64) & (row == (lane >> 3) * PITCH + (lane & 7))
    return [jnp.where(hit, 1.0, 0.0).astype(jnp.bfloat16) for hit in (spread, dense)]


def matrices(place_ref, spread_ref, dense_ref):
    for q, part in enumerate(fine_matrix()):
        place_ref[:, q * LANES : (q + 1) * LANES] = part
    spread_ref[...], dense_ref[...] = coarse_matrices()


def prepare(
    refined_ref, coarse_ref, fine_ref, place_ref, spread_ref, dense_ref, inner_ref, send_ref, scr, scr_c, scr_x
):
    places, far, _ = whereabouts()
    own = places[0]
    lane, x, y, z = positions(8)
    row = lax.broadcasted_iota(jnp.int32, (8, LANES), 0)
    left_half = lane < 64
    for f in range(5):
        for q in range(4):
            tile = fine_ref[f, :, q * 128 : q * 128 + 128]
            for ox in range(2):
                scr[f, pl.ds(ox * 4 + q, 4, stride=8), :] = tile[ox * 4 : ox * 4 + 4]
            part = coarse_ref[f, :, q * 128 : q * 128 + 128]
            scr_c[f, 2 * q : 2 * q + 1, :] = part
            scr_c[f, 2 * q + 1 : 2 * q + 2, :] = part
    sides = [[], []]
    rows = []
    for f in range(5):
        tile = [scr[f, c * 8 : c * 8 + 8, :] for c in range(4)]
        sides[0].append(
            jnp.concatenate([jnp.where(left_half, tile[2 * h], roll(tile[2 * h + 1], 64, 1)) for h in range(2)], axis=1)
        )
        sides[1].append(
            jnp.concatenate([jnp.where(left_half, roll(tile[2 * h], 64, 1), tile[2 * h + 1]) for h in range(2)], axis=1)
        )
        value = scr_c[f]
        rows.append(jnp.where((row & 1) == 1, roll(value, 64, 1), value))
    fine = place(jnp.concatenate(sides[0] + sides[1], axis=0), place_ref[...])
    coarse = place(jnp.concatenate(rows, axis=0), spread_ref[...])
    coarse = [coarse[f * 8 : f * 8 + 8] for f in range(5)]

    covered = jnp.zeros((8, LANES), jnp.float32)
    for o in range(8):
        here = ((x >= 4) == (o >= 4)) & ((y >= 4) == (o % 4 >= 2)) & ((z >= 4) == (o % 2 == 1))
        flag = jnp.broadcast_to(refined_ref[:, o : o + 1], (8, LANES))
        covered = jnp.where(here & (flag > 0), 1.0, covered)
    state = []
    for f in range(5):
        for q in range(8):
            first = (q // 4 * 5 + f) * 8
            part = fine[first : first + 8, q % 4 * 128 : q % 4 * 128 + 128]
            state.append(jnp.where(covered > 0.5, part, coarse[f]))
    state += coarse
    fastest = None
    for u in [[state[f * 8 + q] for f in range(5)] for q in range(8)] + [coarse]:
        v, pressure, sound = primitive(u)
        speed = jnp.abs(v[0]) + jnp.abs(v[1]) + jnp.abs(v[2]) + 3.0 * sound
        fastest = speed if fastest is None else jnp.maximum(fastest, speed)
    fastest = jnp.where(inside(y) & inside(z), fastest, 0.0)
    fastest = jnp.broadcast_to(jnp.max(fastest), (8, LANES))

    zero = jnp.zeros((8, LANES), jnp.float32)
    stored = state + [zero] * 5 + [covered]
    for n in range(COUNT):
        inner_ref[n] = stored[n]

    for t in range(8):
        send_ref[t, 0, FACE - 1 : FACE, :] = fastest[:1]

    def taken(n, at, deep_at):
        return (stored[n - 5], deep_at) if is_deep(n) else (stored[n], at)

    for side, at, deep_at in ((0, 7, 6), (1, 0, 1)):
        for n in range(COUNT):
            value, where = taken(n, at, deep_at)
            target = side * 64 + (n if n < PAIRED else n - PAIRED + 32)
            scr_x[target : target + 1, :] = value[where : where + 1, :]
    dense = place(scr_x[...], dense_ref[...])
    left4 = lax.broadcasted_iota(jnp.int32, (32, LANES), 1) < 64
    row32 = lax.broadcasted_iota(jnp.int32, (32, LANES), 0)
    for side in range(2):
        packed = jnp.where(left4, dense[side * 64 : side * 64 + 32], roll(dense[side * 64 + 32 : side * 64 + 64], 64, 1))
        packed = jnp.where(row32 >= PAIRED, jnp.concatenate([fastest] * 4, axis=0), packed)
        send_ref[own ^ 1, far[0] if side == 0 else 1 - far[0]] = packed

    slots = lane - ((lane * 205) >> 11) * PITCH
    corners_xy, corners_xz, corners = [], [], zero
    for side, at, deep_at in ((0, 7, 6), (1, 0, 1)):
        near = 1 - side
        order = y_order(near)
        blocks = []
        for names in order:
            packed = fastest
            for s, n in enumerate(names):
                value, where = taken(n, at, deep_at)
                packed = jnp.where((lane >> 3) == s, roll(value, s * 8 - where * PITCH, 1), packed)
            blocks.append(packed)
        width = len(order[3]) * 8
        second = (lane >= width) & (lane < 2 * width)
        blocks[3] = jnp.where(second, roll(roll(blocks[3], width, 1), 4, 0), blocks[3])
        part = far[1] if side == 0 else 1 - far[1]
        for block in range(3):
            send_ref[own ^ 2, part, block * 8 : block * 8 + 8, :] = blocks[block]
        send_ref[own ^ 2, part, 24:FACE, :] = blocks[3][:4]
        corners_xy.append((blocks[0][7:8], jnp.where(lane < 80, blocks[1], blocks[0])[0:1]))

        blocks = []
        for block, (names, halves) in enumerate(z_order(near)):
            packed = fastest
            for s, n in enumerate(names):
                value, where = taken(n, at, deep_at)
                packed = jnp.where((slots == s) & (lane < 80), roll(value, s - where, 1), packed)
            if block < 3:
                extra = fastest
                for s, n in enumerate(halves):
                    value, where = taken(n, at, deep_at)
                    extra = jnp.where(slots == s, roll(value, s - where, 1), extra)
                extra = jnp.where(slots < 5, roll(extra, 80, 1), roll(extra, 45, 1))
                packed = jnp.where((lane >= 80) & (lane < MAX_LANE), extra, packed)
            else:
                second = (slots >= 5) & (lane < 80)
                packed = jnp.where(second, roll(roll(packed, 5, 1), 4, 0), packed)
                value = stored[halves[0]]
                lower = roll(value, 4, 0)
                pieces = [roll(value, 80 - at, 1), roll(value, 41 - at, 1), roll(lower, 82 - at, 1), roll(lower, 43 - at, 1)]
                for s, piece in enumerate(pieces):
                    packed = jnp.where((slots == s) & (lane >= 80) & (lane < MAX_LANE), piece, packed)
            blocks.append(packed)
        part = far[2] if side == 0 else 1 - far[2]
        for block in range(3):
            send_ref[own ^ 4, part, block * 8 : block * 8 + 8, :] = blocks[block]
        send_ref[own ^ 4, part, 24:FACE, :] = blocks[3][:4]
        corners_xz.append((blocks[0][7:8], jnp.where(lane < 80, blocks[1], blocks[0])[0:1]))
        for end, first, first_coarse in ((0, 75, 115), (1, 0, 80)):
            to = (side * 2 + end) * 16
            for start, source, i in ((first, blocks[0], 0), (first, blocks[1], 5), (first_coarse, blocks[0], 10)):
                here = (lane >= to + i) & (lane < to + i + 5)
                corners = jnp.where(here, roll(source, to + i - start, 1), corners)
    corners = block_transpose(corners)

    edges = [
        [[corners_xy[e][d] for e in range(2)] for d in range(2)],
        [[corners_xz[e][d] for e in range(2)] for d in range(2)],
        [[corners[e * 2 + d : e * 2 + d + 1] for e in range(2)] for d in range(2)],
    ]
    for (d, e), edge in zip(PAIRS, edges):
        upper, lower = [swapped(far[e] == 1, *half) for half in edge]
        near_near, far_near = swapped(far[d] == 1, upper[0], lower[0])
        near_far, far_far = swapped(far[d] == 1, upper[1], lower[1])
        for r, value in enumerate((near_near, near_far, far_near, far_far)):
            send_ref[own ^ (1 << d) ^ (1 << e), 0, r : r + 1, :] = value


def others(d):
    return [e for e in range(3) if e != d]


def pair(d, e):
    return (1 << d) ^ (1 << e)


def running_maximum(rows):
    fastest = functools.reduce(jnp.maximum, rows)
    lane = lax.broadcasted_iota(jnp.int32, fastest.shape, 1)
    fastest = jnp.where(lane >= MAX_LANE, fastest, 0.0)
    return jnp.broadcast_to(jnp.max(fastest), (1, LANES))


def pass_on(send_ref, own, fastest, faces, edges, corners):
    lane = lax.broadcasted_iota(jnp.int32, (1, LANES), 1)
    for t in range(8):
        send_ref[t, FACE - 1 : FACE, :] = fastest
    for d in range(3):
        slot = own ^ (1 << d)
        send_ref[slot, : FACE - 1, :] = faces[d](0, FACE - 1)
        last = faces[d](FACE - 1, FACE)
        send_ref[slot, FACE - 1 : FACE, :] = jnp.where(lane >= MAX_LANE, fastest, last)
        for r, value in enumerate(edges[d]):
            send_ref[slot, FACE + r : FACE + r + 1, :] = value
    for (d, e), value in zip(PAIRS, corners):
        send_ref[own ^ pair(d, e), 0:1, :] = value


def carry_once(got_ref, send_ref):
    own, to, _ = whereabouts()[0]
    fastest = running_maximum([got_ref[t, 0, FACE - 1 : FACE, :] for t in range(8)])
    faces = [lambda i, j, d=d: got_ref[own ^ (1 << d), 1, i:j, :] for d in range(3)]

    def edge(d, e, r):
        return got_ref[own ^ pair(d, e), 0, r : r + 1, :]

    edges = [[edge(d, e, 1 if e < d else 2) for e in others(d)] for d in range(3)]
    pass_on(send_ref, to, fastest, faces, edges, [edge(d, e, 3) for d, e in PAIRS])


def carry_twice(got_ref, send_ref):
    _, own, to = whereabouts()[0]
    fastest = running_maximum([got_ref[t, FACE - 1 : FACE, :] for t in range(8)])
    faces = [lambda i, j, d=d: got_ref[own ^ (1 << d), i:j, :] for d in range(3)]

    def far_far(d, e):
        return got_ref[own ^ pair(d, e), 0:1, :]

    edges = []
    for d in range(3):
        passed = [got_ref[own ^ (1 << d), FACE + r : FACE + r + 1, :] for r in range(2)]
        edges.append(passed + [far_far(d, e) for e in others(d)])
    pass_on(send_ref, to, fastest, faces, edges, [far_far(d, e) for d, e in PAIRS])


def arrived(got0, got1, got2):
    own, first, twice = whereabouts()
    upper_far = [bit == 1 for bit in first]
    faces = []
    for d in range(3):
        near = got0[own[0] ^ (1 << d), 0]
        far = jnp.where(twice[d], got2[own[2] ^ (1 << d)], got1[own[1] ^ (1 << d)])
        faces.append(swapped(upper_far[d], near, far))

    def once(d, r):
        return got1[own[1] ^ (1 << d), FACE + r : FACE + r + 1, :]

    def again(d, r):
        return got2[own[2] ^ (1 << d), FACE + r : FACE + r + 1, :]

    edges = []
    for d, e in PAIRS:
        of_e, of_d = others(d).index(e), others(e).index(d)
        near_near = got0[own[0] ^ pair(d, e), 0, 0:1, :]
        near_far = jnp.where(twice[e], again(e, of_d), once(e, of_d))
        far_near = jnp.where(twice[d], again(d, of_e), once(d, of_e))
        both = jnp.where(twice[e], got2[own[2] ^ pair(d, e), 0:1, :], again(d, 2 + of_e))
        neither = jnp.where(twice[e], again(e, 2 + of_d), got1[own[1] ^ pair(d, e), 0:1, :])
        far_far = jnp.where(twice[d], both, neither)
        near, far = [swapped(upper_far[e], *half) for half in ((near_near, near_far), (far_near, far_far))]
        above, below = zip(*[swapped(upper_far[d], n, f) for n, f in zip(near, far)])
        edges.append((above, below))
    return faces, edges


def surround(faces, edges, inner_ref, spread, scr_x):
    lane, x, y, z = positions(8)
    row = lax.broadcasted_iota(jnp.int32, (8, LANES), 0)
    left4 = lax.broadcasted_iota(jnp.int32, (32, LANES), 1) < 64
    inner = [inner_ref[n] for n in range(COUNT)]
    rows = []
    for side in range(2):
        value = faces[0][side]
        rows += [jnp.where(left4, value, 0.0), jnp.where(left4, roll(value, 64, 1), 0.0)]
    scr_x[...] = place(jnp.concatenate(rows, axis=0), spread)
    outer = []
    for n in range(COUNT):
        at = n if n < PAIRED else n - PAIRED + 32
        above = jnp.broadcast_to(scr_x[at : at + 1, :], (8, LANES))
        below = jnp.broadcast_to(scr_x[at + 64 : at + 65, :], (8, LANES))
        outer.append(jnp.where(row == 0, above, below))

    def doubled(value):
        return jnp.concatenate([value[24:28], value[24:28]], axis=0)

    for side, (near, at) in enumerate(SIDES):
        blocks = [faces[1][side][block * 8 : block * 8 + 8] for block in range(3)]
        order = y_order(near)
        first = at * PITCH % LANES
        here = (lane >= first) & (lane < first + 8)
        for block, names in zip(blocks, order):
            for s, n in enumerate(names):
                inner[n] = jnp.where(here, roll(block, first - s * 8, 1), inner[n])
        last = doubled(faces[1][side])
        for s, n in enumerate(order[3]):
            value = jnp.where(row < 4, roll(last, first - s * 8, 1), roll(last, first - (s + len(order[3])) * 8, 1))
            inner[n] = jnp.where(here, value, inner[n])
        above, below = [jnp.broadcast_to(edges[0][end][side], (8, LANES)) for end in range(2)]
        edge = jnp.where(row == 0, above, below)
        for s in range(15):
            value = roll(edge, first - s * 8, 1)
            for n in (order[0][s], order[1][s]) if s < 10 else (order[0][s],):
                outer[n] = jnp.where(here, value, outer[n])

    columns = jnp.concatenate([edges[2][end][side] for side in range(2) for end in range(2)] * 2, axis=0)
    columns = block_transpose(columns)
    for side, (near, at) in enumerate(SIDES):
        blocks = [faces[2][side][block * 8 : block * 8 + 8] for block in range(3)]
        order = z_order(near)
        here = (z == at) & (y < 9)
        low_y = y < 4
        above, below = side * 32, side * 32 + 16

        def joined(block):
            return jnp.where(lane < 40, roll(block, -80, 1), roll(block, -45, 1))

        def ended(block, i, below_lane):
            block = jnp.where(lane < 80, block, roll(columns, 80 - above - i, 1))
            return jnp.where(lane >= below_lane, roll(columns, below_lane - below - i, 1), block)

        mains = [ended(blocks[0], 0, 123), ended(blocks[1], 5, 123), blocks[2]]
        halves = [ended(joined(blocks[0]), 10, 118), joined(blocks[1]), joined(blocks[2])]
        for block in range(3):
            for source, names in ((mains[block], order[block][0]), (halves[block], order[block][1])):
                for s, n in enumerate(names):
                    inner[n] = jnp.where(here, roll(source, at - s, 1), inner[n])
        last = doubled(faces[2][side])
        for s, n in enumerate(order[3][0]):
            value = jnp.where(row < 4, roll(last, at - s, 1), roll(last, at - 5 - s, 1))
            inner[n] = jnp.where(here, value, inner[n])
        upper_rows = jnp.where(low_y, roll(last, at - 80, 1), roll(last, at - 41, 1))
        lower_rows = jnp.where(low_y, roll(last, at - 82, 1), roll(last, at - 43, 1))
        n = order[3][1][0]
        inner[n] = jnp.where(here, jnp.where(row < 4, upper_rows, lower_rows), inner[n])

        above, below = [jnp.broadcast_to(edges[1][end][side], (8, LANES)) for end in range(2)]
        edge = jnp.where(row == 0, above, below)
        for s in range(10):
            value = roll(edge, at - s, 1)
            for n in (order[0][0][s], order[1][0][s]):
                outer[n] = jnp.where(here & inside(y), value, outer[n])
        edge = joined(edge)
        for s in range(5):
            n = COARSE + s
            outer[n] = jnp.where(here & inside(y), roll(edge, at - s, 1), outer[n])
    return [jnp.concatenate([i, o], axis=0) for i, o in zip(inner, outer)]


def advance(got0, got1, got2, inner_ref, back_ref, spread_ref, dense_ref, coarse_out, fine_out, scr, scr_x):
    lane, x, y, z = positions(16)
    fastest = running_maximum([got2[t, FACE - 1 : FACE, :] for t in range(8)])
    half16 = 0.5 * (courant / jnp.broadcast_to(fastest, (16, LANES)))
    half = half16[:8]
    faces, edges = arrived(got0, got1, got2)
    state = surround(faces, edges, inner_ref, spread_ref[...], scr_x)
    covered = state[COVER] > 0.5
    fine0 = [[state[f * 8 + q] for f in range(5)] for q in range(8)]
    coarse0 = state[COARSE:DEEP]

    net = coarse_net(coarse0, state[DEEP:COVER], (x, y, z))
    coarse1 = [u - 0.5 * half16 * n for u, n in zip(coarse0, net)]
    net = fine_net(fine0, False)
    fine1 = [
        [jnp.where(covered, fine0[q][f] - half16 * net[q][f], coarse1[f]) for f in range(5)] for q in range(8)
    ]
    net = coarse_net(coarse1, None, None)
    coarse2 = [0.5 * c0[:8] + 0.5 * (c1[:8] - 0.5 * half * n[:8]) for c0, c1, n in zip(coarse0, coarse1, net)]
    net = fine_net(fine1, True)
    mine = inside(y[:8]) & inside(z[:8])
    refined = mine & covered[:8]
    fine2 = [
        [
            jnp.where(refined, 0.5 * fine0[q][f][:8] + 0.5 * (fine1[q][f][:8] - half * net[q][f]), 0.0)
            for f in range(5)
        ]
        for q in range(8)
    ]
    coarse = []
    for f in range(5):
        total = functools.reduce(jnp.add, [fine2[q][f] for q in range(8)])
        coarse.append(jnp.where(mine, jnp.where(refined, 0.125 * total, coarse2[f]), 0.0))

    left_half = lane[:8] < 64
    rows = [jnp.concatenate([fine2[a * 4 + q][f] for q in range(4)], axis=1) for a in range(2) for f in range(5)]
    back = place(jnp.concatenate(rows, axis=0), back_ref[...])
    for f in range(5):
        for h in range(2):
            even = back[f * 8 : f * 8 + 8, h * 128 : h * 128 + 128]
            odd = back[40 + f * 8 : 48 + f * 8, h * 128 : h * 128 + 128]
            scr[f, h * 16 : h * 16 + 8, :] = jnp.where(left_half, even, roll(odd, 64, 1))
            scr[f, h * 16 + 8 : h * 16 + 16, :] = jnp.where(left_half, roll(even, 64, 1), odd)
        for q in range(4):
            for ox in range(2):
                tile = scr[f, pl.ds(ox * 4 + q, 4, stride=8), :]
                fine_out[f, ox * 4 : ox * 4 + 4, q * 128 : q * 128 + 128] = tile
    back = place(jnp.concatenate(coarse, axis=0), dense_ref[...])
    for f in range(5):
        value = back[f * 8 : f * 8 + 8]
        value = jnp.where(left_half, value, roll(roll(value, 64, 1), -1, 0))
        for q in range(4):
            coarse_out[f, :, q * 128 : q * 128 + 128] = value[2 * q : 2 * q + 1]


def shape(*dims):
    return jax.ShapeDtypeStruct(dims, jnp.float32)


def call(kernel, outs, scratch, args, cost=None):
    return pl.pallas_call(
        kernel,
        out_shape=outs,
        in_specs=[pl.BlockSpec(memory_space=pltpu.VMEM)] * len(args),
        out_specs=[pl.BlockSpec(memory_space=pltpu.VMEM)] * len(outs),
        scratch_shapes=scratch,
        cost_estimate=cost,
        compiler_params=pltpu.CompilerParams(vmem_limit_bytes=32 * 1024 * 1024),
    )(*args)


def swap(block, level):
    count = lax.axis_size("boxes")
    low = 3 * level
    first = [device for device in range(count) if not (device >> low) & 7]
    groups = [[device | (slot ^ LEAD[level]) << low for slot in range(8)] for device in first]
    return lax.all_to_all(block, "boxes", 0, 0, axis_index_groups=groups)


def local(coarse_state, fine_state, refined):
    back = jnp.asarray(back_matrix().astype(ml_dtypes.bfloat16))
    fields = lambda *dims: pltpu.VMEM(dims, jnp.float32)
    matrix = lambda *dims: jax.ShapeDtypeStruct(dims, jnp.bfloat16)
    made = call(matrices, [matrix(256, 4 * LANES), matrix(LANES, LANES), matrix(LANES, LANES)], [], (), pl.CostEstimate(flops=50000000, bytes_accessed=327680, transcendentals=0))
    inner, send = call(
        prepare,
        [shape(COUNT, 8, LANES), shape(8, 2, ROWS, LANES)],
        [fields(5, 32, LANES), fields(5, 8, LANES), fields(128, LANES)],
        (refined, jnp.swapaxes(coarse_state, 0, 1), jnp.swapaxes(fine_state[0], 0, 1), *made),
    )
    got0 = swap(send, 0)
    got1 = swap(call(carry_once, [shape(8, ROWS, LANES)], [], (got0,))[0], 1)
    got2 = swap(call(carry_twice, [shape(8, ROWS, LANES)], [], (got1,))[0], 2)
    coarse_out, fine_out = call(
        advance,
        [shape(5, 1, 512), shape(5, 8, 512)],
        [fields(5, 32, LANES), fields(128, LANES)],
        (got0, got1, got2, inner, back, *made[1:]),
    )
    return jnp.swapaxes(coarse_out, 0, 1), jnp.swapaxes(fine_out, 0, 1)[None]


def solution(mesh):
    in_specs = (P("boxes", None, None), P("boxes", None, None, None), P("boxes", None))
    out_specs = (P("boxes", None, None), P("boxes", None, None, None))
    return jax.shard_map(local, mesh=mesh, in_specs=in_specs, out_specs=out_specs, check_vma=False)
```

```python
import functools

import jax
import jax.numpy as jnp
import ml_dtypes
import numpy as np
from jax import lax
from jax.experimental import pallas as pl
from jax.experimental.pallas import tpu as pltpu
from jax.sharding import PartitionSpec as P

PITCH = 10
LANES = 128
FINE = 40
COARSE = FINE
DEEP = COARSE + 5
COVER = DEEP + 5
COUNT = COVER + 1
FACE = 28
ROWS = 32
MAX_LANE = 120
PAIRED = 26
LEAD = (5, 6, 4)
SIDES = ((0, 8), (1, -1))
PAIRS = ((0, 1), (0, 2), (1, 2))
gamma_gas = 1.4
courant = 0.4


def back_matrix():
    back = np.zeros((512, 256), np.float32)
    for y in range(16):
        for z in range(16):
            row = (y // 8 * 2 + z // 8) * 64 + y % 8 * 8 + z % 8
            back[(y % 2 * 2 + z % 2) * 128 + y // 2 * PITCH + z // 2, row] = 1
    return back


def place(values, matrix):
    high = values.astype(jnp.bfloat16)
    rest = values - high.astype(jnp.float32)
    middle = rest.astype(jnp.bfloat16)
    low = (rest - middle.astype(jnp.float32)).astype(jnp.bfloat16)
    rows = values.shape[0]
    parts = jnp.concatenate([high, middle, low], axis=0)
    out = jnp.dot(parts, matrix, preferred_element_type=jnp.float32)
    return out[:rows] + out[rows : 2 * rows] + out[2 * rows :]


def roll(x, shift, axis):
    shift = shift % x.shape[axis]
    return pltpu.roll(x, shift, axis) if shift else x


def positions(rows):
    row = lax.broadcasted_iota(jnp.int32, (rows, LANES), 0)
    lane = lax.broadcasted_iota(jnp.int32, (rows, LANES), 1)
    x = jnp.where(row > 8, row - 16, row)
    along = (lane + PITCH + 1) & (LANES - 1)
    y1 = (along * 205) >> 11
    return lane, x, y1 - 1, along - y1 * PITCH - 1


def inside(pos):
    return (pos >= 0) & (pos < 8)


def primitive(u):
    inverse = 1.0 / u[0]
    v = [u[1 + d] * inverse for d in range(3)]
    pressure = 0.4 * (u[4] - 0.5 * (u[1] * v[0] + u[2] * v[1] + u[3] * v[2]))
    sound = jnp.sqrt(gamma_gas * pressure * inverse)
    return v, pressure, sound


def cell_flux(u, prim, d):
    v, pressure, sound = prim
    flux = [u[1 + d]] + [u[1 + e] * v[d] for e in range(3)] + [(u[4] + pressure) * v[d]]
    flux[1 + d] = flux[1 + d] + pressure
    return list(u) + flux + [jnp.abs(v[d]) + sound]


def face(left, right):
    speed = jnp.maximum(left[10], right[10])
    return [(left[5 + f] + right[5 + f]) - speed * (right[f] - left[f]) for f in range(5)]


def ahead(x, d):
    return roll(x, -1, 0) if d == 0 else roll(x, -PITCH if d == 1 else -1, 1)


def behind(x, d):
    return roll(x, 1, 0) if d == 0 else roll(x, PITCH if d == 1 else 1, 1)


def fine_net(u, beside, beyond):
    row = lax.broadcasted_iota(jnp.int32, (8, LANES), 0)
    prims, prims_beside = [primitive(v) for v in u], [primitive(v) for v in beside]
    total, total_beside = [None] * 8, [None] * 4

    def add(totals, q, net):
        totals[q] = net if totals[q] is None else [s + n for s, n in zip(totals[q], net)]

    def minus(left, right):
        return [a - b for a, b in zip(left, right)]

    def either(flag, first, second):
        return [jnp.where(flag, a, b) for a, b in zip(first, second)]

    for q in range(4):
        low, high = cell_flux(u[q], prims[q], 0), cell_flux(u[q + 4], prims[q + 4], 0)
        near = cell_flux(beside[q], prims_beside[q], 0)
        middle = face(low, high)
        after = face(high, either(row == 7, near, [roll(x, -1, 0) for x in low]))
        first = face(near, low)
        add(total, q, minus(middle, either(row == 0, first, [roll(x, 1, 0) for x in after])))
        add(total, q + 4, minus(after, middle))
        if beyond is not None:
            next_ = cell_flux(beyond[q], primitive(beyond[q]), 0)
            outer = face(either(row == 0, next_, near), either(row == 0, near, next_))
            add(total_beside, q, either(row == 0, minus(first, outer), minus(outer, after)))
    groups = [(u, prims, total, (0, 4))]
    if beyond is not None:
        groups.append((beside, prims_beside, total_beside, (0,)))
    for d in (1, 2):
        bit = 4 >> d
        for cells, prim, totals, starts in groups:
            for low in [start + q for start in starts for q in range(4) if not q & bit]:
                high = low | bit
                left, right = cell_flux(cells[low], prim[low], d), cell_flux(cells[high], prim[high], d)
                middle = face(left, right)
                after = face(right, [ahead(x, d) for x in left])
                add(totals, low, minus(middle, [behind(x, d) for x in after]))
                add(totals, high, minus(after, middle))
    return total, total_beside


def coarse_net(u, deep, pos):
    prim = primitive(u)
    prim_deep = None if deep is None else primitive(deep)
    total = None
    for d in range(3):
        cell = cell_flux(u, prim, d)
        right = [ahead(x, d) for x in cell]
        if deep is not None:
            outer = cell_flux(deep, prim_deep, d)
            last, first = pos[d] == 8, pos[d] == -1
            right = [jnp.where(last, o, r) for o, r in zip(outer, right)]
        after = face(cell, right)
        before = [behind(x, d) for x in after]
        if deep is not None:
            before = [jnp.where(first, o, b) for o, b in zip(face(outer, cell), before)]
        net = [a - b for a, b in zip(after, before)]
        total = net if total is None else [s + n for s, n in zip(total, net)]
    return total


def put_faces(send_ref, slot, upper_far, faces):
    for side, blocks in enumerate(faces):
        first = pl.multiple_of((upper_far if side == 0 else 1 - upper_far) * 32, 8)
        for block in range(3):
            send_ref[slot, pl.ds(first + block * 8, 8), :] = blocks[block]
    near, far = swapped(upper_far == 1, faces[0][3], faces[1][3])
    send_ref[slot, 24:32, :] = jnp.concatenate([near[:4], far[:4]], axis=0)


def is_deep(n):
    return DEEP <= n < COVER


def fine_index(f, a, b, c):
    return f * 8 + a * 4 + b * 2 + c


def y_order(near):
    rest = [fine_index(f, a, 1 - near, c) for f in range(5) for a in range(2) for c in range(2)]
    first = [fine_index(f, 1, near, c) for c in range(2) for f in range(5)]
    second = [fine_index(f, 0, near, c) for c in range(2) for f in range(5)]
    return (
        first + [COARSE + f for f in range(5)] + rest[:1],
        second + [DEEP + f for f in range(5)] + [COVER],
        rest[1:17],
        rest[17:],
    )


def z_order(near):
    rest = [fine_index(f, a, b, 1 - near) for f in range(5) for a in range(2) for b in range(2)]
    first = [fine_index(f, 1, b, near) for b in range(2) for f in range(5)]
    second = [fine_index(f, 0, b, near) for b in range(2) for f in range(5)]
    return (
        (first, [COARSE + f for f in range(5)]),
        (second, [DEEP + f for f in range(5)]),
        (rest[:10], [COVER] + rest[10:14]),
        (rest[14:19], rest[19:]),
    )


def block_transpose(value):
    row = lax.broadcasted_iota(jnp.int32, (8, LANES), 0)
    group = lax.broadcasted_iota(jnp.int32, (8, LANES), 1) >> 4
    out = value
    for step in range(1, 8):
        moved = roll(roll(value, -16 * step, 1), step, 0)
        out = jnp.where(((row - group) & 7) == step, moved, out)
    return out


def swapped(flag, first, second):
    return jnp.where(flag, second, first), jnp.where(flag, first, second)


def whereabouts():
    device = lax.axis_index("boxes")
    own = [((device >> (3 * level)) & 7) ^ lead for level, lead in enumerate(LEAD)]
    first = [(device >> d) & 1 for d in range(3)]
    second = [(device >> (3 + d)) & 1 for d in range(3)]
    return own, first, [a == b for a, b in zip(first, second)]


def fine_matrix():
    row = lax.broadcasted_iota(jnp.int32, (256, LANES), 0)
    lane = lax.broadcasted_iota(jnp.int32, (256, LANES), 1)
    y = ((row >> 7) << 2) + ((row >> 4) & 3)
    z = (((row >> 6) & 1) << 2) + ((row >> 1) & 3)
    hit = lane == y * PITCH + z
    parity = ((row >> 2) & 2) + (row & 1)
    return [jnp.where(hit & (parity == q), 1.0, 0.0).astype(jnp.bfloat16) for q in range(4)]


def coarse_matrices():
    row = lax.broadcasted_iota(jnp.int32, (LANES, LANES), 0)
    lane = lax.broadcasted_iota(jnp.int32, (LANES, LANES), 1)
    spread = (row < 64) & (lane == (row >> 3) * PITCH + (row & 7))
    dense = (lane < 64) & (row == (lane >> 3) * PITCH + (lane & 7))
    return [jnp.where(hit, 1.0, 0.0).astype(jnp.bfloat16) for hit in (spread, dense)]


def matrices(place_ref, spread_ref, dense_ref):
    for q, part in enumerate(fine_matrix()):
        place_ref[:, q * LANES : (q + 1) * LANES] = part
    spread_ref[...], dense_ref[...] = coarse_matrices()


def prepare(
    refined_ref, coarse_ref, fine_ref, place_ref, spread_ref, dense_ref, inner_ref, send_ref, scr, scr_c, scr_x
):
    places, far, _ = whereabouts()
    own = places[0]
    lane, x, y, z = positions(8)
    row = lax.broadcasted_iota(jnp.int32, (8, LANES), 0)
    left_half = lane < 64
    for f in range(5):
        for q in range(4):
            tile = fine_ref[f, :, q * 128 : q * 128 + 128]
            for ox in range(2):
                scr[f, pl.ds(ox * 4 + q, 4, stride=8), :] = tile[ox * 4 : ox * 4 + 4]
            part = coarse_ref[f, :, q * 128 : q * 128 + 128]
            scr_c[f, 2 * q : 2 * q + 1, :] = part
            scr_c[f, 2 * q + 1 : 2 * q + 2, :] = part
    sides = [[], []]
    rows = []
    for f in range(5):
        tile = [scr[f, c * 8 : c * 8 + 8, :] for c in range(4)]
        sides[0].append(
            jnp.concatenate([jnp.where(left_half, tile[2 * h], roll(tile[2 * h + 1], 64, 1)) for h in range(2)], axis=1)
        )
        sides[1].append(
            jnp.concatenate([jnp.where(left_half, roll(tile[2 * h], 64, 1), tile[2 * h + 1]) for h in range(2)], axis=1)
        )
        value = scr_c[f]
        rows.append(jnp.where((row & 1) == 1, roll(value, 64, 1), value))
    fine = place(jnp.concatenate(sides[0] + sides[1], axis=0), place_ref[...])
    coarse = place(jnp.concatenate(rows, axis=0), spread_ref[...])
    coarse = [coarse[f * 8 : f * 8 + 8] for f in range(5)]

    covered = jnp.zeros((8, LANES), jnp.float32)
    for o in range(8):
        here = ((x >= 4) == (o >= 4)) & ((y >= 4) == (o % 4 >= 2)) & ((z >= 4) == (o % 2 == 1))
        flag = jnp.broadcast_to(refined_ref[:, o : o + 1], (8, LANES))
        covered = jnp.where(here & (flag > 0), 1.0, covered)
    state = []
    for f in range(5):
        for q in range(8):
            first = (q // 4 * 5 + f) * 8
            part = fine[first : first + 8, q % 4 * 128 : q % 4 * 128 + 128]
            state.append(jnp.where(covered > 0.5, part, coarse[f]))
    state += coarse
    fastest = None
    for u in [[state[f * 8 + q] for f in range(5)] for q in range(8)] + [coarse]:
        v, pressure, sound = primitive(u)
        speed = jnp.abs(v[0]) + jnp.abs(v[1]) + jnp.abs(v[2]) + 3.0 * sound
        fastest = speed if fastest is None else jnp.maximum(fastest, speed)
    fastest = jnp.where(inside(y) & inside(z), fastest, 0.0)
    fastest = jnp.broadcast_to(jnp.max(fastest), (8, LANES))

    zero = jnp.zeros((8, LANES), jnp.float32)
    stored = state + [zero] * 5 + [covered]
    for n in range(COUNT):
        inner_ref[n] = stored[n]

    for t in range(8):
        send_ref[t, FACE - 1 : FACE, :] = fastest[:1]

    def taken(n, at, deep_at):
        return (stored[n - 5], deep_at) if is_deep(n) else (stored[n], at)

    for side, at, deep_at in ((0, 7, 6), (1, 0, 1)):
        for n in range(COUNT):
            value, where = taken(n, at, deep_at)
            target = side * 64 + (n if n < PAIRED else n - PAIRED + 32)
            scr_x[target : target + 1, :] = value[where : where + 1, :]
    dense = place(scr_x[...], dense_ref[...])
    left4 = lax.broadcasted_iota(jnp.int32, (32, LANES), 1) < 64
    row32 = lax.broadcasted_iota(jnp.int32, (32, LANES), 0)
    faces_x, faces_y, faces_z = [], [], []
    for side in range(2):
        packed = jnp.where(left4, dense[side * 64 : side * 64 + 32], roll(dense[side * 64 + 32 : side * 64 + 64], 64, 1))
        packed = jnp.where(row32 >= PAIRED, jnp.concatenate([fastest] * 4, axis=0), packed)
        faces_x.append([packed[block * 8 : block * 8 + 8] for block in range(4)])
    put_faces(send_ref, own ^ 1, far[0], faces_x)

    slots = lane - ((lane * 205) >> 11) * PITCH
    corners_xy, corners_xz, corners = [], [], zero
    for side, at, deep_at in ((0, 7, 6), (1, 0, 1)):
        near = 1 - side
        order = y_order(near)
        blocks = []
        for names in order:
            packed = fastest
            for s, n in enumerate(names):
                value, where = taken(n, at, deep_at)
                packed = jnp.where((lane >> 3) == s, roll(value, s * 8 - where * PITCH, 1), packed)
            blocks.append(packed)
        width = len(order[3]) * 8
        second = (lane >= width) & (lane < 2 * width)
        blocks[3] = jnp.where(second, roll(roll(blocks[3], width, 1), 4, 0), blocks[3])
        faces_y.append(blocks)
        corners_xy.append((blocks[0][7:8], jnp.where(lane < 80, blocks[1], blocks[0])[0:1]))

        blocks = []
        for block, (names, halves) in enumerate(z_order(near)):
            packed = fastest
            for s, n in enumerate(names):
                value, where = taken(n, at, deep_at)
                packed = jnp.where((slots == s) & (lane < 80), roll(value, s - where, 1), packed)
            if block < 3:
                extra = fastest
                for s, n in enumerate(halves):
                    value, where = taken(n, at, deep_at)
                    extra = jnp.where(slots == s, roll(value, s - where, 1), extra)
                extra = jnp.where(slots < 5, roll(extra, 80, 1), roll(extra, 45, 1))
                packed = jnp.where((lane >= 80) & (lane < MAX_LANE), extra, packed)
            else:
                second = (slots >= 5) & (lane < 80)
                packed = jnp.where(second, roll(roll(packed, 5, 1), 4, 0), packed)
                value = stored[halves[0]]
                lower = roll(value, 4, 0)
                pieces = [roll(value, 80 - at, 1), roll(value, 41 - at, 1), roll(lower, 82 - at, 1), roll(lower, 43 - at, 1)]
                for s, piece in enumerate(pieces):
                    packed = jnp.where((slots == s) & (lane >= 80) & (lane < MAX_LANE), piece, packed)
            blocks.append(packed)
        faces_z.append(blocks)
        corners_xz.append((blocks[0][7:8], jnp.where(lane < 80, blocks[1], blocks[0])[0:1]))
        for end, first, first_coarse in ((0, 75, 115), (1, 0, 80)):
            to = (side * 2 + end) * 16
            for start, source, i in ((first, blocks[0], 0), (first, blocks[1], 5), (first_coarse, blocks[0], 10)):
                here = (lane >= to + i) & (lane < to + i + 5)
                corners = jnp.where(here, roll(source, to + i - start, 1), corners)
    put_faces(send_ref, own ^ 2, far[1], faces_y)
    put_faces(send_ref, own ^ 4, far[2], faces_z)
    corners = block_transpose(corners)

    edges = [
        [[corners_xy[e][d] for e in range(2)] for d in range(2)],
        [[corners_xz[e][d] for e in range(2)] for d in range(2)],
        [[corners[e * 2 + d : e * 2 + d + 1] for e in range(2)] for d in range(2)],
    ]
    for (d, e), edge in zip(PAIRS, edges):
        upper, lower = [swapped(far[e] == 1, *half) for half in edge]
        near_near, far_near = swapped(far[d] == 1, upper[0], lower[0])
        near_far, far_far = swapped(far[d] == 1, upper[1], lower[1])
        for r, value in enumerate((near_near, near_far, far_near, far_far)):
            send_ref[own ^ pair(d, e), r : r + 1, :] = value


def others(d):
    return [e for e in range(3) if e != d]


def pair(d, e):
    return (1 << d) ^ (1 << e)


def running_maximum(rows):
    fastest = functools.reduce(jnp.maximum, rows)
    lane = lax.broadcasted_iota(jnp.int32, fastest.shape, 1)
    fastest = jnp.where(lane >= MAX_LANE, fastest, 0.0)
    return jnp.broadcast_to(jnp.max(fastest), (1, LANES))


def pass_on(send_ref, own, fastest, faces, edges, corners):
    lane = lax.broadcasted_iota(jnp.int32, (1, LANES), 1)
    for t in range(8):
        send_ref[t, FACE - 1 : FACE, :] = fastest
    for d in range(3):
        slot = own ^ (1 << d)
        send_ref[slot, :FACE, :] = faces[d]
        send_ref[slot, FACE - 1 : FACE, :] = jnp.where(lane >= MAX_LANE, fastest, faces[d][FACE - 1 : FACE])
        for r, value in enumerate(edges[d]):
            send_ref[slot, FACE + r : FACE + r + 1, :] = value
    for (d, e), value in zip(PAIRS, corners):
        send_ref[own ^ pair(d, e), 0:1, :] = value


def carry_once(got_ref, send_ref):
    own, to, _ = whereabouts()[0]
    fastest = running_maximum([got_ref[t, FACE - 1 : FACE, :] for t in range(8)])
    faces = [
        jnp.concatenate([got_ref[own ^ (1 << d), 32:, :], got_ref[own ^ (1 << d), FACE:32, :]], axis=0)
        for d in range(3)
    ]

    def edge(d, e, r):
        return got_ref[own ^ pair(d, e), r : r + 1, :]

    edges = [[edge(d, e, 1 if e < d else 2) for e in others(d)] for d in range(3)]
    pass_on(send_ref, to, fastest, faces, edges, [edge(d, e, 3) for d, e in PAIRS])


def carry_twice(got_ref, send_ref):
    _, own, to = whereabouts()[0]
    fastest = running_maximum([got_ref[t, FACE - 1 : FACE, :] for t in range(8)])
    faces = [got_ref[own ^ (1 << d), :FACE, :] for d in range(3)]

    def far_far(d, e):
        return got_ref[own ^ pair(d, e), 0:1, :]

    edges = []
    for d in range(3):
        passed = [got_ref[own ^ (1 << d), FACE + r : FACE + r + 1, :] for r in range(2)]
        edges.append(passed + [far_far(d, e) for e in others(d)])
    pass_on(send_ref, to, fastest, faces, edges, [far_far(d, e) for d, e in PAIRS])


def arrived(got0, got1, got2):
    own, first, twice = whereabouts()
    upper_far = [bit == 1 for bit in first]
    faces = []
    for d in range(3):
        near = got0[own[0] ^ (1 << d), :ROWS]
        far = jnp.where(twice[d], got2[own[2] ^ (1 << d)], got1[own[1] ^ (1 << d)])
        faces.append(swapped(upper_far[d], near, far))

    def once(d, r):
        return got1[own[1] ^ (1 << d), FACE + r : FACE + r + 1, :]

    def again(d, r):
        return got2[own[2] ^ (1 << d), FACE + r : FACE + r + 1, :]

    edges = []
    for d, e in PAIRS:
        of_e, of_d = others(d).index(e), others(e).index(d)
        near_near = got0[own[0] ^ pair(d, e), 0:1, :]
        near_far = jnp.where(twice[e], again(e, of_d), once(e, of_d))
        far_near = jnp.where(twice[d], again(d, of_e), once(d, of_e))
        both = jnp.where(twice[e], got2[own[2] ^ pair(d, e), 0:1, :], again(d, 2 + of_e))
        neither = jnp.where(twice[e], again(e, 2 + of_d), got1[own[1] ^ pair(d, e), 0:1, :])
        far_far = jnp.where(twice[d], both, neither)
        near, far = [swapped(upper_far[e], *half) for half in ((near_near, near_far), (far_near, far_far))]
        above, below = zip(*[swapped(upper_far[d], n, f) for n, f in zip(near, far)])
        edges.append((above, below))
    return faces, edges


def surround(faces, edges, inner_ref, spread, scr_x):
    lane, x, y, z = positions(8)
    row = lax.broadcasted_iota(jnp.int32, (8, LANES), 0)
    left4 = lax.broadcasted_iota(jnp.int32, (32, LANES), 1) < 64
    inner = [inner_ref[n] for n in range(COUNT)]
    rows = []
    for side in range(2):
        value = faces[0][side]
        rows += [jnp.where(left4, value, 0.0), jnp.where(left4, roll(value, 64, 1), 0.0)]
    scr_x[...] = place(jnp.concatenate(rows, axis=0), spread)

    def around(n, above_n=None, upper_row=7):
        above_n = n if above_n is None else above_n
        places = [m if m < PAIRED else m - PAIRED + 32 for m in (above_n, n)]
        above = jnp.broadcast_to(scr_x[places[0] : places[0] + 1, :], (8, LANES))
        below = jnp.broadcast_to(scr_x[places[1] + 64 : places[1] + 65, :], (8, LANES))
        return jnp.where(row == upper_row, above, below)

    beside = [[around(f * 8 + 4 + q, f * 8 + q) for f in range(5)] for q in range(4)]
    beyond = [[around(f * 8 + q, f * 8 + 4 + q) for f in range(5)] for q in range(4)]
    covered = around(COVER)
    coarse_outer = [around(n, upper_row=0) for n in range(COARSE, COVER)]

    def put_beside(n, mask, value):
        f, q = n // 8, n % 4
        beside[q][f] = jnp.where(mask, value, beside[q][f])

    def put_coarse(f, mask, value):
        coarse_outer[f] = jnp.where(mask, value, coarse_outer[f])


    def doubled(value):
        return jnp.concatenate([value[24:28], value[24:28]], axis=0)

    for side, (near, at) in enumerate(SIDES):
        blocks = [faces[1][side][block * 8 : block * 8 + 8] for block in range(3)]
        order = y_order(near)
        first = at * PITCH % LANES
        here = (lane >= first) & (lane < first + 8)
        for block, names in zip(blocks, order):
            for s, n in enumerate(names):
                inner[n] = jnp.where(here, roll(block, first - s * 8, 1), inner[n])
        last = doubled(faces[1][side])
        for s, n in enumerate(order[3]):
            value = jnp.where(row < 4, roll(last, first - s * 8, 1), roll(last, first - (s + len(order[3])) * 8, 1))
            inner[n] = jnp.where(here, value, inner[n])
        above, below = [jnp.broadcast_to(edges[0][end][side], (8, LANES)) for end in range(2)]
        edge, coarse_edge = jnp.where(row == 7, above, below), jnp.where(row == 0, above, below)
        for s in range(10):
            put_beside(order[0][s], here, roll(edge, first - s * 8, 1))
        for s in range(10, 15):
            put_coarse(s - 10, here, roll(coarse_edge, first - s * 8, 1))

    columns = jnp.concatenate([edges[2][end][side] for side in range(2) for end in range(2)] * 2, axis=0)
    columns = block_transpose(columns)
    for side, (near, at) in enumerate(SIDES):
        blocks = [faces[2][side][block * 8 : block * 8 + 8] for block in range(3)]
        order = z_order(near)
        here = (z == at) & (y < 9)
        low_y = y < 4
        above, below = side * 32, side * 32 + 16

        def joined(block):
            return jnp.where(lane < 40, roll(block, -80, 1), roll(block, -45, 1))

        def ended(block, i, below_lane):
            block = jnp.where(lane < 80, block, roll(columns, 80 - above - i, 1))
            return jnp.where(lane >= below_lane, roll(columns, below_lane - below - i, 1), block)

        mains = [ended(blocks[0], 0, 123), ended(blocks[1], 5, 123), blocks[2]]
        halves = [ended(joined(blocks[0]), 10, 118), joined(blocks[1]), joined(blocks[2])]
        for block in range(3):
            for source, names in ((mains[block], order[block][0]), (halves[block], order[block][1])):
                for s, n in enumerate(names):
                    inner[n] = jnp.where(here, roll(source, at - s, 1), inner[n])
        last = doubled(faces[2][side])
        for s, n in enumerate(order[3][0]):
            value = jnp.where(row < 4, roll(last, at - s, 1), roll(last, at - 5 - s, 1))
            inner[n] = jnp.where(here, value, inner[n])
        upper_rows = jnp.where(low_y, roll(last, at - 80, 1), roll(last, at - 41, 1))
        lower_rows = jnp.where(low_y, roll(last, at - 82, 1), roll(last, at - 43, 1))
        n = order[3][1][0]
        inner[n] = jnp.where(here, jnp.where(row < 4, upper_rows, lower_rows), inner[n])

        above, below = [jnp.broadcast_to(edges[1][end][side], (8, LANES)) for end in range(2)]
        edge, coarse_edge = jnp.where(row == 7, above, below), joined(jnp.where(row == 0, above, below))
        for s in range(10):
            put_beside(order[0][0][s], here & inside(y), roll(edge, at - s, 1))
        for s in range(5):
            put_coarse(s, here & inside(y), roll(coarse_edge, at - s, 1))
    fine = [[inner[f * 8 + q] for f in range(5)] for q in range(8)]
    coarse = [jnp.concatenate([i, o], axis=0) for i, o in zip(inner[COARSE:COVER], coarse_outer)]
    return fine, beside, beyond, coarse[:5], coarse[5:], inner[COVER] > 0.5, covered > 0.5


def advance(got0, got1, got2, inner_ref, back_ref, spread_ref, dense_ref, coarse_out, fine_out, scr, scr_x):
    lane, x, y, z = positions(16)
    fastest = running_maximum([got2[t, FACE - 1 : FACE, :] for t in range(8)])
    half16 = 0.5 * (courant / jnp.broadcast_to(fastest, (16, LANES)))
    half = half16[:8]
    faces, edges = arrived(got0, got1, got2)
    fine0, beside, beyond, coarse0, deep, covered, covered_beside = surround(
        faces, edges, inner_ref, spread_ref[...], scr_x
    )
    row = lax.broadcasted_iota(jnp.int32, (8, LANES), 0)

    net = coarse_net(coarse0, deep, (x, y, z))
    coarse1 = [u - 0.5 * half16 * n for u, n in zip(coarse0, net)]
    net, net_beside = fine_net(fine0, beside, beyond)

    def first_section(u, net, covered, coarse):
        return [jnp.where(covered, a - half * n, c) for a, n, c in zip(u, net, coarse)]

    coarse_beside = [jnp.where(row == 7, roll(c[8:], 7, 0), roll(c[8:], 1, 0)) for c in coarse1]
    fine1 = [first_section(fine0[q], net[q], covered, [c[:8] for c in coarse1]) for q in range(8)]
    beside1 = [first_section(beside[q], net_beside[q], covered_beside, coarse_beside) for q in range(4)]
    net = coarse_net(coarse1, None, None)
    coarse2 = [0.5 * c0[:8] + 0.5 * (c1[:8] - 0.5 * half * n[:8]) for c0, c1, n in zip(coarse0, coarse1, net)]
    net, _ = fine_net(fine1, beside1, None)
    mine = inside(y[:8]) & inside(z[:8])
    refined = mine & covered
    fine2 = [
        [
            jnp.where(refined, 0.5 * fine0[q][f] + 0.5 * (fine1[q][f] - half * net[q][f]), 0.0)
            for f in range(5)
        ]
        for q in range(8)
    ]
    coarse = []
    for f in range(5):
        total = functools.reduce(jnp.add, [fine2[q][f] for q in range(8)])
        coarse.append(jnp.where(mine, jnp.where(refined, 0.125 * total, coarse2[f]), 0.0))

    left_half = lane[:8] < 64
    rows = [jnp.concatenate([fine2[a * 4 + q][f] for q in range(4)], axis=1) for a in range(2) for f in range(5)]
    back = place(jnp.concatenate(rows, axis=0), back_ref[...])
    for f in range(5):
        for h in range(2):
            even = back[f * 8 : f * 8 + 8, h * 128 : h * 128 + 128]
            odd = back[40 + f * 8 : 48 + f * 8, h * 128 : h * 128 + 128]
            scr[f, h * 16 : h * 16 + 8, :] = jnp.where(left_half, even, roll(odd, 64, 1))
            scr[f, h * 16 + 8 : h * 16 + 16, :] = jnp.where(left_half, roll(even, 64, 1), odd)
        for q in range(4):
            for ox in range(2):
                tile = scr[f, pl.ds(ox * 4 + q, 4, stride=8), :]
                fine_out[f, ox * 4 : ox * 4 + 4, q * 128 : q * 128 + 128] = tile
    back = place(jnp.concatenate(coarse, axis=0), dense_ref[...])
    for f in range(5):
        value = back[f * 8 : f * 8 + 8]
        value = jnp.where(left_half, value, roll(roll(value, 64, 1), -1, 0))
        for q in range(4):
            coarse_out[f, :, q * 128 : q * 128 + 128] = value[2 * q : 2 * q + 1]


def shape(*dims):
    return jax.ShapeDtypeStruct(dims, jnp.float32)


def call(kernel, outs, scratch, args, cost=None):
    return pl.pallas_call(
        kernel,
        out_shape=outs,
        in_specs=[pl.BlockSpec(memory_space=pltpu.VMEM)] * len(args),
        out_specs=[pl.BlockSpec(memory_space=pltpu.VMEM)] * len(outs),
        scratch_shapes=scratch,
        cost_estimate=cost,
        compiler_params=pltpu.CompilerParams(vmem_limit_bytes=32 * 1024 * 1024),
    )(*args)


def swap(block, level):
    count = lax.axis_size("boxes")
    low = 3 * level
    first = [device for device in range(count) if not (device >> low) & 7]
    groups = [[device | (slot ^ LEAD[level]) << low for slot in range(8)] for device in first]
    return lax.all_to_all(block, "boxes", 0, 0, axis_index_groups=groups)


def local(coarse_state, fine_state, refined):
    back = jnp.asarray(back_matrix().astype(ml_dtypes.bfloat16))
    fields = lambda *dims: pltpu.VMEM(dims, jnp.float32)
    matrix = lambda *dims: jax.ShapeDtypeStruct(dims, jnp.bfloat16)
    made = call(matrices, [matrix(256, 4 * LANES), matrix(LANES, LANES), matrix(LANES, LANES)], [], (), pl.CostEstimate(flops=50000000, bytes_accessed=327680, transcendentals=0))
    inner, send = call(
        prepare,
        [shape(COUNT, 8, LANES), shape(8, 2 * FACE, LANES)],
        [fields(5, 32, LANES), fields(5, 8, LANES), fields(128, LANES)],
        (refined, jnp.swapaxes(coarse_state, 0, 1), jnp.swapaxes(fine_state[0], 0, 1), *made),
    )
    got0 = swap(send, 0)
    got1 = swap(call(carry_once, [shape(8, ROWS, LANES)], [], (got0,))[0], 1)
    got2 = swap(call(carry_twice, [shape(8, ROWS, LANES)], [], (got1,))[0], 2)
    coarse_out, fine_out = call(
        advance,
        [shape(5, 1, 512), shape(5, 8, 512)],
        [fields(5, 32, LANES), fields(128, LANES)],
        (got0, got1, got2, inner, back, *made[1:]),
    )
    return jnp.swapaxes(coarse_out, 0, 1), jnp.swapaxes(fine_out, 0, 1)[None]


def solution(mesh):
    in_specs = (P("boxes", None, None), P("boxes", None, None, None), P("boxes", None))
    out_specs = (P("boxes", None, None), P("boxes", None, None, None))
    return jax.shard_map(local, mesh=mesh, in_specs=in_specs, out_specs=out_specs, check_vma=False)
```

```python
import functools

import jax
import jax.numpy as jnp
import ml_dtypes
import numpy as np
from jax import lax
from jax.experimental import pallas as pl
from jax.experimental.pallas import tpu as pltpu
from jax.sharding import PartitionSpec as P

PITCH = 10
LANES = 128
FINE = 40
COARSE = FINE
DEEP = COARSE + 5
COVER = DEEP + 5
COUNT = COVER + 1
FACE = 28
ROWS = 32
MAX_LANE = 120
PAIRED = 26
LEAD = (5, 6, 4)
SIDES = ((0, 8), (1, -1))
PAIRS = ((0, 1), (0, 2), (1, 2))
gamma_gas = 1.4
courant = 0.4


def back_matrix():
    back = np.zeros((512, 256), np.float32)
    for y in range(16):
        for z in range(16):
            row = (y // 8 * 2 + z // 8) * 64 + y % 8 * 8 + z % 8
            back[(y % 2 * 2 + z % 2) * 128 + y // 2 * PITCH + z // 2, row] = 1
    return back


def place(values, matrix):
    high = values.astype(jnp.bfloat16)
    rest = values - high.astype(jnp.float32)
    middle = rest.astype(jnp.bfloat16)
    low = (rest - middle.astype(jnp.float32)).astype(jnp.bfloat16)
    rows = values.shape[0]
    parts = jnp.concatenate([high, middle, low], axis=0)
    out = jnp.dot(parts, matrix, preferred_element_type=jnp.float32)
    return out[:rows] + out[rows : 2 * rows] + out[2 * rows :]


def roll(x, shift, axis):
    shift = shift % x.shape[axis]
    return pltpu.roll(x, shift, axis) if shift else x


def positions(rows):
    row = lax.broadcasted_iota(jnp.int32, (rows, LANES), 0)
    lane = lax.broadcasted_iota(jnp.int32, (rows, LANES), 1)
    x = jnp.where(row > 8, row - 16, row)
    along = (lane + PITCH + 1) & (LANES - 1)
    y1 = (along * 205) >> 11
    return lane, x, y1 - 1, along - y1 * PITCH - 1


def inside(pos):
    return (pos >= 0) & (pos < 8)


def primitive(u):
    inverse = 1.0 / u[0]
    v = [u[1 + d] * inverse for d in range(3)]
    pressure = 0.4 * (u[4] - 0.5 * (u[1] * v[0] + u[2] * v[1] + u[3] * v[2]))
    sound = jnp.sqrt(gamma_gas * pressure * inverse)
    return v, pressure, sound


def cell_flux(u, prim, d):
    v, pressure, sound = prim
    flux = [u[1 + d]] + [u[1 + e] * v[d] for e in range(3)] + [(u[4] + pressure) * v[d]]
    flux[1 + d] = flux[1 + d] + pressure
    return list(u) + flux + [jnp.abs(v[d]) + sound]


def moved_cell(u, prim, d, shift):
    v, pressure, sound = prim
    u, v_d = [shift(f) for f in u], shift(v[d])
    pressure = shift(pressure)
    flux = [u[1 + d]] + [u[1 + e] * v_d for e in range(3)] + [(u[4] + pressure) * v_d]
    flux[1 + d] = flux[1 + d] + pressure
    return u + flux + [shift(jnp.abs(v[d]) + sound)]


def face(left, right):
    speed = jnp.maximum(left[10], right[10])
    return [(left[5 + f] + right[5 + f]) - speed * (right[f] - left[f]) for f in range(5)]


def ahead(x, d):
    return roll(x, -1, 0) if d == 0 else roll(x, -PITCH if d == 1 else -1, 1)


def behind(x, d):
    return roll(x, 1, 0) if d == 0 else roll(x, PITCH if d == 1 else 1, 1)


def fine_net(u, beside, beyond):
    row = lax.broadcasted_iota(jnp.int32, (8, LANES), 0)
    prims, prims_beside = [primitive(v) for v in u], [primitive(v) for v in beside]
    total, total_beside = [None] * 8, [None] * 4

    def add(totals, q, net):
        totals[q] = net if totals[q] is None else [s + n for s, n in zip(totals[q], net)]

    def minus(left, right):
        return [a - b for a, b in zip(left, right)]

    def either(flag, first, second):
        return [jnp.where(flag, a, b) for a, b in zip(first, second)]

    for q in range(4):
        low, high = cell_flux(u[q], prims[q], 0), cell_flux(u[q + 4], prims[q + 4], 0)
        near = cell_flux(beside[q], prims_beside[q], 0)
        middle = face(low, high)
        after = face(high, either(row == 7, near, moved_cell(u[q], prims[q], 0, lambda x: roll(x, -1, 0))))
        first = face(near, low)
        add(total, q, minus(middle, either(row == 0, first, [roll(x, 1, 0) for x in after])))
        add(total, q + 4, minus(after, middle))
        if beyond is not None:
            next_ = cell_flux(beyond[q], primitive(beyond[q]), 0)
            outer = face(either(row == 0, next_, near), either(row == 0, near, next_))
            add(total_beside, q, either(row == 0, minus(first, outer), minus(outer, after)))
    groups = [(u, prims, total, (0, 4))]
    if beyond is not None:
        groups.append((beside, prims_beside, total_beside, (0,)))
    for d in (1, 2):
        bit = 4 >> d
        for cells, prim, totals, starts in groups:
            for low in [start + q for start in starts for q in range(4) if not q & bit]:
                high = low | bit
                left, right = cell_flux(cells[low], prim[low], d), cell_flux(cells[high], prim[high], d)
                middle = face(left, right)
                after = face(right, moved_cell(cells[low], prim[low], d, lambda x: ahead(x, d)))
                add(totals, low, minus(middle, [behind(x, d) for x in after]))
                add(totals, high, minus(after, middle))
    return total, total_beside


def coarse_net(u, deep, pos):
    prim = primitive(u)
    prim_deep = None if deep is None else primitive(deep)
    total = None
    for d in range(3):
        cell = cell_flux(u, prim, d)
        right = [ahead(x, d) for x in cell]
        if deep is not None:
            outer = cell_flux(deep, prim_deep, d)
            last, first = pos[d] == 8, pos[d] == -1
            right = [jnp.where(last, o, r) for o, r in zip(outer, right)]
        after = face(cell, right)
        before = [behind(x, d) for x in after]
        if deep is not None:
            before = [jnp.where(first, o, b) for o, b in zip(face(outer, cell), before)]
        net = [a - b for a, b in zip(after, before)]
        total = net if total is None else [s + n for s, n in zip(total, net)]
    return total


def put_faces(send_ref, slot, upper_far, faces):
    for side, blocks in enumerate(faces):
        first = pl.multiple_of((upper_far if side == 0 else 1 - upper_far) * 32, 8)
        for block in range(3):
            send_ref[slot, pl.ds(first + block * 8, 8), :] = blocks[block]
    near, far = swapped(upper_far == 1, faces[0][3], faces[1][3])
    send_ref[slot, 24:32, :] = jnp.concatenate([near[:4], far[:4]], axis=0)


def is_deep(n):
    return DEEP <= n < COVER


def fine_index(f, a, b, c):
    return f * 8 + a * 4 + b * 2 + c


def y_order(near):
    rest = [fine_index(f, a, 1 - near, c) for f in range(5) for a in range(2) for c in range(2)]
    first = [fine_index(f, 1, near, c) for c in range(2) for f in range(5)]
    second = [fine_index(f, 0, near, c) for c in range(2) for f in range(5)]
    return (
        first + [COARSE + f for f in range(5)] + rest[:1],
        second + [DEEP + f for f in range(5)] + [COVER],
        rest[1:17],
        rest[17:],
    )


def z_order(near):
    rest = [fine_index(f, a, b, 1 - near) for f in range(5) for a in range(2) for b in range(2)]
    first = [fine_index(f, 1, b, near) for b in range(2) for f in range(5)]
    second = [fine_index(f, 0, b, near) for b in range(2) for f in range(5)]
    return (
        (first, [COARSE + f for f in range(5)]),
        (second, [DEEP + f for f in range(5)]),
        (rest[:10], [COVER] + rest[10:14]),
        (rest[14:19], rest[19:]),
    )


def block_transpose(value):
    row = lax.broadcasted_iota(jnp.int32, (8, LANES), 0)
    group = lax.broadcasted_iota(jnp.int32, (8, LANES), 1) >> 4
    out = value
    for step in range(1, 8):
        moved = roll(roll(value, -16 * step, 1), step, 0)
        out = jnp.where(((row - group) & 7) == step, moved, out)
    return out


def swapped(flag, first, second):
    return jnp.where(flag, second, first), jnp.where(flag, first, second)


def whereabouts():
    device = lax.axis_index("boxes")
    own = [((device >> (3 * level)) & 7) ^ lead for level, lead in enumerate(LEAD)]
    first = [(device >> d) & 1 for d in range(3)]
    second = [(device >> (3 + d)) & 1 for d in range(3)]
    return own, first, [a == b for a, b in zip(first, second)]


def fine_matrix():
    row = lax.broadcasted_iota(jnp.int32, (256, LANES), 0)
    lane = lax.broadcasted_iota(jnp.int32, (256, LANES), 1)
    y = ((row >> 7) << 2) + ((row >> 4) & 3)
    z = (((row >> 6) & 1) << 2) + ((row >> 1) & 3)
    hit = lane == y * PITCH + z
    parity = ((row >> 2) & 2) + (row & 1)
    return [jnp.where(hit & (parity == q), 1.0, 0.0).astype(jnp.bfloat16) for q in range(4)]


def coarse_matrices():
    row = lax.broadcasted_iota(jnp.int32, (LANES, LANES), 0)
    lane = lax.broadcasted_iota(jnp.int32, (LANES, LANES), 1)
    spread = (row < 64) & (lane == (row >> 3) * PITCH + (row & 7))
    dense = (lane < 64) & (row == (lane >> 3) * PITCH + (lane & 7))
    return [jnp.where(hit, 1.0, 0.0).astype(jnp.bfloat16) for hit in (spread, dense)]


def matrices(place_ref, spread_ref, dense_ref):
    for q, part in enumerate(fine_matrix()):
        place_ref[:, q * LANES : (q + 1) * LANES] = part
    spread_ref[...], dense_ref[...] = coarse_matrices()


def prepare(
    refined_ref, coarse_ref, fine_ref, place_ref, spread_ref, dense_ref, inner_ref, send_ref, scr, scr_c, scr_x
):
    places, far, _ = whereabouts()
    own = places[0]
    lane, x, y, z = positions(8)
    row = lax.broadcasted_iota(jnp.int32, (8, LANES), 0)
    left_half = lane < 64
    for f in range(5):
        for q in range(4):
            tile = fine_ref[f, :, q * 128 : q * 128 + 128]
            for ox in range(2):
                scr[f, pl.ds(ox * 4 + q, 4, stride=8), :] = tile[ox * 4 : ox * 4 + 4]
            part = coarse_ref[f, :, q * 128 : q * 128 + 128]
            scr_c[f, 2 * q : 2 * q + 1, :] = part
            scr_c[f, 2 * q + 1 : 2 * q + 2, :] = part
    sides = [[], []]
    rows = []
    for f in range(5):
        tile = [scr[f, c * 8 : c * 8 + 8, :] for c in range(4)]
        sides[0].append(
            jnp.concatenate([jnp.where(left_half, tile[2 * h], roll(tile[2 * h + 1], 64, 1)) for h in range(2)], axis=1)
        )
        sides[1].append(
            jnp.concatenate([jnp.where(left_half, roll(tile[2 * h], 64, 1), tile[2 * h + 1]) for h in range(2)], axis=1)
        )
        value = scr_c[f]
        rows.append(jnp.where((row & 1) == 1, roll(value, 64, 1), value))
    fine = place(jnp.concatenate(sides[0] + sides[1], axis=0), place_ref[...])
    coarse = place(jnp.concatenate(rows, axis=0), spread_ref[...])
    coarse = [coarse[f * 8 : f * 8 + 8] for f in range(5)]

    covered = jnp.zeros((8, LANES), jnp.float32)
    for o in range(8):
        here = ((x >= 4) == (o >= 4)) & ((y >= 4) == (o % 4 >= 2)) & ((z >= 4) == (o % 2 == 1))
        flag = jnp.broadcast_to(refined_ref[:, o : o + 1], (8, LANES))
        covered = jnp.where(here & (flag > 0), 1.0, covered)
    state = []
    for f in range(5):
        for q in range(8):
            first = (q // 4 * 5 + f) * 8
            part = fine[first : first + 8, q % 4 * 128 : q % 4 * 128 + 128]
            state.append(jnp.where(covered > 0.5, part, coarse[f]))
    state += coarse
    fastest = None
    for u in [[state[f * 8 + q] for f in range(5)] for q in range(8)] + [coarse]:
        v, pressure, sound = primitive(u)
        speed = jnp.abs(v[0]) + jnp.abs(v[1]) + jnp.abs(v[2]) + 3.0 * sound
        fastest = speed if fastest is None else jnp.maximum(fastest, speed)
    fastest = jnp.where(inside(y) & inside(z), fastest, 0.0)
    fastest = jnp.broadcast_to(jnp.max(fastest), (8, LANES))

    zero = jnp.zeros((8, LANES), jnp.float32)
    stored = state + [zero] * 5 + [covered]
    for n in range(COUNT):
        inner_ref[n] = stored[n]

    for t in range(8):
        send_ref[t, FACE - 1 : FACE, :] = fastest[:1]

    def taken(n, at, deep_at):
        return (stored[n - 5], deep_at) if is_deep(n) else (stored[n], at)

    for side, at, deep_at in ((0, 7, 6), (1, 0, 1)):
        for n in range(COUNT):
            value, where = taken(n, at, deep_at)
            target = side * 64 + (n if n < PAIRED else n - PAIRED + 32)
            scr_x[target : target + 1, :] = value[where : where + 1, :]
    dense = place(scr_x[...], dense_ref[...])
    left4 = lax.broadcasted_iota(jnp.int32, (32, LANES), 1) < 64
    row32 = lax.broadcasted_iota(jnp.int32, (32, LANES), 0)
    faces_x, faces_y, faces_z = [], [], []
    for side in range(2):
        packed = jnp.where(left4, dense[side * 64 : side * 64 + 32], roll(dense[side * 64 + 32 : side * 64 + 64], 64, 1))
        packed = jnp.where(row32 >= PAIRED, jnp.concatenate([fastest] * 4, axis=0), packed)
        faces_x.append([packed[block * 8 : block * 8 + 8] for block in range(4)])
    put_faces(send_ref, own ^ 1, far[0], faces_x)

    slots = lane - ((lane * 205) >> 11) * PITCH
    corners_xy, corners_xz, corners = [], [], zero
    for side, at, deep_at in ((0, 7, 6), (1, 0, 1)):
        near = 1 - side
        order = y_order(near)
        blocks = []
        for names in order:
            packed = fastest
            for s, n in enumerate(names):
                value, where = taken(n, at, deep_at)
                packed = jnp.where((lane >> 3) == s, roll(value, s * 8 - where * PITCH, 1), packed)
            blocks.append(packed)
        width = len(order[3]) * 8
        second = (lane >= width) & (lane < 2 * width)
        blocks[3] = jnp.where(second, roll(roll(blocks[3], width, 1), 4, 0), blocks[3])
        faces_y.append(blocks)
        corners_xy.append((blocks[0][7:8], jnp.where(lane < 80, blocks[1], blocks[0])[0:1]))

        blocks = []
        for block, (names, halves) in enumerate(z_order(near)):
            packed = fastest
            for s, n in enumerate(names):
                value, where = taken(n, at, deep_at)
                packed = jnp.where((slots == s) & (lane < 80), roll(value, s - where, 1), packed)
            if block < 3:
                extra = fastest
                for s, n in enumerate(halves):
                    value, where = taken(n, at, deep_at)
                    extra = jnp.where(slots == s, roll(value, s - where, 1), extra)
                extra = jnp.where(slots < 5, roll(extra, 80, 1), roll(extra, 45, 1))
                packed = jnp.where((lane >= 80) & (lane < MAX_LANE), extra, packed)
            else:
                second = (slots >= 5) & (lane < 80)
                packed = jnp.where(second, roll(roll(packed, 5, 1), 4, 0), packed)
                value = stored[halves[0]]
                lower = roll(value, 4, 0)
                pieces = [roll(value, 80 - at, 1), roll(value, 41 - at, 1), roll(lower, 82 - at, 1), roll(lower, 43 - at, 1)]
                for s, piece in enumerate(pieces):
                    packed = jnp.where((slots == s) & (lane >= 80) & (lane < MAX_LANE), piece, packed)
            blocks.append(packed)
        faces_z.append(blocks)
        corners_xz.append((blocks[0][7:8], jnp.where(lane < 80, blocks[1], blocks[0])[0:1]))
        for end, first, first_coarse in ((0, 75, 115), (1, 0, 80)):
            to = (side * 2 + end) * 16
            for start, source, i in ((first, blocks[0], 0), (first, blocks[1], 5), (first_coarse, blocks[0], 10)):
                here = (lane >= to + i) & (lane < to + i + 5)
                corners = jnp.where(here, roll(source, to + i - start, 1), corners)
    put_faces(send_ref, own ^ 2, far[1], faces_y)
    put_faces(send_ref, own ^ 4, far[2], faces_z)
    corners = block_transpose(corners)

    edges = [
        [[corners_xy[e][d] for e in range(2)] for d in range(2)],
        [[corners_xz[e][d] for e in range(2)] for d in range(2)],
        [[corners[e * 2 + d : e * 2 + d + 1] for e in range(2)] for d in range(2)],
    ]
    for (d, e), edge in zip(PAIRS, edges):
        upper, lower = [swapped(far[e] == 1, *half) for half in edge]
        near_near, far_near = swapped(far[d] == 1, upper[0], lower[0])
        near_far, far_far = swapped(far[d] == 1, upper[1], lower[1])
        for r, value in enumerate((near_near, near_far, far_near, far_far)):
            send_ref[own ^ pair(d, e), r : r + 1, :] = value


def others(d):
    return [e for e in range(3) if e != d]


def pair(d, e):
    return (1 << d) ^ (1 << e)


def running_maximum(rows):
    fastest = functools.reduce(jnp.maximum, rows)
    lane = lax.broadcasted_iota(jnp.int32, fastest.shape, 1)
    fastest = jnp.where(lane >= MAX_LANE, fastest, 0.0)
    return jnp.broadcast_to(jnp.max(fastest), (1, LANES))


def pass_on(send_ref, own, fastest, faces, edges, corners):
    lane = lax.broadcasted_iota(jnp.int32, (1, LANES), 1)
    for t in range(8):
        send_ref[t, FACE - 1 : FACE, :] = fastest
    for d in range(3):
        slot = own ^ (1 << d)
        send_ref[slot, :FACE, :] = faces[d]
        send_ref[slot, FACE - 1 : FACE, :] = jnp.where(lane >= MAX_LANE, fastest, faces[d][FACE - 1 : FACE])
        for r, value in enumerate(edges[d]):
            send_ref[slot, FACE + r : FACE + r + 1, :] = value
    for (d, e), value in zip(PAIRS, corners):
        send_ref[own ^ pair(d, e), 0:1, :] = value


def carry_once(got_ref, send_ref):
    own, to, _ = whereabouts()[0]
    fastest = running_maximum([got_ref[t, FACE - 1 : FACE, :] for t in range(8)])
    faces = [
        jnp.concatenate([got_ref[own ^ (1 << d), 32:, :], got_ref[own ^ (1 << d), FACE:32, :]], axis=0)
        for d in range(3)
    ]

    def edge(d, e, r):
        return got_ref[own ^ pair(d, e), r : r + 1, :]

    edges = [[edge(d, e, 1 if e < d else 2) for e in others(d)] for d in range(3)]
    pass_on(send_ref, to, fastest, faces, edges, [edge(d, e, 3) for d, e in PAIRS])


def carry_twice(got_ref, send_ref):
    _, own, to = whereabouts()[0]
    fastest = running_maximum([got_ref[t, FACE - 1 : FACE, :] for t in range(8)])
    faces = [got_ref[own ^ (1 << d), :FACE, :] for d in range(3)]

    def far_far(d, e):
        return got_ref[own ^ pair(d, e), 0:1, :]

    edges = []
    for d in range(3):
        passed = [got_ref[own ^ (1 << d), FACE + r : FACE + r + 1, :] for r in range(2)]
        edges.append(passed + [far_far(d, e) for e in others(d)])
    pass_on(send_ref, to, fastest, faces, edges, [far_far(d, e) for d, e in PAIRS])


def arrived(got0, got1, got2):
    own, first, twice = whereabouts()
    upper_far = [bit == 1 for bit in first]
    faces = []
    for d in range(3):
        near = got0[own[0] ^ (1 << d), :ROWS]
        far = jnp.where(twice[d], got2[own[2] ^ (1 << d)], got1[own[1] ^ (1 << d)])
        faces.append(swapped(upper_far[d], near, far))

    def once(d, r):
        return got1[own[1] ^ (1 << d), FACE + r : FACE + r + 1, :]

    def again(d, r):
        return got2[own[2] ^ (1 << d), FACE + r : FACE + r + 1, :]

    edges = []
    for d, e in PAIRS:
        of_e, of_d = others(d).index(e), others(e).index(d)
        near_near = got0[own[0] ^ pair(d, e), 0:1, :]
        near_far = jnp.where(twice[e], again(e, of_d), once(e, of_d))
        far_near = jnp.where(twice[d], again(d, of_e), once(d, of_e))
        both = jnp.where(twice[e], got2[own[2] ^ pair(d, e), 0:1, :], again(d, 2 + of_e))
        neither = jnp.where(twice[e], again(e, 2 + of_d), got1[own[1] ^ pair(d, e), 0:1, :])
        far_far = jnp.where(twice[d], both, neither)
        near, far = [swapped(upper_far[e], *half) for half in ((near_near, near_far), (far_near, far_far))]
        above, below = zip(*[swapped(upper_far[d], n, f) for n, f in zip(near, far)])
        edges.append((above, below))
    return faces, edges


def surround(faces, edges, inner_ref, spread, scr_x):
    lane, x, y, z = positions(8)
    row = lax.broadcasted_iota(jnp.int32, (8, LANES), 0)
    left4 = lax.broadcasted_iota(jnp.int32, (32, LANES), 1) < 64
    inner = [inner_ref[n] for n in range(COUNT)]
    rows = []
    for side in range(2):
        value = faces[0][side]
        rows += [jnp.where(left4, value, 0.0), jnp.where(left4, roll(value, 64, 1), 0.0)]
    scr_x[...] = place(jnp.concatenate(rows, axis=0), spread)

    def around(n, above_n=None, upper_row=7):
        above_n = n if above_n is None else above_n
        places = [m if m < PAIRED else m - PAIRED + 32 for m in (above_n, n)]
        above = jnp.broadcast_to(scr_x[places[0] : places[0] + 1, :], (8, LANES))
        below = jnp.broadcast_to(scr_x[places[1] + 64 : places[1] + 65, :], (8, LANES))
        return jnp.where(row == upper_row, above, below)

    beside = [[around(f * 8 + 4 + q, f * 8 + q) for f in range(5)] for q in range(4)]
    beyond = [[around(f * 8 + q, f * 8 + 4 + q) for f in range(5)] for q in range(4)]
    covered = around(COVER)
    coarse_outer = [around(n, upper_row=0) for n in range(COARSE, COVER)]

    def put_beside(n, mask, value):
        f, q = n // 8, n % 4
        beside[q][f] = jnp.where(mask, value, beside[q][f])

    def put_coarse(f, mask, value):
        coarse_outer[f] = jnp.where(mask, value, coarse_outer[f])


    def doubled(value):
        return jnp.concatenate([value[24:28], value[24:28]], axis=0)

    for side, (near, at) in enumerate(SIDES):
        blocks = [faces[1][side][block * 8 : block * 8 + 8] for block in range(3)]
        order = y_order(near)
        first = at * PITCH % LANES
        here = (lane >= first) & (lane < first + 8)
        for block, names in zip(blocks, order):
            for s, n in enumerate(names):
                inner[n] = jnp.where(here, roll(block, first - s * 8, 1), inner[n])
        last = doubled(faces[1][side])
        for s, n in enumerate(order[3]):
            value = jnp.where(row < 4, roll(last, first - s * 8, 1), roll(last, first - (s + len(order[3])) * 8, 1))
            inner[n] = jnp.where(here, value, inner[n])
        above, below = [jnp.broadcast_to(edges[0][end][side], (8, LANES)) for end in range(2)]
        edge, coarse_edge = jnp.where(row == 7, above, below), jnp.where(row == 0, above, below)
        for s in range(10):
            put_beside(order[0][s], here, roll(edge, first - s * 8, 1))
        for s in range(10, 15):
            put_coarse(s - 10, here, roll(coarse_edge, first - s * 8, 1))

    columns = jnp.concatenate([edges[2][end][side] for side in range(2) for end in range(2)] * 2, axis=0)
    columns = block_transpose(columns)
    for side, (near, at) in enumerate(SIDES):
        blocks = [faces[2][side][block * 8 : block * 8 + 8] for block in range(3)]
        order = z_order(near)
        here = (z == at) & (y < 9)
        low_y = y < 4
        above, below = side * 32, side * 32 + 16

        def joined(block):
            return jnp.where(lane < 40, roll(block, -80, 1), roll(block, -45, 1))

        def ended(block, i, below_lane):
            block = jnp.where(lane < 80, block, roll(columns, 80 - above - i, 1))
            return jnp.where(lane >= below_lane, roll(columns, below_lane - below - i, 1), block)

        mains = [ended(blocks[0], 0, 123), ended(blocks[1], 5, 123), blocks[2]]
        halves = [ended(joined(blocks[0]), 10, 118), joined(blocks[1]), joined(blocks[2])]
        for block in range(3):
            for source, names in ((mains[block], order[block][0]), (halves[block], order[block][1])):
                for s, n in enumerate(names):
                    inner[n] = jnp.where(here, roll(source, at - s, 1), inner[n])
        last = doubled(faces[2][side])
        for s, n in enumerate(order[3][0]):
            value = jnp.where(row < 4, roll(last, at - s, 1), roll(last, at - 5 - s, 1))
            inner[n] = jnp.where(here, value, inner[n])
        upper_rows = jnp.where(low_y, roll(last, at - 80, 1), roll(last, at - 41, 1))
        lower_rows = jnp.where(low_y, roll(last, at - 82, 1), roll(last, at - 43, 1))
        n = order[3][1][0]
        inner[n] = jnp.where(here, jnp.where(row < 4, upper_rows, lower_rows), inner[n])

        above, below = [jnp.broadcast_to(edges[1][end][side], (8, LANES)) for end in range(2)]
        edge, coarse_edge = jnp.where(row == 7, above, below), joined(jnp.where(row == 0, above, below))
        for s in range(10):
            put_beside(order[0][0][s], here & inside(y), roll(edge, at - s, 1))
        for s in range(5):
            put_coarse(s, here & inside(y), roll(coarse_edge, at - s, 1))
    fine = [[inner[f * 8 + q] for f in range(5)] for q in range(8)]
    coarse = [jnp.concatenate([i, o], axis=0) for i, o in zip(inner[COARSE:COVER], coarse_outer)]
    return fine, beside, beyond, coarse[:5], coarse[5:], inner[COVER] > 0.5, covered > 0.5


def advance(got0, got1, got2, inner_ref, back_ref, spread_ref, dense_ref, coarse_out, fine_out, scr, scr_x):
    lane, x, y, z = positions(16)
    fastest = running_maximum([got2[t, FACE - 1 : FACE, :] for t in range(8)])
    half16 = 0.5 * (courant / jnp.broadcast_to(fastest, (16, LANES)))
    half = half16[:8]
    faces, edges = arrived(got0, got1, got2)
    fine0, beside, beyond, coarse0, deep, covered, covered_beside = surround(
        faces, edges, inner_ref, spread_ref[...], scr_x
    )
    row = lax.broadcasted_iota(jnp.int32, (8, LANES), 0)

    net = coarse_net(coarse0, deep, (x, y, z))
    coarse1 = [u - 0.5 * half16 * n for u, n in zip(coarse0, net)]
    net, net_beside = fine_net(fine0, beside, beyond)

    def first_section(u, net, covered, coarse):
        return [jnp.where(covered, a - half * n, c) for a, n, c in zip(u, net, coarse)]

    coarse_beside = [jnp.where(row == 7, roll(c[8:], 7, 0), roll(c[8:], 1, 0)) for c in coarse1]
    fine1 = [first_section(fine0[q], net[q], covered, [c[:8] for c in coarse1]) for q in range(8)]
    beside1 = [first_section(beside[q], net_beside[q], covered_beside, coarse_beside) for q in range(4)]
    net = coarse_net(coarse1, None, None)
    coarse2 = [0.5 * c0[:8] + 0.5 * (c1[:8] - 0.5 * half * n[:8]) for c0, c1, n in zip(coarse0, coarse1, net)]
    net, _ = fine_net(fine1, beside1, None)
    mine = inside(y[:8]) & inside(z[:8])
    refined = mine & covered
    fine2 = [
        [
            jnp.where(refined, 0.5 * fine0[q][f] + 0.5 * (fine1[q][f] - half * net[q][f]), 0.0)
            for f in range(5)
        ]
        for q in range(8)
    ]
    coarse = []
    for f in range(5):
        total = functools.reduce(jnp.add, [fine2[q][f] for q in range(8)])
        coarse.append(jnp.where(mine, jnp.where(refined, 0.125 * total, coarse2[f]), 0.0))

    left_half = lane[:8] < 64
    rows = [jnp.concatenate([fine2[a * 4 + q][f] for q in range(4)], axis=1) for a in range(2) for f in range(5)]
    back = place(jnp.concatenate(rows, axis=0), back_ref[...])
    for f in range(5):
        for h in range(2):
            even = back[f * 8 : f * 8 + 8, h * 128 : h * 128 + 128]
            odd = back[40 + f * 8 : 48 + f * 8, h * 128 : h * 128 + 128]
            scr[f, h * 16 : h * 16 + 8, :] = jnp.where(left_half, even, roll(odd, 64, 1))
            scr[f, h * 16 + 8 : h * 16 + 16, :] = jnp.where(left_half, roll(even, 64, 1), odd)
        for q in range(4):
            for ox in range(2):
                tile = scr[f, pl.ds(ox * 4 + q, 4, stride=8), :]
                fine_out[f, ox * 4 : ox * 4 + 4, q * 128 : q * 128 + 128] = tile
    back = place(jnp.concatenate(coarse, axis=0), dense_ref[...])
    for f in range(5):
        value = back[f * 8 : f * 8 + 8]
        value = jnp.where(left_half, value, roll(roll(value, 64, 1), -1, 0))
        for q in range(4):
            coarse_out[f, :, q * 128 : q * 128 + 128] = value[2 * q : 2 * q + 1]


def shape(*dims):
    return jax.ShapeDtypeStruct(dims, jnp.float32)


def call(kernel, outs, scratch, args, cost=None):
    return pl.pallas_call(
        kernel,
        out_shape=outs,
        in_specs=[pl.BlockSpec(memory_space=pltpu.VMEM)] * len(args),
        out_specs=[pl.BlockSpec(memory_space=pltpu.VMEM)] * len(outs),
        scratch_shapes=scratch,
        cost_estimate=cost,
        compiler_params=pltpu.CompilerParams(vmem_limit_bytes=32 * 1024 * 1024),
    )(*args)


def swap(block, level):
    count = lax.axis_size("boxes")
    low = 3 * level
    first = [device for device in range(count) if not (device >> low) & 7]
    groups = [[device | (slot ^ LEAD[level]) << low for slot in range(8)] for device in first]
    return lax.all_to_all(block, "boxes", 0, 0, axis_index_groups=groups)


def local(coarse_state, fine_state, refined):
    back = jnp.asarray(back_matrix().astype(ml_dtypes.bfloat16))
    fields = lambda *dims: pltpu.VMEM(dims, jnp.float32)
    matrix = lambda *dims: jax.ShapeDtypeStruct(dims, jnp.bfloat16)
    made = call(matrices, [matrix(256, 4 * LANES), matrix(LANES, LANES), matrix(LANES, LANES)], [], (), pl.CostEstimate(flops=50000000, bytes_accessed=327680, transcendentals=0))
    inner, send = call(
        prepare,
        [shape(COUNT, 8, LANES), shape(8, 2 * FACE, LANES)],
        [fields(5, 40, LANES), fields(5, 8, LANES), fields(128, LANES)],
        (refined, jnp.swapaxes(coarse_state, 0, 1), jnp.swapaxes(fine_state[0], 0, 1), *made),
    )
    got0 = swap(send, 0)
    got1 = swap(call(carry_once, [shape(8, ROWS, LANES)], [], (got0,))[0], 1)
    got2 = swap(call(carry_twice, [shape(8, ROWS, LANES)], [], (got1,))[0], 2)
    coarse_out, fine_out = call(
        advance,
        [shape(5, 1, 512), shape(5, 8, 512)],
        [fields(5, 40, LANES), fields(128, LANES)],
        (got0, got1, got2, inner, back, *made[1:]),
    )
    return jnp.swapaxes(coarse_out, 0, 1), jnp.swapaxes(fine_out, 0, 1)[None]


def solution(mesh):
    in_specs = (P("boxes", None, None), P("boxes", None, None, None), P("boxes", None))
    out_specs = (P("boxes", None, None), P("boxes", None, None, None))
    return jax.shard_map(local, mesh=mesh, in_specs=in_specs, out_specs=out_specs, check_vma=False)
```

```python
import functools

import jax
import jax.numpy as jnp
import ml_dtypes
import numpy as np
from jax import lax
from jax.experimental import pallas as pl
from jax.experimental.pallas import tpu as pltpu
from jax.sharding import PartitionSpec as P

PITCH = 10
LANES = 128
FINE = 40
COARSE = FINE
DEEP = COARSE + 5
COVER = DEEP + 5
COUNT = COVER + 1
FACE = 28
ROWS = 32
MAX_LANE = 120
PAIRED = 26
LEAD = (5, 6, 4)
SIDES = ((0, 8), (1, -1))
PAIRS = ((0, 1), (0, 2), (1, 2))
gamma_gas = 1.4
courant = 0.4


def back_matrix():
    back = np.zeros((512, 256), np.float32)
    for y in range(16):
        for z in range(16):
            row = (y // 8 * 2 + z // 8) * 64 + y % 8 * 8 + z % 8
            back[(y % 2 * 2 + z % 2) * 128 + y // 2 * PITCH + z // 2, row] = 1
    return back


def place(values, matrix):
    high = values.astype(jnp.bfloat16)
    rest = values - high.astype(jnp.float32)
    middle = rest.astype(jnp.bfloat16)
    low = (rest - middle.astype(jnp.float32)).astype(jnp.bfloat16)
    rows = values.shape[0]
    parts = jnp.concatenate([high, middle, low], axis=0)
    out = jnp.dot(parts, matrix, preferred_element_type=jnp.float32)
    return out[:rows] + out[rows : 2 * rows] + out[2 * rows :]


def roll(x, shift, axis):
    shift = shift % x.shape[axis]
    return pltpu.roll(x, shift, axis) if shift else x


def positions(rows):
    row = lax.broadcasted_iota(jnp.int32, (rows, LANES), 0)
    lane = lax.broadcasted_iota(jnp.int32, (rows, LANES), 1)
    x = jnp.where(row > 8, row - 16, row)
    along = (lane + PITCH + 1) & (LANES - 1)
    y1 = (along * 205) >> 11
    return lane, x, y1 - 1, along - y1 * PITCH - 1


def inside(pos):
    return (pos >= 0) & (pos < 8)


def primitive(u):
    inverse = 1.0 / u[0]
    v = [u[1 + d] * inverse for d in range(3)]
    pressure = 0.4 * (u[4] - 0.5 * (u[1] * v[0] + u[2] * v[1] + u[3] * v[2]))
    sound = jnp.sqrt(gamma_gas * pressure * inverse)
    return v, pressure, sound


def cell_flux(u, prim, d):
    v, pressure, sound = prim
    flux = [u[1 + d]] + [u[1 + e] * v[d] for e in range(3)] + [(u[4] + pressure) * v[d]]
    flux[1 + d] = flux[1 + d] + pressure
    return list(u) + flux + [jnp.abs(v[d]) + sound]


def moved_cell(u, prim, d, shift):
    v, pressure, sound = prim
    u, v_d = [shift(f) for f in u], shift(v[d])
    pressure = shift(pressure)
    flux = [u[1 + d]] + [u[1 + e] * v_d for e in range(3)] + [(u[4] + pressure) * v_d]
    flux[1 + d] = flux[1 + d] + pressure
    return u + flux + [shift(jnp.abs(v[d]) + sound)]


def face(left, right):
    speed = jnp.maximum(left[10], right[10])
    return [(left[5 + f] + right[5 + f]) - speed * (right[f] - left[f]) for f in range(5)]


def ahead(x, d):
    return roll(x, -1, 0) if d == 0 else roll(x, -PITCH if d == 1 else -1, 1)


def behind(x, d):
    return roll(x, 1, 0) if d == 0 else roll(x, PITCH if d == 1 else 1, 1)


def fine_net(u, beside, beyond):
    row = lax.broadcasted_iota(jnp.int32, (8, LANES), 0)
    prims, prims_beside = [primitive(v) for v in u], [primitive(v) for v in beside]
    total, total_beside = [None] * 8, [None] * 4

    def add(totals, q, net):
        totals[q] = net if totals[q] is None else [s + n for s, n in zip(totals[q], net)]

    def minus(left, right):
        return [a - b for a, b in zip(left, right)]

    def either(flag, first, second):
        return [jnp.where(flag, a, b) for a, b in zip(first, second)]

    for q in range(4):
        low, high = cell_flux(u[q], prims[q], 0), cell_flux(u[q + 4], prims[q + 4], 0)
        near = cell_flux(beside[q], prims_beside[q], 0)
        middle = face(low, high)
        after = face(high, either(row == 7, near, moved_cell(u[q], prims[q], 0, lambda x: roll(x, -1, 0))))
        first = face(near, low)
        add(total, q, minus(middle, either(row == 0, first, [roll(x, 1, 0) for x in after])))
        add(total, q + 4, minus(after, middle))
        if beyond is not None:
            next_ = cell_flux(beyond[q], primitive(beyond[q]), 0)
            outer = face(either(row == 0, next_, near), either(row == 0, near, next_))
            add(total_beside, q, either(row == 0, minus(first, outer), minus(outer, after)))
    groups = [(u, prims, total, (0, 4))]
    if beyond is not None:
        groups.append((beside, prims_beside, total_beside, (0,)))
    for d in (1, 2):
        bit = 4 >> d
        for cells, prim, totals, starts in groups:
            for low in [start + q for start in starts for q in range(4) if not q & bit]:
                high = low | bit
                left, right = cell_flux(cells[low], prim[low], d), cell_flux(cells[high], prim[high], d)
                middle = face(left, right)
                after = face(right, moved_cell(cells[low], prim[low], d, lambda x: ahead(x, d)))
                add(totals, low, minus(middle, [behind(x, d) for x in after]))
                add(totals, high, minus(after, middle))
    return total, total_beside


def coarse_net(u, deep, pos, inner=False):
    prim = primitive(u)
    prim_deep = None if deep is None else primitive(deep)
    total = None
    for d in range(3):
        if inner and d == 1:
            u, prim = [x[:8] for x in u], ([x[:8] for x in prim[0]], prim[1][:8], prim[2][:8])
            total = [x[:8] for x in total]
        cell = cell_flux(u, prim, d)
        right = [ahead(x, d) for x in cell]
        if deep is not None:
            outer = cell_flux(deep, prim_deep, d)
            last, first = pos[d] == 8, pos[d] == -1
            right = [jnp.where(last, o, r) for o, r in zip(outer, right)]
        after = face(cell, right)
        before = [behind(x, d) for x in after]
        if deep is not None:
            before = [jnp.where(first, o, b) for o, b in zip(face(outer, cell), before)]
        net = [a - b for a, b in zip(after, before)]
        total = net if total is None else [s + n for s, n in zip(total, net)]
    return total


def put_faces(send_ref, slot, upper_far, faces):
    for side, blocks in enumerate(faces):
        first = pl.multiple_of((upper_far if side == 0 else 1 - upper_far) * 32, 8)
        for block in range(3):
            send_ref[slot, pl.ds(first + block * 8, 8), :] = blocks[block]
    near, far = swapped(upper_far == 1, faces[0][3], faces[1][3])
    send_ref[slot, 24:32, :] = jnp.concatenate([near[:4], far[:4]], axis=0)


def is_deep(n):
    return DEEP <= n < COVER


def fine_index(f, a, b, c):
    return f * 8 + a * 4 + b * 2 + c


def y_order(near):
    rest = [fine_index(f, a, 1 - near, c) for f in range(5) for a in range(2) for c in range(2)]
    first = [fine_index(f, 1, near, c) for c in range(2) for f in range(5)]
    second = [fine_index(f, 0, near, c) for c in range(2) for f in range(5)]
    return (
        first + [COARSE + f for f in range(5)] + rest[:1],
        second + [DEEP + f for f in range(5)] + [COVER],
        rest[1:17],
        rest[17:],
    )


def z_order(near):
    rest = [fine_index(f, a, b, 1 - near) for f in range(5) for a in range(2) for b in range(2)]
    first = [fine_index(f, 1, b, near) for b in range(2) for f in range(5)]
    second = [fine_index(f, 0, b, near) for b in range(2) for f in range(5)]
    return (
        (first, [COARSE + f for f in range(5)]),
        (second, [DEEP + f for f in range(5)]),
        (rest[:10], [COVER] + rest[10:14]),
        (rest[14:19], rest[19:]),
    )


def block_transpose(value):
    row = lax.broadcasted_iota(jnp.int32, (8, LANES), 0)
    group = lax.broadcasted_iota(jnp.int32, (8, LANES), 1) >> 4
    out = value
    for step in range(1, 8):
        moved = roll(roll(value, -16 * step, 1), step, 0)
        out = jnp.where(((row - group) & 7) == step, moved, out)
    return out


def swapped(flag, first, second):
    return jnp.where(flag, second, first), jnp.where(flag, first, second)


def whereabouts():
    device = lax.axis_index("boxes")
    own = [((device >> (3 * level)) & 7) ^ lead for level, lead in enumerate(LEAD)]
    first = [(device >> d) & 1 for d in range(3)]
    second = [(device >> (3 + d)) & 1 for d in range(3)]
    return own, first, [a == b for a, b in zip(first, second)]


def fine_matrix():
    row = lax.broadcasted_iota(jnp.int32, (256, LANES), 0)
    lane = lax.broadcasted_iota(jnp.int32, (256, LANES), 1)
    y = ((row >> 7) << 2) + ((row >> 4) & 3)
    z = (((row >> 6) & 1) << 2) + ((row >> 1) & 3)
    hit = lane == y * PITCH + z
    parity = ((row >> 2) & 2) + (row & 1)
    return [jnp.where(hit & (parity == q), 1.0, 0.0).astype(jnp.bfloat16) for q in range(4)]


def coarse_matrices():
    row = lax.broadcasted_iota(jnp.int32, (LANES, LANES), 0)
    lane = lax.broadcasted_iota(jnp.int32, (LANES, LANES), 1)
    spread = (row < 64) & (lane == (row >> 3) * PITCH + (row & 7))
    dense = (lane < 64) & (row == (lane >> 3) * PITCH + (lane & 7))
    return [jnp.where(hit, 1.0, 0.0).astype(jnp.bfloat16) for hit in (spread, dense)]


def matrices(place_ref, spread_ref, dense_ref):
    for q, part in enumerate(fine_matrix()):
        place_ref[:, q * LANES : (q + 1) * LANES] = part
    spread_ref[...], dense_ref[...] = coarse_matrices()


def prepare(
    refined_ref, coarse_ref, fine_ref, place_ref, spread_ref, dense_ref, inner_ref, send_ref, scr, scr_c, scr_x
):
    places, far, _ = whereabouts()
    own = places[0]
    lane, x, y, z = positions(8)
    row = lax.broadcasted_iota(jnp.int32, (8, LANES), 0)
    left_half = lane < 64
    for f in range(5):
        for q in range(4):
            tile = fine_ref[f, :, q * 128 : q * 128 + 128]
            for ox in range(2):
                scr[f, pl.ds(ox * 4 + q, 4, stride=8), :] = tile[ox * 4 : ox * 4 + 4]
            part = coarse_ref[f, :, q * 128 : q * 128 + 128]
            scr_c[f, 2 * q : 2 * q + 1, :] = part
            scr_c[f, 2 * q + 1 : 2 * q + 2, :] = part
    sides = [[], []]
    rows = []
    for f in range(5):
        tile = [scr[f, c * 8 : c * 8 + 8, :] for c in range(4)]
        sides[0].append(
            jnp.concatenate([jnp.where(left_half, tile[2 * h], roll(tile[2 * h + 1], 64, 1)) for h in range(2)], axis=1)
        )
        sides[1].append(
            jnp.concatenate([jnp.where(left_half, roll(tile[2 * h], 64, 1), tile[2 * h + 1]) for h in range(2)], axis=1)
        )
        value = scr_c[f]
        rows.append(jnp.where((row & 1) == 1, roll(value, 64, 1), value))
    fine = place(jnp.concatenate(sides[0] + sides[1], axis=0), place_ref[...])
    coarse = place(jnp.concatenate(rows, axis=0), spread_ref[...])
    coarse = [coarse[f * 8 : f * 8 + 8] for f in range(5)]

    covered = jnp.zeros((8, LANES), jnp.float32)
    for o in range(8):
        here = ((x >= 4) == (o >= 4)) & ((y >= 4) == (o % 4 >= 2)) & ((z >= 4) == (o % 2 == 1))
        flag = jnp.broadcast_to(refined_ref[:, o : o + 1], (8, LANES))
        covered = jnp.where(here & (flag > 0), 1.0, covered)
    state = []
    for f in range(5):
        for q in range(8):
            first = (q // 4 * 5 + f) * 8
            part = fine[first : first + 8, q % 4 * 128 : q % 4 * 128 + 128]
            state.append(jnp.where(covered > 0.5, part, coarse[f]))
    state += coarse
    fastest = None
    for u in [[state[f * 8 + q] for f in range(5)] for q in range(8)] + [coarse]:
        v, pressure, sound = primitive(u)
        speed = jnp.abs(v[0]) + jnp.abs(v[1]) + jnp.abs(v[2]) + 3.0 * sound
        fastest = speed if fastest is None else jnp.maximum(fastest, speed)
    fastest = jnp.where(inside(y) & inside(z), fastest, 0.0)
    fastest = jnp.broadcast_to(jnp.max(fastest), (8, LANES))

    zero = jnp.zeros((8, LANES), jnp.float32)
    stored = state + [zero] * 5 + [covered]
    for n in range(COUNT):
        inner_ref[n] = stored[n]

    for t in range(8):
        send_ref[t, FACE - 1 : FACE, :] = fastest[:1]

    def taken(n, at, deep_at):
        return (stored[n - 5], deep_at) if is_deep(n) else (stored[n], at)

    for side, at, deep_at in ((0, 7, 6), (1, 0, 1)):
        for n in range(COUNT):
            value, where = taken(n, at, deep_at)
            target = side * 64 + (n if n < PAIRED else n - PAIRED + 32)
            scr_x[target : target + 1, :] = value[where : where + 1, :]
    dense = place(scr_x[...], dense_ref[...])
    left4 = lax.broadcasted_iota(jnp.int32, (32, LANES), 1) < 64
    row32 = lax.broadcasted_iota(jnp.int32, (32, LANES), 0)
    faces_x, faces_y, faces_z = [], [], []
    for side in range(2):
        packed = jnp.where(left4, dense[side * 64 : side * 64 + 32], roll(dense[side * 64 + 32 : side * 64 + 64], 64, 1))
        packed = jnp.where(row32 >= PAIRED, jnp.concatenate([fastest] * 4, axis=0), packed)
        faces_x.append([packed[block * 8 : block * 8 + 8] for block in range(4)])
    put_faces(send_ref, own ^ 1, far[0], faces_x)

    slots = lane - ((lane * 205) >> 11) * PITCH
    corners_xy, corners_xz, corners = [], [], zero
    for side, at, deep_at in ((0, 7, 6), (1, 0, 1)):
        near = 1 - side
        order = y_order(near)
        blocks = []
        for names in order:
            packed = fastest
            for s, n in enumerate(names):
                value, where = taken(n, at, deep_at)
                packed = jnp.where((lane >> 3) == s, roll(value, s * 8 - where * PITCH, 1), packed)
            blocks.append(packed)
        width = len(order[3]) * 8
        second = (lane >= width) & (lane < 2 * width)
        blocks[3] = jnp.where(second, roll(roll(blocks[3], width, 1), 4, 0), blocks[3])
        faces_y.append(blocks)
        corners_xy.append((blocks[0][7:8], jnp.where(lane < 80, blocks[1], blocks[0])[0:1]))

        blocks = []
        for block, (names, halves) in enumerate(z_order(near)):
            packed = fastest
            for s, n in enumerate(names):
                value, where = taken(n, at, deep_at)
                packed = jnp.where((slots == s) & (lane < 80), roll(value, s - where, 1), packed)
            if block < 3:
                extra = fastest
                for s, n in enumerate(halves):
                    value, where = taken(n, at, deep_at)
                    extra = jnp.where(slots == s, roll(value, s - where, 1), extra)
                extra = jnp.where(slots < 5, roll(extra, 80, 1), roll(extra, 45, 1))
                packed = jnp.where((lane >= 80) & (lane < MAX_LANE), extra, packed)
            else:
                second = (slots >= 5) & (lane < 80)
                packed = jnp.where(second, roll(roll(packed, 5, 1), 4, 0), packed)
                value = stored[halves[0]]
                lower = roll(value, 4, 0)
                pieces = [roll(value, 80 - at, 1), roll(value, 41 - at, 1), roll(lower, 82 - at, 1), roll(lower, 43 - at, 1)]
                for s, piece in enumerate(pieces):
                    packed = jnp.where((slots == s) & (lane >= 80) & (lane < MAX_LANE), piece, packed)
            blocks.append(packed)
        faces_z.append(blocks)
        corners_xz.append((blocks[0][7:8], jnp.where(lane < 80, blocks[1], blocks[0])[0:1]))
        for end, first, first_coarse in ((0, 75, 115), (1, 0, 80)):
            to = (side * 2 + end) * 16
            for start, source, i in ((first, blocks[0], 0), (first, blocks[1], 5), (first_coarse, blocks[0], 10)):
                here = (lane >= to + i) & (lane < to + i + 5)
                corners = jnp.where(here, roll(source, to + i - start, 1), corners)
    put_faces(send_ref, own ^ 2, far[1], faces_y)
    put_faces(send_ref, own ^ 4, far[2], faces_z)
    corners = block_transpose(corners)

    edges = [
        [[corners_xy[e][d] for e in range(2)] for d in range(2)],
        [[corners_xz[e][d] for e in range(2)] for d in range(2)],
        [[corners[e * 2 + d : e * 2 + d + 1] for e in range(2)] for d in range(2)],
    ]
    for (d, e), edge in zip(PAIRS, edges):
        upper, lower = [swapped(far[e] == 1, *half) for half in edge]
        near_near, far_near = swapped(far[d] == 1, upper[0], lower[0])
        near_far, far_far = swapped(far[d] == 1, upper[1], lower[1])
        for r, value in enumerate((near_near, near_far, far_near, far_far)):
            send_ref[own ^ pair(d, e), r : r + 1, :] = value


def others(d):
    return [e for e in range(3) if e != d]


def pair(d, e):
    return (1 << d) ^ (1 << e)


def running_maximum(rows):
    fastest = functools.reduce(jnp.maximum, rows)
    lane = lax.broadcasted_iota(jnp.int32, fastest.shape, 1)
    fastest = jnp.where(lane >= MAX_LANE, fastest, 0.0)
    return jnp.broadcast_to(jnp.max(fastest), (1, LANES))


def pass_on(send_ref, own, fastest, faces, edges, corners):
    lane = lax.broadcasted_iota(jnp.int32, (1, LANES), 1)
    for t in range(8):
        send_ref[t, FACE - 1 : FACE, :] = fastest
    for d in range(3):
        slot = own ^ (1 << d)
        send_ref[slot, :FACE, :] = faces[d]
        send_ref[slot, FACE - 1 : FACE, :] = jnp.where(lane >= MAX_LANE, fastest, faces[d][FACE - 1 : FACE])
        for r, value in enumerate(edges[d]):
            send_ref[slot, FACE + r : FACE + r + 1, :] = value
    for (d, e), value in zip(PAIRS, corners):
        send_ref[own ^ pair(d, e), 0:1, :] = value


def carry_once(got_ref, send_ref):
    own, to, _ = whereabouts()[0]
    fastest = running_maximum([got_ref[t, FACE - 1 : FACE, :] for t in range(8)])
    faces = [
        jnp.concatenate([got_ref[own ^ (1 << d), 32:, :], got_ref[own ^ (1 << d), FACE:32, :]], axis=0)
        for d in range(3)
    ]

    def edge(d, e, r):
        return got_ref[own ^ pair(d, e), r : r + 1, :]

    edges = [[edge(d, e, 1 if e < d else 2) for e in others(d)] for d in range(3)]
    pass_on(send_ref, to, fastest, faces, edges, [edge(d, e, 3) for d, e in PAIRS])


def carry_twice(got_ref, send_ref):
    _, own, to = whereabouts()[0]
    fastest = running_maximum([got_ref[t, FACE - 1 : FACE, :] for t in range(8)])
    faces = [got_ref[own ^ (1 << d), :FACE, :] for d in range(3)]

    def far_far(d, e):
        return got_ref[own ^ pair(d, e), 0:1, :]

    edges = []
    for d in range(3):
        passed = [got_ref[own ^ (1 << d), FACE + r : FACE + r + 1, :] for r in range(2)]
        edges.append(passed + [far_far(d, e) for e in others(d)])
    pass_on(send_ref, to, fastest, faces, edges, [far_far(d, e) for d, e in PAIRS])


def arrived(got0, got1, got2):
    own, first, twice = whereabouts()
    upper_far = [bit == 1 for bit in first]
    faces = []
    for d in range(3):
        near = got0[own[0] ^ (1 << d), :ROWS]
        far = jnp.where(twice[d], got2[own[2] ^ (1 << d)], got1[own[1] ^ (1 << d)])
        faces.append(swapped(upper_far[d], near, far))

    def once(d, r):
        return got1[own[1] ^ (1 << d), FACE + r : FACE + r + 1, :]

    def again(d, r):
        return got2[own[2] ^ (1 << d), FACE + r : FACE + r + 1, :]

    edges = []
    for d, e in PAIRS:
        of_e, of_d = others(d).index(e), others(e).index(d)
        near_near = got0[own[0] ^ pair(d, e), 0:1, :]
        near_far = jnp.where(twice[e], again(e, of_d), once(e, of_d))
        far_near = jnp.where(twice[d], again(d, of_e), once(d, of_e))
        both = jnp.where(twice[e], got2[own[2] ^ pair(d, e), 0:1, :], again(d, 2 + of_e))
        neither = jnp.where(twice[e], again(e, 2 + of_d), got1[own[1] ^ pair(d, e), 0:1, :])
        far_far = jnp.where(twice[d], both, neither)
        near, far = [swapped(upper_far[e], *half) for half in ((near_near, near_far), (far_near, far_far))]
        above, below = zip(*[swapped(upper_far[d], n, f) for n, f in zip(near, far)])
        edges.append((above, below))
    return faces, edges


def surround(faces, edges, inner_ref, spread, scr_x):
    lane, x, y, z = positions(8)
    row = lax.broadcasted_iota(jnp.int32, (8, LANES), 0)
    left4 = lax.broadcasted_iota(jnp.int32, (32, LANES), 1) < 64
    inner = [inner_ref[n] for n in range(COUNT)]
    rows = []
    for side in range(2):
        value = faces[0][side]
        rows += [jnp.where(left4, value, 0.0), jnp.where(left4, roll(value, 64, 1), 0.0)]
    scr_x[...] = place(jnp.concatenate(rows, axis=0), spread)

    def around(n, above_n=None, upper_row=7):
        above_n = n if above_n is None else above_n
        places = [m if m < PAIRED else m - PAIRED + 32 for m in (above_n, n)]
        above = jnp.broadcast_to(scr_x[places[0] : places[0] + 1, :], (8, LANES))
        below = jnp.broadcast_to(scr_x[places[1] + 64 : places[1] + 65, :], (8, LANES))
        return jnp.where(row == upper_row, above, below)

    beside = [[around(f * 8 + 4 + q, f * 8 + q) for f in range(5)] for q in range(4)]
    beyond = [[around(f * 8 + q, f * 8 + 4 + q) for f in range(5)] for q in range(4)]
    covered = around(COVER)
    coarse_outer = [around(n, upper_row=0) for n in range(COARSE, COVER)]

    def put_beside(n, mask, value):
        f, q = n // 8, n % 4
        beside[q][f] = jnp.where(mask, value, beside[q][f])

    def put_coarse(f, mask, value):
        coarse_outer[f] = jnp.where(mask, value, coarse_outer[f])


    def doubled(value):
        return jnp.concatenate([value[24:28], value[24:28]], axis=0)

    for side, (near, at) in enumerate(SIDES):
        blocks = [faces[1][side][block * 8 : block * 8 + 8] for block in range(3)]
        order = y_order(near)
        first = at * PITCH % LANES
        here = (lane >= first) & (lane < first + 8)
        for block, names in zip(blocks, order):
            for s, n in enumerate(names):
                inner[n] = jnp.where(here, roll(block, first - s * 8, 1), inner[n])
        last = doubled(faces[1][side])
        for s, n in enumerate(order[3]):
            value = jnp.where(row < 4, roll(last, first - s * 8, 1), roll(last, first - (s + len(order[3])) * 8, 1))
            inner[n] = jnp.where(here, value, inner[n])
        above, below = [jnp.broadcast_to(edges[0][end][side], (8, LANES)) for end in range(2)]
        edge, coarse_edge = jnp.where(row == 7, above, below), jnp.where(row == 0, above, below)
        for s in range(10):
            put_beside(order[0][s], here, roll(edge, first - s * 8, 1))
        for s in range(10, 15):
            put_coarse(s - 10, here, roll(coarse_edge, first - s * 8, 1))

    columns = jnp.concatenate([edges[2][end][side] for side in range(2) for end in range(2)] * 2, axis=0)
    columns = block_transpose(columns)
    for side, (near, at) in enumerate(SIDES):
        blocks = [faces[2][side][block * 8 : block * 8 + 8] for block in range(3)]
        order = z_order(near)
        here = (z == at) & (y < 9)
        low_y = y < 4
        above, below = side * 32, side * 32 + 16

        def joined(block):
            return jnp.where(lane < 40, roll(block, -80, 1), roll(block, -45, 1))

        def ended(block, i, below_lane):
            block = jnp.where(lane < 80, block, roll(columns, 80 - above - i, 1))
            return jnp.where(lane >= below_lane, roll(columns, below_lane - below - i, 1), block)

        mains = [ended(blocks[0], 0, 123), ended(blocks[1], 5, 123), blocks[2]]
        halves = [ended(joined(blocks[0]), 10, 118), joined(blocks[1]), joined(blocks[2])]
        for block in range(3):
            for source, names in ((mains[block], order[block][0]), (halves[block], order[block][1])):
                for s, n in enumerate(names):
                    inner[n] = jnp.where(here, roll(source, at - s, 1), inner[n])
        last = doubled(faces[2][side])
        for s, n in enumerate(order[3][0]):
            value = jnp.where(row < 4, roll(last, at - s, 1), roll(last, at - 5 - s, 1))
            inner[n] = jnp.where(here, value, inner[n])
        upper_rows = jnp.where(low_y, roll(last, at - 80, 1), roll(last, at - 41, 1))
        lower_rows = jnp.where(low_y, roll(last, at - 82, 1), roll(last, at - 43, 1))
        n = order[3][1][0]
        inner[n] = jnp.where(here, jnp.where(row < 4, upper_rows, lower_rows), inner[n])

        above, below = [jnp.broadcast_to(edges[1][end][side], (8, LANES)) for end in range(2)]
        edge, coarse_edge = jnp.where(row == 7, above, below), joined(jnp.where(row == 0, above, below))
        for s in range(10):
            put_beside(order[0][0][s], here & inside(y), roll(edge, at - s, 1))
        for s in range(5):
            put_coarse(s, here & inside(y), roll(coarse_edge, at - s, 1))
    fine = [[inner[f * 8 + q] for f in range(5)] for q in range(8)]
    coarse = [jnp.concatenate([i, o], axis=0) for i, o in zip(inner[COARSE:COVER], coarse_outer)]
    return fine, beside, beyond, coarse[:5], coarse[5:], inner[COVER] > 0.5, covered > 0.5


def advance(got0, got1, got2, inner_ref, back_ref, spread_ref, dense_ref, coarse_out, fine_out, scr, scr_x):
    lane, x, y, z = positions(16)
    fastest = running_maximum([got2[t, FACE - 1 : FACE, :] for t in range(8)])
    half16 = 0.5 * (courant / jnp.broadcast_to(fastest, (16, LANES)))
    half = half16[:8]
    faces, edges = arrived(got0, got1, got2)
    fine0, beside, beyond, coarse0, deep, covered, covered_beside = surround(
        faces, edges, inner_ref, spread_ref[...], scr_x
    )
    row = lax.broadcasted_iota(jnp.int32, (8, LANES), 0)

    net = coarse_net(coarse0, deep, (x, y, z))
    coarse1 = [u - 0.5 * half16 * n for u, n in zip(coarse0, net)]
    net, net_beside = fine_net(fine0, beside, beyond)

    def first_section(u, net, covered, coarse):
        return [jnp.where(covered, a - half * n, c) for a, n, c in zip(u, net, coarse)]

    coarse_beside = [jnp.where(row == 7, roll(c[8:], 7, 0), roll(c[8:], 1, 0)) for c in coarse1]
    fine1 = [first_section(fine0[q], net[q], covered, [c[:8] for c in coarse1]) for q in range(8)]
    beside1 = [first_section(beside[q], net_beside[q], covered_beside, coarse_beside) for q in range(4)]
    net = coarse_net(coarse1, None, None, True)
    coarse2 = [0.5 * c0[:8] + 0.5 * (c1[:8] - 0.5 * half * n[:8]) for c0, c1, n in zip(coarse0, coarse1, net)]
    net, _ = fine_net(fine1, beside1, None)
    mine = inside(y[:8]) & inside(z[:8])
    refined = mine & covered
    fine2 = [
        [
            jnp.where(refined, 0.5 * fine0[q][f] + 0.5 * (fine1[q][f] - half * net[q][f]), 0.0)
            for f in range(5)
        ]
        for q in range(8)
    ]
    coarse = []
    for f in range(5):
        total = functools.reduce(jnp.add, [fine2[q][f] for q in range(8)])
        coarse.append(jnp.where(mine, jnp.where(refined, 0.125 * total, coarse2[f]), 0.0))

    left_half = lane[:8] < 64
    rows = [jnp.concatenate([fine2[a * 4 + q][f] for q in range(4)], axis=1) for a in range(2) for f in range(5)]
    back = place(jnp.concatenate(rows, axis=0), back_ref[...])
    for f in range(5):
        for h in range(2):
            even = back[f * 8 : f * 8 + 8, h * 128 : h * 128 + 128]
            odd = back[40 + f * 8 : 48 + f * 8, h * 128 : h * 128 + 128]
            scr[f, h * 16 : h * 16 + 8, :] = jnp.where(left_half, even, roll(odd, 64, 1))
            scr[f, h * 16 + 8 : h * 16 + 16, :] = jnp.where(left_half, roll(even, 64, 1), odd)
        for q in range(4):
            for ox in range(2):
                tile = scr[f, pl.ds(ox * 4 + q, 4, stride=8), :]
                fine_out[f, ox * 4 : ox * 4 + 4, q * 128 : q * 128 + 128] = tile
    back = place(jnp.concatenate(coarse, axis=0), dense_ref[...])
    for f in range(5):
        value = back[f * 8 : f * 8 + 8]
        value = jnp.where(left_half, value, roll(roll(value, 64, 1), -1, 0))
        for q in range(4):
            coarse_out[f, :, q * 128 : q * 128 + 128] = value[2 * q : 2 * q + 1]


def shape(*dims):
    return jax.ShapeDtypeStruct(dims, jnp.float32)


def call(kernel, outs, scratch, args, cost=None):
    return pl.pallas_call(
        kernel,
        out_shape=outs,
        in_specs=[pl.BlockSpec(memory_space=pltpu.VMEM)] * len(args),
        out_specs=[pl.BlockSpec(memory_space=pltpu.VMEM)] * len(outs),
        scratch_shapes=scratch,
        cost_estimate=cost,
        compiler_params=pltpu.CompilerParams(vmem_limit_bytes=32 * 1024 * 1024),
    )(*args)


def swap(block, level):
    count = lax.axis_size("boxes")
    low = 3 * level
    first = [device for device in range(count) if not (device >> low) & 7]
    groups = [[device | (slot ^ LEAD[level]) << low for slot in range(8)] for device in first]
    return lax.all_to_all(block, "boxes", 0, 0, axis_index_groups=groups)


def local(coarse_state, fine_state, refined):
    back = jnp.asarray(back_matrix().astype(ml_dtypes.bfloat16))
    fields = lambda *dims: pltpu.VMEM(dims, jnp.float32)
    matrix = lambda *dims: jax.ShapeDtypeStruct(dims, jnp.bfloat16)
    made = call(matrices, [matrix(256, 4 * LANES), matrix(LANES, LANES), matrix(LANES, LANES)], [], (), pl.CostEstimate(flops=50000000, bytes_accessed=327680, transcendentals=0))
    inner, send = call(
        prepare,
        [shape(COUNT, 8, LANES), shape(8, 2 * FACE, LANES)],
        [fields(5, 40, LANES), fields(5, 8, LANES), fields(128, LANES)],
        (refined, jnp.swapaxes(coarse_state, 0, 1), jnp.swapaxes(fine_state[0], 0, 1), *made),
    )
    got0 = swap(send, 0)
    got1 = swap(call(carry_once, [shape(8, ROWS, LANES)], [], (got0,))[0], 1)
    got2 = swap(call(carry_twice, [shape(8, ROWS, LANES)], [], (got1,))[0], 2)
    coarse_out, fine_out = call(
        advance,
        [shape(5, 1, 512), shape(5, 8, 512)],
        [fields(5, 40, LANES), fields(128, LANES)],
        (got0, got1, got2, inner, back, *made[1:]),
    )
    return jnp.swapaxes(coarse_out, 0, 1), jnp.swapaxes(fine_out, 0, 1)[None]


def solution(mesh):
    in_specs = (P("boxes", None, None), P("boxes", None, None, None), P("boxes", None))
    out_specs = (P("boxes", None, None), P("boxes", None, None, None))
    return jax.shard_map(local, mesh=mesh, in_specs=in_specs, out_specs=out_specs, check_vma=False)
```

```python
import functools

import jax
import jax.numpy as jnp
import ml_dtypes
import numpy as np
from jax import lax
from jax.experimental import pallas as pl
from jax.experimental.pallas import tpu as pltpu
from jax.sharding import PartitionSpec as P

PITCH = 10
LANES = 128
FINE = 40
COARSE = FINE
DEEP = COARSE + 5
COVER = DEEP + 5
COUNT = COVER + 1
FACE = 28
ROWS = 32
MAX_LANE = 120
PAIRED = 26
LEAD = (5, 6, 4)
SIDES = ((0, 8), (1, -1))
PAIRS = ((0, 1), (0, 2), (1, 2))
gamma_gas = 1.4
courant = 0.4


def back_matrix():
    back = np.zeros((512, 256), np.float32)
    for y in range(16):
        for z in range(16):
            row = (y // 8 * 2 + z // 8) * 64 + y % 8 * 8 + z % 8
            back[(y % 2 * 2 + z % 2) * 128 + y // 2 * PITCH + z // 2, row] = 1
    return back


def place(values, matrix):
    high = values.astype(jnp.bfloat16)
    rest = values - high.astype(jnp.float32)
    middle = rest.astype(jnp.bfloat16)
    low = (rest - middle.astype(jnp.float32)).astype(jnp.bfloat16)
    rows = values.shape[0]
    parts = jnp.concatenate([high, middle, low], axis=0)
    out = jnp.dot(parts, matrix, preferred_element_type=jnp.float32)
    return out[:rows] + out[rows : 2 * rows] + out[2 * rows :]


def roll(x, shift, axis):
    shift = shift % x.shape[axis]
    return pltpu.roll(x, shift, axis) if shift else x


def positions(rows):
    row = lax.broadcasted_iota(jnp.int32, (rows, LANES), 0)
    lane = lax.broadcasted_iota(jnp.int32, (rows, LANES), 1)
    x = jnp.where(row > 8, row - 16, row)
    along = (lane + PITCH + 1) & (LANES - 1)
    y1 = (along * 205) >> 11
    return lane, x, y1 - 1, along - y1 * PITCH - 1


def inside(pos):
    return (pos >= 0) & (pos < 8)


def primitive(u):
    inverse = 1.0 / u[0]
    v = [u[1 + d] * inverse for d in range(3)]
    pressure = 0.4 * (u[4] - 0.5 * (u[1] * v[0] + u[2] * v[1] + u[3] * v[2]))
    sound = jnp.sqrt(gamma_gas * pressure * inverse)
    return v, pressure, sound


def cell_flux(u, prim, d):
    v, pressure, sound = prim
    flux = [u[1 + d]] + [u[1 + e] * v[d] for e in range(3)] + [(u[4] + pressure) * v[d]]
    flux[1 + d] = flux[1 + d] + pressure
    return list(u) + flux + [jnp.abs(v[d]) + sound]


def moved_cell(u, prim, d, shift):
    v, pressure, sound = prim
    u, v_d = [shift(f) for f in u], shift(v[d])
    pressure = shift(pressure)
    flux = [u[1 + d]] + [u[1 + e] * v_d for e in range(3)] + [(u[4] + pressure) * v_d]
    flux[1 + d] = flux[1 + d] + pressure
    return u + flux + [shift(jnp.abs(v[d]) + sound)]


def face(left, right):
    speed = jnp.maximum(left[10], right[10])
    return [(left[5 + f] + right[5 + f]) - speed * (right[f] - left[f]) for f in range(5)]


def ahead(x, d):
    return roll(x, -1, 0) if d == 0 else roll(x, -PITCH if d == 1 else -1, 1)


def behind(x, d):
    return roll(x, 1, 0) if d == 0 else roll(x, PITCH if d == 1 else 1, 1)


def fine_net(u, beside, beyond):
    row = lax.broadcasted_iota(jnp.int32, (8, LANES), 0)
    prims, prims_beside = [primitive(v) for v in u], [primitive(v) for v in beside]
    total, total_beside = [None] * 8, [None] * 4

    def add(totals, q, net):
        totals[q] = net if totals[q] is None else [s + n for s, n in zip(totals[q], net)]

    def minus(left, right):
        return [a - b for a, b in zip(left, right)]

    def either(flag, first, second):
        return [jnp.where(flag, a, b) for a, b in zip(first, second)]

    for q in range(4):
        low, high = cell_flux(u[q], prims[q], 0), cell_flux(u[q + 4], prims[q + 4], 0)
        near = cell_flux(beside[q], prims_beside[q], 0)
        middle = face(low, high)
        after = face(high, either(row == 7, near, moved_cell(u[q], prims[q], 0, lambda x: roll(x, -1, 0))))
        first = face(near, low)
        add(total, q, minus(middle, either(row == 0, first, [roll(x, 1, 0) for x in after])))
        add(total, q + 4, minus(after, middle))
        if beyond is not None:
            next_ = cell_flux(beyond[q], primitive(beyond[q]), 0)
            outer = face(either(row == 0, next_, near), either(row == 0, near, next_))
            add(total_beside, q, either(row == 0, minus(first, outer), minus(outer, after)))
    groups = [(u, prims, total, (0, 4))]
    if beyond is not None:
        groups.append((beside, prims_beside, total_beside, (0,)))
    for d in (1, 2):
        bit = 4 >> d
        for cells, prim, totals, starts in groups:
            for low in [start + q for start in starts for q in range(4) if not q & bit]:
                high = low | bit
                left, right = cell_flux(cells[low], prim[low], d), cell_flux(cells[high], prim[high], d)
                middle = face(left, right)
                after = face(right, moved_cell(cells[low], prim[low], d, lambda x: ahead(x, d)))
                add(totals, low, minus(middle, [behind(x, d) for x in after]))
                add(totals, high, minus(after, middle))
    return total, total_beside


def coarse_net(u, deep, pos, inner=False):
    prim = primitive(u)
    prim_deep = None if deep is None else primitive(deep)
    total = None
    for d in range(3):
        if inner and d == 1:
            u, prim = [x[:8] for x in u], ([x[:8] for x in prim[0]], prim[1][:8], prim[2][:8])
            total = [x[:8] for x in total]
        cell = cell_flux(u, prim, d)
        right = [ahead(x, d) for x in cell]
        if deep is not None:
            outer = cell_flux(deep, prim_deep, d)
            last, first = pos[d] == 8, pos[d] == -1
            right = [jnp.where(last, o, r) for o, r in zip(outer, right)]
        after = face(cell, right)
        before = [behind(x, d) for x in after]
        if deep is not None:
            before = [jnp.where(first, o, b) for o, b in zip(face(outer, cell), before)]
        net = [a - b for a, b in zip(after, before)]
        total = net if total is None else [s + n for s, n in zip(total, net)]
    return total


def put_faces(send_ref, slot, upper_far, faces):
    for side, blocks in enumerate(faces):
        first = pl.multiple_of((upper_far if side == 0 else 1 - upper_far) * 32, 8)
        for block in range(3):
            send_ref[slot, pl.ds(first + block * 8, 8), :] = blocks[block]
    near, far = swapped(upper_far == 1, faces[0][3], faces[1][3])
    send_ref[slot, 24:32, :] = jnp.concatenate([near[:4], far[:4]], axis=0)


def is_deep(n):
    return DEEP <= n < COVER


def fine_index(f, a, b, c):
    return f * 8 + a * 4 + b * 2 + c


def y_order(near):
    rest = [fine_index(f, a, 1 - near, c) for f in range(5) for a in range(2) for c in range(2)]
    first = [fine_index(f, 1, near, c) for c in range(2) for f in range(5)]
    second = [fine_index(f, 0, near, c) for c in range(2) for f in range(5)]
    return (
        first + [COARSE + f for f in range(5)] + rest[:1],
        second + [DEEP + f for f in range(5)] + [COVER],
        rest[1:17],
        rest[17:],
    )


def z_order(near):
    rest = [fine_index(f, a, b, 1 - near) for f in range(5) for a in range(2) for b in range(2)]
    first = [fine_index(f, 1, b, near) for b in range(2) for f in range(5)]
    second = [fine_index(f, 0, b, near) for b in range(2) for f in range(5)]
    return (
        (first, [COARSE + f for f in range(5)]),
        (second, [DEEP + f for f in range(5)]),
        (rest[:10], [COVER] + rest[10:14]),
        (rest[14:19], rest[19:]),
    )


def block_transpose(value):
    row = lax.broadcasted_iota(jnp.int32, (8, LANES), 0)
    group = lax.broadcasted_iota(jnp.int32, (8, LANES), 1) >> 4
    out = value
    for step in range(1, 8):
        moved = roll(roll(value, -16 * step, 1), step, 0)
        out = jnp.where(((row - group) & 7) == step, moved, out)
    return out


def swapped(flag, first, second):
    return jnp.where(flag, second, first), jnp.where(flag, first, second)


def whereabouts():
    device = lax.axis_index("boxes")
    own = [((device >> (3 * level)) & 7) ^ lead for level, lead in enumerate(LEAD)]
    first = [(device >> d) & 1 for d in range(3)]
    second = [(device >> (3 + d)) & 1 for d in range(3)]
    return own, first, [a == b for a, b in zip(first, second)]


def fine_matrix():
    row = lax.broadcasted_iota(jnp.int32, (256, LANES), 0)
    lane = lax.broadcasted_iota(jnp.int32, (256, LANES), 1)
    y = ((row >> 7) << 2) + ((row >> 4) & 3)
    z = (((row >> 6) & 1) << 2) + ((row >> 1) & 3)
    hit = lane == y * PITCH + z
    parity = ((row >> 2) & 2) + (row & 1)
    return [jnp.where(hit & (parity == q), 1.0, 0.0).astype(jnp.bfloat16) for q in range(4)]


def coarse_matrices():
    row = lax.broadcasted_iota(jnp.int32, (LANES, LANES), 0)
    lane = lax.broadcasted_iota(jnp.int32, (LANES, LANES), 1)
    spread = (row < 64) & (lane == (row >> 3) * PITCH + (row & 7))
    dense = (lane < 64) & (row == (lane >> 3) * PITCH + (lane & 7))
    return [jnp.where(hit, 1.0, 0.0).astype(jnp.bfloat16) for hit in (spread, dense)]


def matrices(place_ref, spread_ref, dense_ref):
    for q, part in enumerate(fine_matrix()):
        place_ref[:, q * LANES : (q + 1) * LANES] = part
    spread_ref[...], dense_ref[...] = coarse_matrices()


def prepare(
    refined_ref, coarse_ref, fine_ref, place_ref, spread_ref, dense_ref, inner_ref, send_ref, scr, scr_c, scr_x
):
    places, far, _ = whereabouts()
    own = places[0]
    lane, x, y, z = positions(8)
    row = lax.broadcasted_iota(jnp.int32, (8, LANES), 0)
    left_half = lane < 64
    for f in range(5):
        for q in range(4):
            tile = fine_ref[f, :, q * 128 : q * 128 + 128]
            for ox in range(2):
                scr[f, pl.ds(ox * 4 + q, 4, stride=8), :] = tile[ox * 4 : ox * 4 + 4]
            part = coarse_ref[f, :, q * 128 : q * 128 + 128]
            scr_c[f, 2 * q : 2 * q + 1, :] = part
            scr_c[f, 2 * q + 1 : 2 * q + 2, :] = part
    sides = [[], []]
    rows = []
    for f in range(5):
        tile = [scr[f, c * 8 : c * 8 + 8, :] for c in range(4)]
        sides[0].append(
            jnp.concatenate([jnp.where(left_half, tile[2 * h], roll(tile[2 * h + 1], 64, 1)) for h in range(2)], axis=1)
        )
        sides[1].append(
            jnp.concatenate([jnp.where(left_half, roll(tile[2 * h], 64, 1), tile[2 * h + 1]) for h in range(2)], axis=1)
        )
        value = scr_c[f]
        rows.append(jnp.where((row & 1) == 1, roll(value, 64, 1), value))
    fine = place(jnp.concatenate(sides[0] + sides[1], axis=0), place_ref[...])
    coarse = place(jnp.concatenate(rows, axis=0), spread_ref[...])
    coarse = [coarse[f * 8 : f * 8 + 8] for f in range(5)]

    covered = jnp.zeros((8, LANES), jnp.float32)
    for o in range(8):
        here = ((x >= 4) == (o >= 4)) & ((y >= 4) == (o % 4 >= 2)) & ((z >= 4) == (o % 2 == 1))
        flag = jnp.broadcast_to(refined_ref[:, o : o + 1], (8, LANES))
        covered = jnp.where(here & (flag > 0), 1.0, covered)
    state = []
    for f in range(5):
        for q in range(8):
            first = (q // 4 * 5 + f) * 8
            part = fine[first : first + 8, q % 4 * 128 : q % 4 * 128 + 128]
            state.append(jnp.where(covered > 0.5, part, coarse[f]))
    state += coarse
    fastest = None
    for u in [[state[f * 8 + q] for f in range(5)] for q in range(8)] + [coarse]:
        v, pressure, sound = primitive(u)
        speed = jnp.abs(v[0]) + jnp.abs(v[1]) + jnp.abs(v[2]) + 3.0 * sound
        fastest = speed if fastest is None else jnp.maximum(fastest, speed)
    fastest = jnp.where(inside(y) & inside(z), fastest, 0.0)
    fastest = jnp.broadcast_to(jnp.max(fastest), (8, LANES))

    zero = jnp.zeros((8, LANES), jnp.float32)
    stored = state + [zero] * 5 + [covered]
    for n in range(COUNT):
        inner_ref[n] = stored[n]

    for t in range(8):
        send_ref[t, FACE - 1 : FACE, :] = fastest[:1]

    def taken(n, at, deep_at):
        return (stored[n - 5], deep_at) if is_deep(n) else (stored[n], at)

    for side, at, deep_at in ((0, 7, 6), (1, 0, 1)):
        for n in range(COUNT):
            value, where = taken(n, at, deep_at)
            target = side * 64 + (n if n < PAIRED else n - PAIRED + 32)
            scr_x[target : target + 1, :] = value[where : where + 1, :]
    dense = place(scr_x[...], dense_ref[...])
    left4 = lax.broadcasted_iota(jnp.int32, (32, LANES), 1) < 64
    row32 = lax.broadcasted_iota(jnp.int32, (32, LANES), 0)
    faces_x, faces_y, faces_z = [], [], []
    for side in range(2):
        packed = jnp.where(left4, dense[side * 64 : side * 64 + 32], roll(dense[side * 64 + 32 : side * 64 + 64], 64, 1))
        packed = jnp.where(row32 >= PAIRED, jnp.concatenate([fastest] * 4, axis=0), packed)
        faces_x.append([packed[block * 8 : block * 8 + 8] for block in range(4)])
    put_faces(send_ref, own ^ 1, far[0], faces_x)

    slots = lane - ((lane * 205) >> 11) * PITCH
    corners_xy, corners_xz, corners = [], [], zero
    for side, at, deep_at in ((0, 7, 6), (1, 0, 1)):
        near = 1 - side
        order = y_order(near)
        blocks = []
        for names in order:
            packed = fastest
            for s, n in enumerate(names):
                value, where = taken(n, at, deep_at)
                packed = jnp.where((lane >> 3) == s, roll(value, s * 8 - where * PITCH, 1), packed)
            blocks.append(packed)
        width = len(order[3]) * 8
        second = (lane >= width) & (lane < 2 * width)
        blocks[3] = jnp.where(second, roll(roll(blocks[3], width, 1), 4, 0), blocks[3])
        faces_y.append(blocks)
        corners_xy.append((blocks[0][7:8], jnp.where(lane < 80, blocks[1], blocks[0])[0:1]))

        blocks = []
        for block, (names, halves) in enumerate(z_order(near)):
            packed = fastest
            for s, n in enumerate(names):
                value, where = taken(n, at, deep_at)
                packed = jnp.where((slots == s) & (lane < 80), roll(value, s - where, 1), packed)
            if block < 3:
                extra = fastest
                for s, n in enumerate(halves):
                    value, where = taken(n, at, deep_at)
                    extra = jnp.where(slots == s, roll(value, s - where, 1), extra)
                extra = jnp.where(slots < 5, roll(extra, 80, 1), roll(extra, 45, 1))
                packed = jnp.where((lane >= 80) & (lane < MAX_LANE), extra, packed)
            else:
                second = (slots >= 5) & (lane < 80)
                packed = jnp.where(second, roll(roll(packed, 5, 1), 4, 0), packed)
                value = stored[halves[0]]
                lower = roll(value, 4, 0)
                pieces = [roll(value, 80 - at, 1), roll(value, 41 - at, 1), roll(lower, 82 - at, 1), roll(lower, 43 - at, 1)]
                for s, piece in enumerate(pieces):
                    packed = jnp.where((slots == s) & (lane >= 80) & (lane < MAX_LANE), piece, packed)
            blocks.append(packed)
        faces_z.append(blocks)
        corners_xz.append((blocks[0][7:8], jnp.where(lane < 80, blocks[1], blocks[0])[0:1]))
        for end, first, first_coarse in ((0, 75, 115), (1, 0, 80)):
            to = (side * 2 + end) * 16
            for start, source, i in ((first, blocks[0], 0), (first, blocks[1], 5), (first_coarse, blocks[0], 10)):
                here = (lane >= to + i) & (lane < to + i + 5)
                corners = jnp.where(here, roll(source, to + i - start, 1), corners)
    put_faces(send_ref, own ^ 2, far[1], faces_y)
    put_faces(send_ref, own ^ 4, far[2], faces_z)
    corners = block_transpose(corners)

    edges = [
        [[corners_xy[e][d] for e in range(2)] for d in range(2)],
        [[corners_xz[e][d] for e in range(2)] for d in range(2)],
        [[corners[e * 2 + d : e * 2 + d + 1] for e in range(2)] for d in range(2)],
    ]
    for (d, e), edge in zip(PAIRS, edges):
        upper, lower = [swapped(far[e] == 1, *half) for half in edge]
        near_near, far_near = swapped(far[d] == 1, upper[0], lower[0])
        near_far, far_far = swapped(far[d] == 1, upper[1], lower[1])
        for r, value in enumerate((near_near, near_far, far_near, far_far)):
            send_ref[own ^ pair(d, e), r : r + 1, :] = value


def others(d):
    return [e for e in range(3) if e != d]


def pair(d, e):
    return (1 << d) ^ (1 << e)


def so_far(rows):
    return functools.reduce(jnp.maximum, rows)


def running_maximum(rows):
    fastest = so_far(rows)
    lane = lax.broadcasted_iota(jnp.int32, fastest.shape, 1)
    fastest = jnp.where(lane >= MAX_LANE, fastest, 0.0)
    return jnp.broadcast_to(jnp.max(fastest), (1, LANES))


def pass_on(send_ref, own, fastest, faces, edges, corners):
    lane = lax.broadcasted_iota(jnp.int32, (1, LANES), 1)
    for t in range(8):
        send_ref[t, FACE - 1 : FACE, :] = fastest
    for d in range(3):
        slot = own ^ (1 << d)
        send_ref[slot, :FACE, :] = faces[d]
        send_ref[slot, FACE - 1 : FACE, :] = jnp.where(lane >= MAX_LANE, fastest, faces[d][FACE - 1 : FACE])
        for r, value in enumerate(edges[d]):
            send_ref[slot, FACE + r : FACE + r + 1, :] = value
    for (d, e), value in zip(PAIRS, corners):
        send_ref[own ^ pair(d, e), 0:1, :] = value


def carry_once(got_ref, send_ref):
    own, to, _ = whereabouts()[0]
    fastest = so_far([got_ref[t, FACE - 1 : FACE, :] for t in range(8)])
    faces = [
        jnp.concatenate([got_ref[own ^ (1 << d), 32:, :], got_ref[own ^ (1 << d), FACE:32, :]], axis=0)
        for d in range(3)
    ]

    def edge(d, e, r):
        return got_ref[own ^ pair(d, e), r : r + 1, :]

    edges = [[edge(d, e, 1 if e < d else 2) for e in others(d)] for d in range(3)]
    pass_on(send_ref, to, fastest, faces, edges, [edge(d, e, 3) for d, e in PAIRS])


def carry_twice(got_ref, send_ref):
    _, own, to = whereabouts()[0]
    fastest = so_far([got_ref[t, FACE - 1 : FACE, :] for t in range(8)])
    faces = [got_ref[own ^ (1 << d), :FACE, :] for d in range(3)]

    def far_far(d, e):
        return got_ref[own ^ pair(d, e), 0:1, :]

    edges = []
    for d in range(3):
        passed = [got_ref[own ^ (1 << d), FACE + r : FACE + r + 1, :] for r in range(2)]
        edges.append(passed + [far_far(d, e) for e in others(d)])
    pass_on(send_ref, to, fastest, faces, edges, [far_far(d, e) for d, e in PAIRS])


def arrived(got0, got1, got2):
    own, first, twice = whereabouts()
    upper_far = [bit == 1 for bit in first]
    faces = []
    for d in range(3):
        near = got0[own[0] ^ (1 << d), :ROWS]
        far = jnp.where(twice[d], got2[own[2] ^ (1 << d)], got1[own[1] ^ (1 << d)])
        faces.append(swapped(upper_far[d], near, far))

    def once(d, r):
        return got1[own[1] ^ (1 << d), FACE + r : FACE + r + 1, :]

    def again(d, r):
        return got2[own[2] ^ (1 << d), FACE + r : FACE + r + 1, :]

    edges = []
    for d, e in PAIRS:
        of_e, of_d = others(d).index(e), others(e).index(d)
        near_near = got0[own[0] ^ pair(d, e), 0:1, :]
        near_far = jnp.where(twice[e], again(e, of_d), once(e, of_d))
        far_near = jnp.where(twice[d], again(d, of_e), once(d, of_e))
        both = jnp.where(twice[e], got2[own[2] ^ pair(d, e), 0:1, :], again(d, 2 + of_e))
        neither = jnp.where(twice[e], again(e, 2 + of_d), got1[own[1] ^ pair(d, e), 0:1, :])
        far_far = jnp.where(twice[d], both, neither)
        near, far = [swapped(upper_far[e], *half) for half in ((near_near, near_far), (far_near, far_far))]
        above, below = zip(*[swapped(upper_far[d], n, f) for n, f in zip(near, far)])
        edges.append((above, below))
    return faces, edges


def surround(faces, edges, inner_ref, spread, scr_x):
    lane, x, y, z = positions(8)
    row = lax.broadcasted_iota(jnp.int32, (8, LANES), 0)
    left4 = lax.broadcasted_iota(jnp.int32, (32, LANES), 1) < 64
    inner = [inner_ref[n] for n in range(COUNT)]
    rows = []
    for side in range(2):
        value = faces[0][side]
        rows += [jnp.where(left4, value, 0.0), jnp.where(left4, roll(value, 64, 1), 0.0)]
    scr_x[...] = place(jnp.concatenate(rows, axis=0), spread)

    def around(n, above_n=None, upper_row=7):
        above_n = n if above_n is None else above_n
        places = [m if m < PAIRED else m - PAIRED + 32 for m in (above_n, n)]
        above = jnp.broadcast_to(scr_x[places[0] : places[0] + 1, :], (8, LANES))
        below = jnp.broadcast_to(scr_x[places[1] + 64 : places[1] + 65, :], (8, LANES))
        return jnp.where(row == upper_row, above, below)

    beside = [[around(f * 8 + 4 + q, f * 8 + q) for f in range(5)] for q in range(4)]
    beyond = [[around(f * 8 + q, f * 8 + 4 + q) for f in range(5)] for q in range(4)]
    covered = around(COVER)
    coarse_outer = [around(n, upper_row=0) for n in range(COARSE, COVER)]

    def put_beside(n, mask, value):
        f, q = n // 8, n % 4
        beside[q][f] = jnp.where(mask, value, beside[q][f])

    def put_coarse(f, mask, value):
        coarse_outer[f] = jnp.where(mask, value, coarse_outer[f])


    def doubled(value):
        return jnp.concatenate([value[24:28], value[24:28]], axis=0)

    for side, (near, at) in enumerate(SIDES):
        blocks = [faces[1][side][block * 8 : block * 8 + 8] for block in range(3)]
        order = y_order(near)
        first = at * PITCH % LANES
        here = (lane >= first) & (lane < first + 8)
        for block, names in zip(blocks, order):
            for s, n in enumerate(names):
                inner[n] = jnp.where(here, roll(block, first - s * 8, 1), inner[n])
        last = doubled(faces[1][side])
        for s, n in enumerate(order[3]):
            value = jnp.where(row < 4, roll(last, first - s * 8, 1), roll(last, first - (s + len(order[3])) * 8, 1))
            inner[n] = jnp.where(here, value, inner[n])
        above, below = [jnp.broadcast_to(edges[0][end][side], (8, LANES)) for end in range(2)]
        edge, coarse_edge = jnp.where(row == 7, above, below), jnp.where(row == 0, above, below)
        for s in range(10):
            put_beside(order[0][s], here, roll(edge, first - s * 8, 1))
        for s in range(10, 15):
            put_coarse(s - 10, here, roll(coarse_edge, first - s * 8, 1))

    columns = jnp.concatenate([edges[2][end][side] for side in range(2) for end in range(2)] * 2, axis=0)
    columns = block_transpose(columns)
    for side, (near, at) in enumerate(SIDES):
        blocks = [faces[2][side][block * 8 : block * 8 + 8] for block in range(3)]
        order = z_order(near)
        here = (z == at) & (y < 9)
        low_y = y < 4
        above, below = side * 32, side * 32 + 16

        def joined(block):
            return jnp.where(lane < 40, roll(block, -80, 1), roll(block, -45, 1))

        def ended(block, i, below_lane):
            block = jnp.where(lane < 80, block, roll(columns, 80 - above - i, 1))
            return jnp.where(lane >= below_lane, roll(columns, below_lane - below - i, 1), block)

        mains = [ended(blocks[0], 0, 123), ended(blocks[1], 5, 123), blocks[2]]
        halves = [ended(joined(blocks[0]), 10, 118), joined(blocks[1]), joined(blocks[2])]
        for block in range(3):
            for source, names in ((mains[block], order[block][0]), (halves[block], order[block][1])):
                for s, n in enumerate(names):
                    inner[n] = jnp.where(here, roll(source, at - s, 1), inner[n])
        last = doubled(faces[2][side])
        for s, n in enumerate(order[3][0]):
            value = jnp.where(row < 4, roll(last, at - s, 1), roll(last, at - 5 - s, 1))
            inner[n] = jnp.where(here, value, inner[n])
        upper_rows = jnp.where(low_y, roll(last, at - 80, 1), roll(last, at - 41, 1))
        lower_rows = jnp.where(low_y, roll(last, at - 82, 1), roll(last, at - 43, 1))
        n = order[3][1][0]
        inner[n] = jnp.where(here, jnp.where(row < 4, upper_rows, lower_rows), inner[n])

        above, below = [jnp.broadcast_to(edges[1][end][side], (8, LANES)) for end in range(2)]
        edge, coarse_edge = jnp.where(row == 7, above, below), joined(jnp.where(row == 0, above, below))
        for s in range(10):
            put_beside(order[0][0][s], here & inside(y), roll(edge, at - s, 1))
        for s in range(5):
            put_coarse(s, here & inside(y), roll(coarse_edge, at - s, 1))
    fine = [[inner[f * 8 + q] for f in range(5)] for q in range(8)]
    coarse = [jnp.concatenate([i, o], axis=0) for i, o in zip(inner[COARSE:COVER], coarse_outer)]
    return fine, beside, beyond, coarse[:5], coarse[5:], inner[COVER] > 0.5, covered > 0.5


def advance(got0, got1, got2, inner_ref, back_ref, spread_ref, dense_ref, coarse_out, fine_out, scr, scr_x):
    lane, x, y, z = positions(16)
    fastest = running_maximum([got2[t, FACE - 1 : FACE, :] for t in range(8)])
    half16 = 0.5 * (courant / jnp.broadcast_to(fastest, (16, LANES)))
    half = half16[:8]
    faces, edges = arrived(got0, got1, got2)
    fine0, beside, beyond, coarse0, deep, covered, covered_beside = surround(
        faces, edges, inner_ref, spread_ref[...], scr_x
    )
    row = lax.broadcasted_iota(jnp.int32, (8, LANES), 0)

    net = coarse_net(coarse0, deep, (x, y, z))
    coarse1 = [u - 0.5 * half16 * n for u, n in zip(coarse0, net)]
    net, net_beside = fine_net(fine0, beside, beyond)

    def first_section(u, net, covered, coarse):
        return [jnp.where(covered, a - half * n, c) for a, n, c in zip(u, net, coarse)]

    coarse_beside = [jnp.where(row == 7, roll(c[8:], 7, 0), roll(c[8:], 1, 0)) for c in coarse1]
    fine1 = [first_section(fine0[q], net[q], covered, [c[:8] for c in coarse1]) for q in range(8)]
    beside1 = [first_section(beside[q], net_beside[q], covered_beside, coarse_beside) for q in range(4)]
    net = coarse_net(coarse1, None, None, True)
    coarse2 = [0.5 * c0[:8] + 0.5 * (c1[:8] - 0.5 * half * n[:8]) for c0, c1, n in zip(coarse0, coarse1, net)]
    net, _ = fine_net(fine1, beside1, None)
    mine = inside(y[:8]) & inside(z[:8])
    refined = mine & covered
    fine2 = [
        [
            jnp.where(refined, 0.5 * fine0[q][f] + 0.5 * (fine1[q][f] - half * net[q][f]), 0.0)
            for f in range(5)
        ]
        for q in range(8)
    ]
    coarse = []
    for f in range(5):
        total = functools.reduce(jnp.add, [fine2[q][f] for q in range(8)])
        coarse.append(jnp.where(mine, jnp.where(refined, 0.125 * total, coarse2[f]), 0.0))

    left_half = lane[:8] < 64
    rows = [jnp.concatenate([fine2[a * 4 + q][f] for q in range(4)], axis=1) for a in range(2) for f in range(5)]
    back = place(jnp.concatenate(rows, axis=0), back_ref[...])
    for f in range(5):
        for h in range(2):
            even = back[f * 8 : f * 8 + 8, h * 128 : h * 128 + 128]
            odd = back[40 + f * 8 : 48 + f * 8, h * 128 : h * 128 + 128]
            scr[f, h * 16 : h * 16 + 8, :] = jnp.where(left_half, even, roll(odd, 64, 1))
            scr[f, h * 16 + 8 : h * 16 + 16, :] = jnp.where(left_half, roll(even, 64, 1), odd)
        for q in range(4):
            for ox in range(2):
                tile = scr[f, pl.ds(ox * 4 + q, 4, stride=8), :]
                fine_out[f, ox * 4 : ox * 4 + 4, q * 128 : q * 128 + 128] = tile
    back = place(jnp.concatenate(coarse, axis=0), dense_ref[...])
    for f in range(5):
        value = back[f * 8 : f * 8 + 8]
        value = jnp.where(left_half, value, roll(roll(value, 64, 1), -1, 0))
        for q in range(4):
            coarse_out[f, :, q * 128 : q * 128 + 128] = value[2 * q : 2 * q + 1]


def shape(*dims):
    return jax.ShapeDtypeStruct(dims, jnp.float32)


def call(kernel, outs, scratch, args, cost=None):
    return pl.pallas_call(
        kernel,
        out_shape=outs,
        in_specs=[pl.BlockSpec(memory_space=pltpu.VMEM)] * len(args),
        out_specs=[pl.BlockSpec(memory_space=pltpu.VMEM)] * len(outs),
        scratch_shapes=scratch,
        cost_estimate=cost,
        compiler_params=pltpu.CompilerParams(vmem_limit_bytes=32 * 1024 * 1024),
    )(*args)


def swap(block, level):
    count = lax.axis_size("boxes")
    low = 3 * level
    first = [device for device in range(count) if not (device >> low) & 7]
    groups = [[device | (slot ^ LEAD[level]) << low for slot in range(8)] for device in first]
    return lax.all_to_all(block, "boxes", 0, 0, axis_index_groups=groups)


def local(coarse_state, fine_state, refined):
    back = jnp.asarray(back_matrix().astype(ml_dtypes.bfloat16))
    fields = lambda *dims: pltpu.VMEM(dims, jnp.float32)
    matrix = lambda *dims: jax.ShapeDtypeStruct(dims, jnp.bfloat16)
    made = call(matrices, [matrix(256, 4 * LANES), matrix(LANES, LANES), matrix(LANES, LANES)], [], (), pl.CostEstimate(flops=50000000, bytes_accessed=327680, transcendentals=0))
    inner, send = call(
        prepare,
        [shape(COUNT, 8, LANES), shape(8, 2 * FACE, LANES)],
        [fields(5, 40, LANES), fields(5, 8, LANES), fields(128, LANES)],
        (refined, jnp.swapaxes(coarse_state, 0, 1), jnp.swapaxes(fine_state[0], 0, 1), *made),
    )
    got0 = swap(send, 0)
    got1 = swap(call(carry_once, [shape(8, ROWS, LANES)], [], (got0,))[0], 1)
    got2 = swap(call(carry_twice, [shape(8, ROWS, LANES)], [], (got1,))[0], 2)
    coarse_out, fine_out = call(
        advance,
        [shape(5, 1, 512), shape(5, 8, 512)],
        [fields(5, 40, LANES), fields(128, LANES)],
        (got0, got1, got2, inner, back, *made[1:]),
    )
    return jnp.swapaxes(coarse_out, 0, 1), jnp.swapaxes(fine_out, 0, 1)[None]


def solution(mesh):
    in_specs = (P("boxes", None, None), P("boxes", None, None, None), P("boxes", None))
    out_specs = (P("boxes", None, None), P("boxes", None, None, None))
    return jax.shard_map(local, mesh=mesh, in_specs=in_specs, out_specs=out_specs, check_vma=False)
```
